32 devices in a mesh: fsdp: 8 (over z, x), tp: 4 (over y, core).
Axes of the slice: x: 2, y: 2, z: 4, core: 2. Of those that a mesh axis runs over, the one named last changes fastest.
Arguments:
- patch_embeddings: bfloat16 [2, 6400, 768], P(None, ('fsdp', 'tp')), may hold values from -6 to 6
- upstream_gradient: bfloat16 [2, 6400, 768], P(None, ('fsdp', 'tp')), may hold values from -6 to 6
- picture_valid_count: int32 [2, 32], P(None, 'fsdp'), may hold values from 147 to 197, as said below
- assigned_specialists: int32 [2, 6400, 2], P(None, 'fsdp'), may hold values from 0 to 3, all different within a row
- filling_sequence_place: int32 [2, 8, 800], P(None, 'fsdp'), may hold values from 0 to 799, each once within a row
- leading_scale_factor: bfloat16 [768], P('fsdp'), may hold values from 0.5 to 1.5
- leading_offset_vector: bfloat16 [768], P('fsdp'), may hold values from -1.25 to 1.25
- query_value_matrix: bfloat16 [768, 3, 768], P('fsdp', None, 'tp'), may hold values from -0.21875 to 0.21875
- mixing_projection_matrix: bfloat16 [768, 768], P('tp', 'fsdp'), may hold values from -1.5 to 1.5
- mixing_offset_vector: bfloat16 [768], P('fsdp'), may hold values from -1.25 to 1.25
- central_scale_factor: bfloat16 [768], P('fsdp'), may hold values from 0.5 to 1.5
- central_offset_vector: bfloat16 [768], P('fsdp'), may hold values from -1.25 to 1.25
- gating_projection: bfloat16 [768, 4], P('fsdp'), may hold values from -0.15625 to 0.15625
- specialist_widen_matrix: bfloat16 [4, 768, 3072], P(None, 'fsdp', 'tp'), may hold values from -0.21875 to 0.21875
- specialist_inner_offset: bfloat16 [4, 3072], P(None, 'tp'), may hold values from -0.625 to 0.625
- specialist_contract_matrix: bfloat16 [4, 3072, 768], P(None, 'tp', 'fsdp'), may hold values from -0.4375 to 0.4375
- specialist_final_offset: bfloat16 [4, 768], P(None, 'fsdp'), may hold values from -0.625 to 0.625
Outputs:
- layer_output: float32 [2, 6400, 768], P(None, ('fsdp', 'tp'))
- grad_tokens: float32 [2, 6400, 768], P(None, ('fsdp', 'tp'))
- grad_pregain: float32 [768], P('fsdp')
- grad_preshift: float32 [768], P('fsdp')
- grad_attnweight: float32 [768, 3, 768], P('fsdp', None, 'tp')
- grad_attnoutput: float32 [768, 768], P('tp', 'fsdp')
- grad_attnbias: float32 [768], P('fsdp')
- grad_midgain: float32 [768], P('fsdp')
- grad_midshift: float32 [768], P('fsdp')
- grad_router: float32 [768, 4], P('fsdp')
- grad_hidden: float32 [4, 768, 3072], P(None, 'fsdp', 'tp')
- grad_hiddenbias: float32 [4, 3072], P(None, 'tp')
- grad_expertout: float32 [4, 3072, 768], P(None, 'tp', 'fsdp')
- grad_outputbias: float32 [4, 768], P(None, 'fsdp')
The draws below stay inside these ranges and needn't reach their ends.
Inputs may be any that keep to these rules, and one draw needn't show every extreme that they name: `picture_valid_count`: the first image of every group in every micro-batch has 197 real tokens.
All inputs are finite; a program needn't handle non-finite values.
Results may differ from the reference program's by a relative error of at most 0.018.
Values may be sent and summed in bfloat16 or wider, within the bound.
A program may use at most 104 MiB of HBM per device.

```python
import math
import jax
import jax.numpy as jnp
from jax import lax

EMBED_WIDTH = 768
HEAD_DIM = 64
FF = 3072
EXPERTS = 4
SEQ = 200
MB = 2
IMG_MB = 4
LIVE = 197
TOK_MB = 800
CAPACITY = 400
TOK_ALL = 6400
N_FSDP = 8


def draw_picture_valid_count(key, part):
    key = jax.random.fold_in(key, 11)
    cut_count = jax.random.randint(key, (MB, IMG_MB * N_FSDP), 0, SEQ // 4 + 1)
    lengths = LIVE - cut_count
    first_image = jnp.arange(IMG_MB * N_FSDP) % IMG_MB == 0
    return jnp.where(first_image[None, :], LIVE, lengths).astype(jnp.int32)


def spiked(drawn, rng, source, target, blocks, factor):
    owner, partner = [(jnp.arange(drawn.shape[axis_at]) // (drawn.shape[axis_at] // blocks)).reshape([-1 if axis == axis_at else 1 for axis in range(drawn.ndim)]) for axis_at in (source, target)]
    chosen = jax.random.permutation(rng, blocks)[partner]
    strong = (owner == chosen) | (owner == (partner + blocks // 2) % blocks)
    return jnp.where(strong, factor * drawn, drawn)


def block_levels(own_key, dims, shards, smallest, high):
    level, own = 1.0, jax.random.fold_in(own_key, 6)
    for axis_at, shards_of in shards:
        draws = jnp.exp(jax.random.uniform(jax.random.fold_in(own, axis_at), (shards_of,), jnp.float32, smallest / len(shards), high / len(shards)))
        level = level * jnp.repeat(draws, dims[axis_at] // shards_of).reshape([-1 if axis == axis_at else 1 for axis in range(len(dims))])
    return level


def picks_of(key, rows, amount, top, lift):
    sequence = jax.random.permutation(jax.random.fold_in(key, 1), amount)
    favour = sequence
    for power in range(3):
        favour = favour * favour // amount
    favour = favour * lift // amount
    lots = jax.random.randint(jax.random.fold_in(key, 2), (rows, amount), 0, 4096) + favour
    sure = jax.random.permutation(jax.random.fold_in(key, 3), rows)[jnp.arange(amount) % rows]
    lots = jnp.where(jnp.arange(rows)[:, None] == sure[None, :], 1 << 14, lots)
    priority = lots * amount + jnp.arange(amount)
    return lax.top_k(priority.astype(jnp.int32), top)[1].astype(jnp.int32)


def gaussian(own_key, shape, width, reach, cuts=(), held_as=jnp.bfloat16):
    level = block_levels(own_key, shape, cuts, -0.22, 0.18) if cuts else 1.0
    array = jax.random.normal(own_key, shape, jnp.float32) * width * level
    return jnp.minimum(jnp.maximum(array, -reach), reach).astype(held_as)


def noise_with(own_key, extent, scale, reach, cuts, heavy, held_as=jnp.bfloat16):
    drawn = scale * jax.random.normal(own_key, extent, jnp.float32)
    if cuts:
        drawn = drawn * block_levels(own_key, extent, cuts, -0.22, 0.18)
    return jnp.clip(spiked(drawn, jax.random.fold_in(own_key, 3), *heavy), -reach, reach).astype(held_as)


def setup_inputs(seed: int = 0) -> dict:
    splits = jax.random.split(jax.random.key(seed), 18)
    patch_embeddings = gaussian(splits[0], (MB, TOK_ALL, EMBED_WIDTH), 1.0, 6.0, ((1, 32),))
    upstream_gradient = noise_with(splits[1], (MB, TOK_ALL, EMBED_WIDTH), 1.0, 6.0, ((1, 32),), (1, 2, 32, 2.75))
    picture_valid_count = draw_picture_valid_count(jax.random.fold_in(splits[17], 71), 0)
    assigned_specialists = picks_of(splits[3], MB * TOK_ALL, EXPERTS, 2, 0).reshape((MB, TOK_ALL, 2))
    filling_sequence_place = jax.vmap(lambda own: jax.random.permutation(own, TOK_MB))(jax.random.split(splits[4], MB * N_FSDP)).reshape((MB, N_FSDP, TOK_MB)).astype(jnp.int32)
    leading_scale_factor = jnp.clip(1.0 + 0.1 * jax.random.normal(splits[5], (EMBED_WIDTH,), jnp.float32), 0.5, 1.5).astype(jnp.bfloat16)
    leading_offset_vector = gaussian(splits[6], (EMBED_WIDTH,), 0.2, 1.25, ((0, 8),))
    query_value_matrix = gaussian(splits[7], (EMBED_WIDTH, 3, EMBED_WIDTH), EMBED_WIDTH ** -0.5, 0.21875, ((0, 8), (2, 4)))
    mixing_projection_matrix = gaussian(splits[8], (EMBED_WIDTH, EMBED_WIDTH), (max(1, EMBED_WIDTH // 48)) ** -0.5, 1.5, ((0, 4), (1, 8)))
    mixing_offset_vector = gaussian(splits[9], (EMBED_WIDTH,), 0.2, 1.25, ((0, 8),))
    central_scale_factor = jnp.clip(1.0 + 0.1 * jax.random.normal(splits[10], (EMBED_WIDTH,), jnp.float32), 0.5, 1.5).astype(jnp.bfloat16)
    central_offset_vector = gaussian(splits[11], (EMBED_WIDTH,), 0.2, 1.25, ((0, 8),))
    gating_projection = gaussian(splits[12], (EMBED_WIDTH, EXPERTS), (2 * EMBED_WIDTH) ** -0.5, 0.15625, ((0, 8),))
    specialist_widen_matrix = gaussian(splits[13], (EXPERTS, EMBED_WIDTH, FF), EMBED_WIDTH ** -0.5, 0.21875, ((1, 8), (2, 4)))
    specialist_inner_offset = gaussian(splits[14], (EXPERTS, FF), 0.1, 0.625, ((1, 4),))
    specialist_contract_matrix = gaussian(splits[15], (EXPERTS, FF, EMBED_WIDTH), (FF // 16) ** -0.5, 0.4375, ((1, 4), (2, 8)))
    specialist_final_offset = gaussian(splits[16], (EXPERTS, EMBED_WIDTH), 0.1, 0.625, ((1, 8),))
    return dict(patch_embeddings=patch_embeddings, upstream_gradient=upstream_gradient, picture_valid_count=picture_valid_count, assigned_specialists=assigned_specialists, filling_sequence_place=filling_sequence_place, leading_scale_factor=leading_scale_factor, leading_offset_vector=leading_offset_vector, query_value_matrix=query_value_matrix, mixing_projection_matrix=mixing_projection_matrix, mixing_offset_vector=mixing_offset_vector, central_scale_factor=central_scale_factor, central_offset_vector=central_offset_vector, gating_projection=gating_projection, specialist_widen_matrix=specialist_widen_matrix, specialist_inner_offset=specialist_inner_offset, specialist_contract_matrix=specialist_contract_matrix, specialist_final_offset=specialist_final_offset)


NORM_EPS = 1e-06
MASK_FILL = -1000000000.0

@jax.custom_vjp
def coarse_numeric_format(v):
    return lax.optimization_barrier(v.astype(jnp.bfloat16)).astype(jnp.float32)

@jax.custom_vjp
def low_back(v):
    return v

def low_keep(v):
    return (coarse_numeric_format(v), None)

def low_pass(kept, grad):
    return (grad,)

def back_keep(v):
    return (v, None)

def back_low(kept, grad):
    return (coarse_numeric_format(grad),)
coarse_numeric_format.defvjp(low_keep, low_pass)
low_back.defvjp(back_keep, back_low)

def standardize_features(values, gain_vec, shift_vec):
    row_mean = lax.optimization_barrier(jnp.mean(values, axis=-1, keepdims=True))
    centred = values - row_mean
    row_var = lax.optimization_barrier(jnp.mean(centred * centred, axis=-1, keepdims=True))
    return centred * lax.rsqrt(row_var + NORM_EPS) * gain_vec + shift_vec

def route_slots(route_ids, priority_ids, expert_count, slot_count):
    row_count = route_ids.shape[0]
    order_key = (priority_ids[:, None] + row_count * jnp.arange(2, dtype=jnp.int32)[None, :]).reshape(-1)
    chosen = route_ids.reshape(-1)
    rank_order = jnp.argsort(order_key)
    ranked = chosen[rank_order]
    onehot = (ranked[:, None] == jnp.arange(expert_count, dtype=jnp.int32)[None, :]).astype(jnp.int32)
    before = jnp.cumsum(onehot, axis=0) - onehot
    place_ranked = lax.optimization_barrier(jnp.sum(before * onehot, axis=1))
    place_all = jnp.zeros_like(place_ranked).at[rank_order].set(place_ranked)
    kept_mask = place_all < slot_count
    slot_ids = jnp.where(kept_mask, chosen * slot_count + place_all, expert_count * slot_count).astype(jnp.int32)
    owner_ids = jnp.full((expert_count * slot_count + 1,), 2 * row_count, jnp.int32)
    owner_ids = owner_ids.at[slot_ids].set(jnp.arange(2 * row_count, dtype=jnp.int32))
    return (slot_ids.reshape(row_count, 2), kept_mask.reshape(row_count, 2), owner_ids[:expert_count * slot_count])

def block_forward(learnable_collection, incoming_token_matrix, route_ids, priority_ids, key_lengths):
    leading_scale_factor, leading_offset_vector, query_value_matrix, mixing_projection_matrix, mixing_offset_vector, central_scale_factor, central_offset_vector, gating_projection, specialist_widen_matrix, specialist_inner_offset, specialist_contract_matrix, specialist_final_offset = learnable_collection
    highest = lax.Precision.HIGHEST
    row_count = incoming_token_matrix.shape[0]
    model_width = incoming_token_matrix.shape[1]
    image_count = key_lengths.shape[0]
    seq_len = row_count // image_count
    head_count = query_value_matrix.shape[2] // HEAD_DIM
    initial_standardized_tokens = coarse_numeric_format(standardize_features(incoming_token_matrix, leading_scale_factor, leading_offset_vector))
    projected = jnp.einsum('td,dcf->tcf', initial_standardized_tokens, query_value_matrix, precision=highest)
    queries = coarse_numeric_format(low_back(projected[:, 0])).reshape(image_count, seq_len, head_count, HEAD_DIM)
    keys_all = coarse_numeric_format(low_back(projected[:, 1])).reshape(image_count, seq_len, head_count, HEAD_DIM)
    values = coarse_numeric_format(low_back(projected[:, 2])).reshape(image_count, seq_len, head_count, HEAD_DIM)
    score_scale = 1.0 / math.sqrt(HEAD_DIM)
    scores = low_back(jnp.einsum('ishd,ithd->ihst', queries, keys_all, precision=highest) * score_scale)
    visible = jnp.arange(seq_len, dtype=jnp.int32)[None, :] < key_lengths[:, None]
    scores = jnp.where(visible[:, None, None, :], scores, MASK_FILL)
    row_top = lax.optimization_barrier(jnp.max(scores, axis=-1, keepdims=True))
    exp_terms = jnp.exp(scores - row_top)
    att_probs = coarse_numeric_format(exp_terms / lax.optimization_barrier(jnp.sum(exp_terms, axis=-1, keepdims=True)))
    att_mixed = jnp.einsum('ihst,ithd->ishd', att_probs, values, precision=highest).reshape(row_count, head_count * HEAD_DIM)
    att_mixed = coarse_numeric_format(low_back(att_mixed))
    hidden_one = incoming_token_matrix + low_back(jnp.dot(att_mixed, mixing_projection_matrix, precision=highest)) + mixing_offset_vector
    normed_two = coarse_numeric_format(standardize_features(hidden_one, central_scale_factor, central_offset_vector))
    logits = low_back(jnp.dot(normed_two, gating_projection, precision=highest))
    logit_top = lax.optimization_barrier(jnp.max(logits, axis=1, keepdims=True))
    logit_exp = jnp.exp(logits - logit_top)
    router_probs = logit_exp / lax.optimization_barrier(jnp.sum(logit_exp, axis=1, keepdims=True))
    gate_vals = jnp.take_along_axis(router_probs, route_ids, axis=1)
    slot_ids, kept_mask, owner_ids = route_slots(route_ids, priority_ids, EXPERTS, CAPACITY)
    padded_rows = jnp.concatenate([normed_two, jnp.zeros((1, model_width), jnp.float32)])
    source_rows = jnp.where(owner_ids < 2 * row_count, owner_ids // 2, row_count)
    dispatched = padded_rows[source_rows].reshape(EXPERTS, CAPACITY, model_width)
    pre_act = low_back(jnp.einsum('ecd,edf->ecf', dispatched, specialist_widen_matrix, precision=highest) + specialist_inner_offset[:, None, :])
    activation = coarse_numeric_format(jax.nn.gelu(pre_act, approximate=False))
    expert_rows = low_back(jnp.einsum('ecf,efd->ecd', activation, specialist_contract_matrix, precision=highest)) + specialist_final_offset[:, None, :]
    expert_pad = jnp.concatenate([expert_rows.reshape(EXPERTS * CAPACITY, model_width), jnp.zeros((1, model_width), jnp.float32)])
    picked = expert_pad[slot_ids]
    pair_weight = gate_vals * kept_mask.astype(jnp.float32)
    return hidden_one + lax.optimization_barrier(jnp.sum(pair_weight[:, :, None] * picked, axis=1))

def reference(patch_embeddings, upstream_gradient, picture_valid_count, assigned_specialists, filling_sequence_place, leading_scale_factor, leading_offset_vector, query_value_matrix, mixing_projection_matrix, mixing_offset_vector, central_scale_factor, central_offset_vector, gating_projection, specialist_widen_matrix, specialist_inner_offset, specialist_contract_matrix, specialist_final_offset):
    coefficient_package = tuple((coefficient_operand.astype(jnp.float32) for coefficient_operand in (leading_scale_factor, leading_offset_vector, query_value_matrix, mixing_projection_matrix, mixing_offset_vector, central_scale_factor, central_offset_vector, gating_projection, specialist_widen_matrix, specialist_inner_offset, specialist_contract_matrix, specialist_final_offset)))
    block_count = MB * N_FSDP
    route_blocks = assigned_specialists.reshape(block_count, TOK_MB, 2)
    priority_blocks = filling_sequence_place.reshape(block_count, TOK_MB)
    length_blocks = picture_valid_count.reshape(block_count, IMG_MB)

    def forward(token_rows, *learnable_collection):

        def one_block(item_tuple):
            return block_forward(learnable_collection, *item_tuple)
        outputs = lax.map(jax.checkpoint(one_block), (token_rows.reshape(block_count, TOK_MB, EMBED_WIDTH), route_blocks, priority_blocks, length_blocks))
        return outputs.reshape(MB, TOK_MB * N_FSDP, EMBED_WIDTH)
    layer_output, pullback = jax.vjp(forward, patch_embeddings.astype(jnp.float32), *coefficient_package)
    grads = pullback(upstream_gradient.astype(jnp.float32))
    return (layer_output, grads[0], grads[1], grads[2], grads[3], grads[4], grads[5], grads[6], grads[7], grads[8], grads[9], grads[10], grads[11], grads[12])
```

```python
import functools
import math

import jax
import jax.numpy as jnp
from jax import lax
from jax.experimental import pallas as pl
from jax.experimental.pallas import tpu as pltpu
from jax.sharding import PartitionSpec as P

HEAD_DIM = 64
NORM_EPS = 1e-06
MASK_FILL = -1000000000.0
MESH = pl.DeviceIdType.MESH
BF = jnp.bfloat16
F32 = jnp.float32
DMA = pltpu.SemaphoreType.DMA

EARLY_GATHER = 2
EARLY_REDUCE = 2
VMEM_LIMIT = 60 << 20


def dot_nn(a, b):
    return lax.dot_general(a, b, (((1,), (0,)), ((), ())), preferred_element_type=F32)


def dot_nt(a, b):
    return lax.dot_general(a, b, (((1,), (1,)), ((), ())), preferred_element_type=F32)


def dot_tn(a, b):
    return lax.dot_general(a, b, (((0,), (0,)), ((), ())), preferred_element_type=F32)


def norm_parts(values):
    row_mean = jnp.mean(values, axis=-1, keepdims=True)
    centred = values - row_mean
    row_var = jnp.mean(centred * centred, axis=-1, keepdims=True)
    inv_std = lax.rsqrt(row_var + NORM_EPS)
    return centred * inv_std, inv_std


def norm_back(scaled, normed, inv_std):
    return inv_std * (
        scaled
        - jnp.mean(scaled, axis=-1, keepdims=True)
        - normed * jnp.mean(scaled * normed, axis=-1, keepdims=True)
    )


def gelu_parts(x):
    z = jnp.abs(x) * (1.0 / math.sqrt(2.0))
    t = 1.0 / (1.0 + 0.3275911 * z)
    expo = jnp.exp(-0.5 * x * x)
    poly = t * (
        0.254829592
        + t * (-0.284496736 + t * (1.421413741 + t * (-1.453152027 + t * 1.061405429)))
    )
    tail = 0.5 * poly * expo
    cdf = jnp.where(x >= 0, 1.0 - tail, tail)
    return x * cdf, cdf + x * (expo * (1.0 / math.sqrt(2.0 * math.pi)))


def remote(src, dst, send, recv, dev):
    return pltpu.make_async_remote_copy(
        src_ref=src, dst_ref=dst, send_sem=send, recv_sem=recv, device_id=dev, device_id_type=MESH
    )


class Net:
    def __init__(self, fsdp):
        self.fsdp = fsdp
        self.half = fsdp // 2
        self.f = f = lax.axis_index("fsdp")
        self.t = t = lax.axis_index("tp")
        self.pf = f + 1 - 2 * lax.rem(f, 2)
        self.t2 = lax.rem(t + 2, 4)
        self.s = t + 1 - 2 * lax.rem(t, 2)
        self.s2 = lax.rem(self.s + 2, 4)
        self.partner = (self.pf, t)
        self.across = (f, self.t2)
        self.sibling = (f, self.s)

    def at(self, base, k):
        return lax.rem(base + 2 * k + self.fsdp, self.fsdp)

    def line(self, k):
        return (self.at(self.f, k), self.t)

    def barrier(self):
        sem = pltpu.get_barrier_semaphore()
        peers = [self.partner, self.across, self.sibling]
        peers += [self.line(k) for k in range(1, self.half)]
        for peer in peers:
            pl.semaphore_signal(sem, inc=1, device_id=peer, device_id_type=MESH)
        pl.semaphore_wait(sem, len(peers))


class Gather:
    def __init__(self, net, block, sems, unit):
        self.net, self.block, self.unit = net, block, unit
        self.ps, self.pr, self.ls, self.lr = sems

    def _pair(self, j, k):
        u = self.unit
        return remote(self.block(j), self.block(j), self.ps.at[u, k], self.pr.at[u, k], self.net.partner)

    def _line(self, j, k):
        u = self.unit
        return remote(self.block(j), self.block(j), self.ls.at[u, k], self.lr.at[u, k], self.net.line(k))

    def start(self):
        n = self.net
        for k in range(1, n.half):
            self._line(n.f, k).start()
        self._pair(n.f, 0).start()

    def forward(self):
        n = self.net
        for k in range(1, n.half):
            j = n.at(n.f, -k)
            self._line(j, k).wait_recv()
            self._pair(j, k).start()

    def finish(self):
        n = self.net
        for k in range(n.half):
            self._pair(n.at(n.pf, -k), k).wait_recv()

    def drain(self):
        n = self.net
        for k in range(n.half):
            self._pair(n.f, k).wait_send()
        for k in range(1, n.half):
            self._line(n.f, k).wait_send()


class Reduce:
    def __init__(self, net, block, first, second, sems, unit):
        self.net, self.block, self.first, self.second, self.unit = net, block, first, second, unit
        self.ps, self.pr, self.ls, self.lr = sems

    def _pair(self, k):
        n, u = self.net, self.unit
        return remote(
            self.block(n.at(n.pf, k)), self.first(k), self.ps.at[u, k], self.pr.at[u, k], n.partner
        )

    def _line(self, k):
        n, u = self.net, self.unit
        return remote(
            self.block(n.at(n.f, k)), self.second(k), self.ls.at[u, k], self.lr.at[u, k], n.line(k)
        )

    def start(self):
        for k in list(range(1, self.net.half)) + [0]:
            self._pair(k).start()

    def middle(self):
        n = self.net
        for k in range(1, n.half):
            self._pair(k).wait_recv()
            mine = self.block(n.at(n.f, k))
            mine[...] = (mine[...].astype(F32) + self.first(k)[...].astype(F32)).astype(BF)
            self._line(k).start()

    def finish(self):
        n = self.net
        self._pair(0).wait_recv()
        total = self.block(n.f)[...].astype(F32) + self.first(0)[...].astype(F32)
        for k in range(1, n.half):
            self._line(k).wait_recv()
            total = total + self.second(k)[...].astype(F32)
        return total

    def drain(self):
        for k in range(self.net.half):
            self._pair(k).wait_send()
        for k in range(1, self.net.half):
            self._line(k).wait_send()


class RowGather:
    def __init__(self, net, block, sems, unit):
        self.net, self.block, self.unit = net, block, unit
        self.ys, self.yr, self.cs, self.cr = sems

    def _y(self, j):
        u = self.unit
        return remote(self.block(j), self.block(j), self.ys.at[u], self.yr.at[u], self.net.across)

    def _c(self, j, k):
        u = self.unit
        return remote(self.block(j), self.block(j), self.cs.at[u, k], self.cr.at[u, k], self.net.sibling)

    def start(self):
        self._y(self.net.t).start()
        self._c(self.net.t, 0).start()

    def forward(self):
        n = self.net
        self._y(n.t2).wait_recv()
        self._c(n.t2, 1).start()

    def finish(self):
        n = self.net
        self._c(n.s, 0).wait_recv()
        self._c(n.s2, 1).wait_recv()

    def drain(self):
        n = self.net
        self._y(n.t).wait_send()
        self._c(n.t, 0).wait_send()
        self._c(n.t2, 1).wait_send()


class RowReduce:
    def __init__(self, net, block, first, second, sems, unit):
        self.net, self.block, self.first, self.second, self.unit = net, block, first, second, unit
        self.ys, self.yr, self.cs, self.cr = sems

    def _c(self, k):
        n, u = self.net, self.unit
        j = n.s2 if k == 0 else n.s
        return remote(self.block(j), self.first(k), self.cs.at[u, k], self.cr.at[u, k], n.sibling)

    def _y(self):
        n, u = self.net, self.unit
        return remote(self.block(n.t2), self.second(), self.ys.at[u], self.yr.at[u], n.across)

    def start(self):
        self._c(0).start()
        self._c(1).start()

    def middle(self, add=None):
        n = self.net
        self._c(0).wait_recv()
        mine = self.block(n.t2)
        if add is None:
            mine[...] = (mine[...].astype(F32) + self.first(0)[...].astype(F32)).astype(BF)
        else:
            add(mine, self.first(0))
        self._y().start()

    def finish(self):
        n = self.net
        self._c(1).wait_recv()
        self._y().wait_recv()
        return (
            self.block(n.t)[...].astype(F32)
            + self.first(1)[...].astype(F32)
            + self.second()[...].astype(F32)
        )

    def drain(self):
        self._c(0).wait_send()
        self._c(1).wait_send()
        self._y().wait_send()


def head_masks(rows, width):
    lane = lax.broadcasted_iota(jnp.int32, (rows, width), 1)
    return [
        (lane >= h * HEAD_DIM) & (lane < (h + 1) * HEAD_DIM) for h in range(width // HEAD_DIM)
    ]


def stack_heads(rows, masks):
    zero = jnp.zeros_like(rows)
    return jnp.concatenate([jnp.where(mask, rows, zero) for mask in masks], axis=0)


def merge_heads(stacked, masks):
    count = masks[0].shape[0]
    total = jnp.where(masks[0], stacked[:count], 0.0)
    for h in range(1, len(masks)):
        total = jnp.where(masks[h], stacked[h * count : (h + 1) * count], total)
    return total


def front_kernel(fsdp, early, *refs):
    it = iter(refs)
    take = lambda n: [next(it) for _ in range(n)]
    cnt, x_in, dy_in, par_in, aw_in, w1_in, w2_in = take(7)
    xg, dyg, rin, qkv, prob, mix, hid, n2g, awg, par, wg = take(11)
    parg, part, first, second = take(4)
    ga = take(4)
    rg = take(4)
    rr = take(4)
    (loc,) = take(1)
    net = Net(fsdp)
    f, t = net.f, net.t
    rows, width = x_in.shape[1], x_in.shape[2]
    images = xg.shape[0] // 2
    hw = qkv.shape[3]
    own = width // fsdp

    gat_par = Gather(net, lambda j: parg.at[j], ga, 0)
    gat_aw = Gather(net, lambda j: awg.at[j], ga, 1)
    gat_e = [Gather(net, (lambda e: lambda j: wg.at[e, j])(e), ga, 2 + e) for e in range(early)]
    row_x = [RowGather(net, (lambda m: lambda j: xg.at[m * images + j])(m), rg, m) for m in range(2)]
    row_dy = [RowGather(net, (lambda m: lambda j: dyg.at[m * images + j])(m), rg, 2 + m) for m in range(2)]
    row_n2 = [RowGather(net, (lambda m: lambda j: n2g.at[m * images + j])(m), rg, 4 + m) for m in range(2)]
    red = [
        RowReduce(
            net,
            (lambda m: lambda j: part.at[m, j])(m),
            (lambda m: lambda k: first.at[m, k])(m),
            (lambda m: lambda: second.at[m])(m),
            rr,
            m,
        )
        for m in range(2)
    ]

    copies = []
    for e in range(early):
        for i, src in enumerate((w1_in, w2_in)):
            copies.append(pltpu.make_async_copy(src.at[e], wg.at[e, f, i], loc.at[2 * e + i]))
    for copy in copies:
        copy.start()
    parg[f] = par_in[...]
    awg[f] = aw_in[...]
    for m in range(2):
        xg[m * images + t] = x_in[m]
        dyg[m * images + t] = dy_in[m]
    net.barrier()
    gat_par.start()
    row_x[0].start()
    gat_aw.start()
    row_x[1].start()
    for copy in copies:
        copy.wait()
    if early:
        gat_e[0].start()
    gat_par.forward()
    for m in range(2):
        row_dy[m].start()
    gat_aw.forward()
    row_x[0].forward()
    gat_par.finish()

    place = lax.broadcasted_iota(jnp.int32, (128, width), 0)
    column = lax.broadcasted_iota(jnp.int32, (128, width), 1)
    joined = jnp.zeros((16, width), F32)
    for j in range(fsdp):
        hot = ((column == place + j * own) & (place < own)).astype(BF)
        joined = joined + dot_nn(parg[j], hot)
    par[...] = joined
    gain_one, shift_one = par[0:1, :], par[1:2, :]
    mix_bias, gain_two, shift_two = par[2:3, :], par[3:4, :], par[4:5, :]

    def first_norm(i, carry):
        normed, _ = norm_parts(xg[i].astype(F32))
        rin[i] = (normed * gain_one + shift_one).astype(BF)
        return carry

    row_x[0].finish()
    lax.fori_loop(0, images, first_norm, 0)
    row_x[1].forward()
    if early:
        gat_e[0].forward()
    if early > 1:
        gat_e[1].start()
    row_x[1].finish()
    lax.fori_loop(images, 2 * images, first_norm, 0)
    gat_aw.finish()

    weights = awg[...].reshape(width, 4 * hw)
    for m in range(2):
        block = rin[m * images : (m + 1) * images].reshape(images * rows, width)
        for c in range(3):
            made = dot_nn(block, weights[:, c * hw : (c + 1) * hw])
            qkv[c, m * images : (m + 1) * images] = made.astype(BF).reshape(images, rows, hw)
    for m in range(2):
        row_dy[m].forward()
    masks = head_masks(rows, hw)
    key_pos = lax.broadcasted_iota(jnp.int32, (len(masks) * rows, rows), 1)

    def attend(i, carry):
        stacked = stack_heads(qkv[0, i], masks)
        scores = dot_nt(stacked, qkv[1, i]) * (1.0 / math.sqrt(HEAD_DIM))
        scores = jnp.where(key_pos < cnt[i], scores, MASK_FILL)
        expo = jnp.exp(scores - jnp.max(scores, axis=-1, keepdims=True))
        probs = (expo / jnp.sum(expo, axis=-1, keepdims=True)).astype(BF)
        prob[i] = probs
        mix[i] = merge_heads(dot_nn(probs, qkv[2, i]), masks).astype(BF)
        return carry

    out_w = awg[...].reshape(width, 4 * hw)[:, 3 * hw :]
    for m in range(2):
        lax.fori_loop(m * images, (m + 1) * images, attend, 0)
        block = mix[m * images : (m + 1) * images].reshape(images * rows, hw)
        part[m] = dot_nt(block, out_w).astype(BF).reshape(images, rows, width)
        red[m].start()
        if m == 0:
            red[0].middle()
            for e in range(1, early):
                gat_e[e].forward()
                if e + 1 < early:
                    gat_e[e + 1].start()
    red[1].middle()
    for m in range(2):
        hidden = x_in[m].astype(F32) + red[m].finish() + mix_bias
        hid[m] = hidden
        normed, _ = norm_parts(hidden)
        n2g[m * images + t] = (normed * gain_two + shift_two).astype(BF)
        row_n2[m].start()
    for m in range(2):
        row_n2[m].forward()
        row_dy[m].finish()
    for m in range(2):
        row_n2[m].finish()
    for e in range(early):
        gat_e[e].finish()
    for op in [gat_par, gat_aw] + gat_e + row_x + row_dy + row_n2 + red:
        op.drain()


def expert_kernel(fsdp, early, reduce_early, *refs):
    it = iter(refs)
    take = lambda n: [next(it) for _ in range(n)]
    n2g, dyg, par, wearly, w1_in, w2_in, b1, route, prio = take(9)
    total, gout, glate, hb, ob = take(5)
    wbuf, acc, hot_s, xs, vs, gas, dps, sid, rp, part, first, second, r1, r2 = take(14)
    ga = take(4)
    rs = take(4)
    rr = take(4)
    loc, late_sem = take(2)
    net = Net(fsdp)
    f, t = net.f, net.t
    experts, slots = wbuf.shape[0], hot_s.shape[1]
    rows, width = n2g.shape[1], n2g.shape[2]
    images = n2g.shape[0] // 2
    full = images * rows
    ff = wbuf.shape[4]
    late = experts - early

    def gather(e):
        return Gather(net, lambda j: wbuf.at[e, j], ga, e - early)

    def reduce(e):
        return Reduce(
            net,
            lambda j: wbuf.at[e, j],
            lambda k: r1.at[e, k],
            lambda k: r2.at[e, k],
            rs,
            e,
        )

    copies = []
    for e in range(early):
        copies.append(pltpu.make_async_copy(wearly.at[e], wbuf.at[e], loc.at[e]))
    own_copies = []
    for e in range(early, experts):
        for i, src in enumerate((w1_in, w2_in)):
            own_copies.append(
                pltpu.make_async_copy(src.at[e], wbuf.at[e, f, i], loc.at[experts + 2 * e + i])
            )
    for copy in own_copies + copies:
        copy.start()
    net.barrier()
    for copy in own_copies:
        copy.wait()
    if late:
        gather(early).start()

    for m in range(2):
        e0, e1, order = route[m, 0:1, :], route[m, 1:2, :], route[m, 2:3, :]
        lower = (prio[m] < order).astype(BF)
        kind = lax.broadcasted_iota(jnp.int32, (16, full), 0)
        named = jnp.where(kind < experts, e0, e1) == jnp.where(kind < experts, kind, kind - experts)
        named = jnp.where((kind < 2 * experts) & named, 1.0, 0.0)
        counts = dot_nn(named.astype(BF), lower)
        totals = jnp.sum(named, axis=1, keepdims=True)
        for k in range(2):
            mine = jnp.zeros((1, full), F32)
            where_slot = jnp.full((1, full), -1.0, F32)
            for e in range(experts):
                c = k * experts + e
                before = counts[c : c + 1, :]
                if k == 1:
                    before = before + totals[e : e + 1, :]
                kept = (named[c : c + 1, :] > 0.5) & (before < slots)
                where_slot = jnp.where(kept, before + e * slots, where_slot)
            sid[m, k : k + 1, :] = where_slot.astype(jnp.int32)
        n2m = n2g[m * images : (m + 1) * images].reshape(full, width)
        logits = dot_nt(par[...].astype(BF), n2m)[5 : 5 + experts, :]
        expo = jnp.exp(logits - jnp.max(logits, axis=0, keepdims=True))
        rp[m, 0:experts, :] = expo / jnp.sum(expo, axis=0, keepdims=True)
        acc[m] = jnp.zeros_like(acc[m])
    hb[...] = jnp.zeros_like(hb)
    ob[...] = jnp.zeros_like(ob)
    for copy in copies:
        copy.wait()

    slot_row = lax.broadcasted_iota(jnp.int32, (slots, full), 0)
    lane = lax.broadcasted_iota(jnp.int32, (slots, 128), 1)

    def expert(e, carry):
        if late:

            @pl.when((e + 1 >= early) & (e + 1 < experts) & (e + 1 > early))
            def _():
                gather(e + 1).start()

        gates = []
        for m in range(2):
            hot = (slot_row + e * slots == sid[m, 0:1, :]) | (slot_row + e * slots == sid[m, 1:2, :])
            hot_s[m] = jnp.where(hot, 1.0, 0.0).astype(BF)
            gates.append(
                jnp.sum(jnp.where(hot, rp[m, pl.ds(e, 1), :], 0.0), axis=1, keepdims=True)
            )
            n2m = n2g[m * images : (m + 1) * images].reshape(full, width)
            dym = dyg[m * images : (m + 1) * images].reshape(full, width)
            xs[m] = dot_nn(hot_s[m], n2m).astype(BF)
            vals = dot_nn(hot_s[m], dym)
            ob[pl.ds(e, 1), :] += jnp.sum(gates[m] * vals, axis=0, keepdims=True)
            vs[m] = vals.astype(BF)
        if late:

            @pl.when(e >= early)
            def _():
                gather(e).forward()
                gather(e).finish()

        w1 = wbuf[e, :, 0].reshape(width, ff)
        w2 = wbuf[e, :, 1].reshape(width, ff)
        for m in range(2):
            pre = dot_nn(xs[m], w1) + b1[pl.ds(e, 1), :]
            act, slope = gelu_parts(pre)
            gas[m] = (gates[m] * act).astype(BF)
            back = dot_nn(vs[m], w2)
            d_gate = jnp.sum(act * back, axis=1, keepdims=True)
            d_pre = gates[m] * slope * back
            hb[pl.ds(e, 1), :] += jnp.sum(d_pre, axis=0, keepdims=True)
            dps[m] = d_pre.astype(BF)
            high = d_gate.astype(BF)
            low = (d_gate - high.astype(F32)).astype(BF)
            zero = jnp.zeros((slots, 128), BF)
            made = [dot_nt(gas[m], w2).astype(BF), dot_nt(dps[m], w1).astype(BF)]
            made.append(
                jnp.where(lane == e, high, jnp.where(lane == 16 + e, jnp.ones_like(zero), zero))
            )
            made.append(jnp.where(lane == e, low, zero))
            acc[m] += dot_tn(hot_s[m], jnp.concatenate(made, axis=1))
        if late:

            @pl.when(e >= early)
            def _():
                gather(e).drain()

        two = 2 * slots
        wbuf[e, :, 0] = (
            dot_tn(xs[...].reshape(two, width), dps[...].reshape(two, ff))
            .astype(BF)
            .reshape(fsdp, width // fsdp, ff)
        )
        wbuf[e, :, 1] = (
            dot_tn(vs[...].reshape(two, width), gas[...].reshape(two, ff))
            .astype(BF)
            .reshape(fsdp, width // fsdp, ff)
        )
        if reduce_early:

            @pl.when(e < reduce_early)
            def _():
                reduce(e).start()

            @pl.when((e >= 1) & (e <= reduce_early))
            def _():
                reduce(e - 1).middle()

        if reduce_early < experts:

            @pl.when(e >= reduce_early)
            def _():
                pltpu.make_async_copy(
                    wbuf.at[e], glate.at[e - reduce_early], late_sem.at[e - reduce_early]
                ).start()

        return carry

    lax.fori_loop(0, experts, expert, 0)

    red = [
        RowReduce(
            net,
            (lambda m: lambda j: part.at[m, j])(m),
            (lambda m: lambda k: first.at[m, k])(m),
            (lambda m: lambda: second.at[m])(m),
            rr,
            m,
        )
        for m in range(2)
    ]
    wide = 2 * width

    def add_split(mine, other):
        mine[:, :wide] = (mine[:, :wide].astype(F32) + other[:, :wide].astype(F32)).astype(BF)
        pair = [mine[:, wide : wide + 128].astype(F32), mine[:, wide + 128 :].astype(F32)]
        pair += [other[:, wide : wide + 128].astype(F32), other[:, wide + 128 :].astype(F32)]
        value = (pair[0] + pair[2]) + (pair[1] + pair[3])
        high = value.astype(BF)
        mine[:, wide : wide + 128] = high
        mine[:, wide + 128 :] = (value - high.astype(F32)).astype(BF)

    for m in range(2):
        part[m, :, :, :wide] = acc[m, :, :wide].astype(BF).reshape(images, rows, wide)
        value = acc[m, :, wide : wide + 128] + acc[m, :, wide + 128 :]
        high = value.astype(BF)
        part[m, :, :, wide : wide + 128] = high.reshape(images, rows, 128)
        part[m, :, :, wide + 128 :] = (value - high.astype(F32)).astype(BF).reshape(images, rows, 128)
        red[m].start()
    for m in range(2):
        red[m].middle(add_split)
    if reduce_early == experts:
        reduce(experts - 1).middle()
    for e in range(reduce_early):
        gout[e] = reduce(e).finish()
        reduce(e).drain()
    for m in range(2):
        total[m] = red[m].finish()
        red[m].drain()
    for e in range(reduce_early, experts):
        pltpu.make_async_copy(
            wbuf.at[e], glate.at[e - reduce_early], late_sem.at[e - reduce_early]
        ).wait()


def back_kernel(fsdp, experts, *refs):
    it = iter(refs)
    take = lambda n: [next(it) for _ in range(n)]
    total, hid, n2g, dy_in, x_in, xg, rin, qkv, prob, mix, awg, par, gl, hb, ob = take(15)
    y_out, gx_out, ga_out, gl_out, small = take(5)
    hlg, dmx, dpj, dh, gaw, part, first, second, r1, r2, a1, a2, z1, z2, z3, z4, zs = take(17)
    rs = take(4)
    rg = take(4)
    rr = take(4)
    sm_s, sm_r = take(2)
    net = Net(fsdp)
    f, t = net.f, net.t
    rows, width = hid.shape[1], hid.shape[2]
    images = n2g.shape[0] // 2
    full = images * rows
    hw = qkv.shape[3]
    live = y_out.shape[1]
    late = gl.shape[0]
    wide = 2 * width
    scale = 1.0 / math.sqrt(HEAD_DIM)

    red_g = [
        Reduce(
            net,
            (lambda e: lambda j: gl.at[e, j])(e),
            (lambda e: lambda k: r1.at[e, k])(e),
            (lambda e: lambda k: r2.at[e, k])(e),
            rs,
            e,
        )
        for e in range(late)
    ]
    red_a = Reduce(net, lambda j: gaw.at[j], lambda k: a1.at[k], lambda k: a2.at[k], rs, late)
    row_h = [RowGather(net, (lambda m: lambda j: hlg.at[m * images + j])(m), rg, m) for m in range(2)]
    red = [
        RowReduce(
            net,
            (lambda m: lambda j: part.at[m, j])(m),
            (lambda m: lambda k: first.at[m, k])(m),
            (lambda m: lambda: second.at[m])(m),
            rr,
            m,
        )
        for m in range(2)
    ]
    net.barrier()
    for op in red_g:
        op.start()

    gain_one, gain_two = par[0:1, :], par[3:4, :]
    shift_two = par[4:5, :]
    zs[...] = jnp.zeros_like(zs)
    lane = lax.broadcasted_iota(jnp.int32, (rows, 128), 1)
    lane16 = lax.broadcasted_iota(jnp.int32, (rows, 16), 1)
    router_lane = (lane16 >= 5) & (lane16 < 5 + experts)
    for m in range(2):
        hidden = hid[m]
        normed, inv = norm_parts(hidden)
        dy = dy_in[m].astype(F32)
        n2 = n2g[m * images + t]
        logits = jnp.where(router_lane, dot_nt(n2, par[...].astype(BF)), -1e30)
        expo = jnp.exp(logits - jnp.max(logits, axis=1, keepdims=True))
        probs = expo / jnp.sum(expo, axis=1, keepdims=True)
        sums = total[m, :, wide : wide + 128] + total[m, :, wide + 128 :]
        pcol, qcol, out = [], [], hidden + total[m, :, :width]
        for e in range(experts):
            p_e = jnp.sum(jnp.where(lane16 == 5 + e, probs, 0.0), axis=1, keepdims=True)
            kept = 0.25 * jnp.sum(jnp.where(lane == 16 + e, sums, 0.0), axis=1, keepdims=True)
            q_e = jnp.sum(jnp.where(lane == e, sums, 0.0), axis=1, keepdims=True)
            bias = par[5 + experts + e : 6 + experts + e, :]
            q_e = q_e + kept * jnp.sum(dy * bias, axis=1, keepdims=True)
            out = out + (kept * p_e) * bias
            pcol.append(p_e)
            qcol.append(q_e)
        y_out[m] = out[:live]
        mean_q = pcol[0] * qcol[0]
        for e in range(1, experts):
            mean_q = mean_q + pcol[e] * qcol[e]
        mid = total[m, :, width:wide]
        for e in range(experts):
            d_logit = (pcol[e] * (qcol[e] - mean_q)).astype(BF).astype(F32)
            mid = mid + d_logit * par[5 + e : 6 + e, :]
            zs[5 + e : 6 + e, :] += jnp.sum(d_logit * n2.astype(F32), axis=0, keepdims=True)
        d_hidden = dy + norm_back(mid * gain_two, normed, inv)
        dh[m] = d_hidden
        hlg[m * images + t] = d_hidden.astype(BF)
        row_h[m].start()
        zs[2:3, :] += jnp.sum(d_hidden, axis=0, keepdims=True)
        zs[3:4, :] += jnp.sum(mid * normed, axis=0, keepdims=True)
        zs[4:5, :] += jnp.sum(mid, axis=0, keepdims=True)
    zs[5 + experts : 5 + 2 * experts, :] = 0.25 * ob[0:experts, :]
    zs[16 : 16 + experts, :] = hb[0:experts, :]
    for m in range(2):
        row_h[m].forward()

    masks = head_masks(rows, hw)
    weights = awg[...].reshape(width, 4 * hw)

    def attend_back(i, carry):
        stacked_d = stack_heads(dmx[i], masks)
        stacked_q = stack_heads(qkv[0, i], masks)
        probs_low = prob[i]
        probs = probs_low.astype(F32)
        d_prob = dot_nt(stacked_d, qkv[2, i])
        d_score = probs * (d_prob - jnp.sum(probs * d_prob, axis=-1, keepdims=True))
        d_score = d_score.astype(BF)
        dpj[0, i] = (merge_heads(dot_nn(d_score, qkv[1, i]), masks) * scale).astype(BF)
        dpj[1, i] = (dot_tn(d_score, stacked_q) * scale).astype(BF)
        dpj[2, i] = dot_tn(probs_low, stacked_d).astype(BF)
        return carry

    for m in range(2):
        row_h[m].finish()
        span = slice(m * images, (m + 1) * images)
        block = hlg[span].reshape(full, width)
        dmx[span] = dot_nn(block, weights[:, 3 * hw :]).astype(BF).reshape(images, rows, hw)
        lax.fori_loop(m * images, (m + 1) * images, attend_back, 0)
        low = jnp.zeros((full, width), F32)
        for c in range(3):
            low = low + dot_nt(dpj[c, span].reshape(full, hw), weights[:, c * hw : (c + 1) * hw])
        part[m] = low.astype(BF).reshape(images, rows, width)
        red[m].start()
        if m == 0:
            for op in red_g:
                op.middle()
        red[m].middle()

    flat_in = rin[...].reshape(2 * full, width)
    flat_h = hlg[...].reshape(2 * full, width)
    made = [dot_tn(flat_in, dpj[c].reshape(2 * full, hw)) for c in range(3)]
    made.append(dot_tn(flat_h, mix[...].reshape(2 * full, hw)))
    gaw[...] = jnp.concatenate(made, axis=1).astype(BF).reshape(fsdp, width // fsdp, 4 * hw)
    red_a.start()
    for m in range(2):
        low = red[m].finish()
        normed, inv = norm_parts(x_in[m].astype(F32))
        gx_out[m] = (dh[m] + norm_back(low * gain_one, normed, inv))[:live]
        zs[0:1, :] += jnp.sum(low * normed, axis=0, keepdims=True)
        zs[1:2, :] += jnp.sum(low, axis=0, keepdims=True)
    red_a.middle()

    hops = [(z1, 0, net.sibling), (z2, 1, net.across), (z3, 2, net.partner)]
    for buf, i, dev in hops:
        part_of = slice(0, 16) if i < 2 else slice(0, 24)
        src = zs.at[part_of]
        copy = remote(src, buf, sm_s.at[i], sm_r.at[i], dev)
        copy.start()
        copy.wait()
        zs[part_of] = zs[part_of] + buf[...]
    for k in range(1, net.half):
        remote(zs, z4.at[k], sm_s.at[2 + k], sm_r.at[2 + k], net.line(k)).start()
    for e in range(late):
        gl_out[e] = red_g[e].finish()
    ga_out[...] = red_a.finish()
    sums = zs[...]
    for k in range(1, net.half):
        remote(zs, z4.at[k], sm_s.at[2 + k], sm_r.at[2 + k], net.line(k)).wait()
        sums = sums + z4[k]
    small[...] = sums
    for op in red_g + [red_a] + row_h + red:
        op.drain()


def vmem(shape, dtype=BF):
    return pltpu.VMEM(shape, dtype)


def spec(space):
    return pl.BlockSpec(memory_space=space)


V = pltpu.VMEM
H = pltpu.HBM


def pair_sems(units, half):
    return [DMA((units, half)) for _ in range(4)]


def row_sems(units):
    return [DMA((units,)), DMA((units,)), DMA((units, 2)), DMA((units, 2))]


def per_device(
    patch_embeddings,
    upstream_gradient,
    picture_valid_count,
    assigned_specialists,
    filling_sequence_place,
    leading_scale_factor,
    leading_offset_vector,
    query_value_matrix,
    mixing_projection_matrix,
    mixing_offset_vector,
    central_scale_factor,
    central_offset_vector,
    gating_projection,
    specialist_widen_matrix,
    specialist_inner_offset,
    specialist_contract_matrix,
    specialist_final_offset,
):
    fsdp = lax.axis_size("fsdp")
    half = fsdp // 2
    tp = lax.axis_size("tp")
    own_rows, width = patch_embeddings.shape[1:]
    rows = -(-own_rows // 16) * 16
    images = tp
    full = images * rows
    own = leading_scale_factor.shape[0]
    hw = query_value_matrix.shape[2]
    heads = hw // HEAD_DIM
    experts, _, ff = specialist_widen_matrix.shape
    slots = 2 * own_rows * tp // experts
    early = min(EARLY_GATHER, experts)
    red_early = min(EARLY_REDUCE, experts)
    late = experts - early
    late_red = experts - red_early
    f_index = lax.axis_index("fsdp")

    pad_rows = ((0, 0), (0, rows - own_rows), (0, 0))
    x_own = jnp.pad(patch_embeddings, pad_rows)
    dy_own = jnp.pad(upstream_gradient, pad_rows)
    counts = picture_valid_count.reshape(2 * images)
    small_par = jnp.concatenate(
        [
            leading_scale_factor[None],
            leading_offset_vector[None],
            mixing_offset_vector[None],
            central_scale_factor[None],
            central_offset_vector[None],
            gating_projection.T,
            specialist_final_offset,
        ]
    )
    small_par = jnp.pad(small_par, ((0, 16 - small_par.shape[0]), (0, 128 - own)))
    att_w = jnp.concatenate(
        [query_value_matrix.reshape(own, 3 * hw), mixing_projection_matrix.T], axis=1
    )
    w1 = specialist_widen_matrix
    w2 = specialist_contract_matrix.transpose(0, 2, 1)
    by_image = lambda a, fill: jnp.pad(
        a.reshape(2, -1, images, own_rows),
        ((0, 0), (0, 0), (0, 0), (0, rows - own_rows)),
        constant_values=fill,
    ).reshape(2, -1, full)
    prio_row = by_image(filling_sequence_place, own_rows * tp)
    route = jnp.concatenate(
        [
            by_image(assigned_specialists.transpose(0, 2, 1), -1),
            prio_row,
            jnp.zeros((2, 5, full), jnp.int32),
        ],
        axis=1,
    )
    prio_col = prio_row.reshape(2, full, 1)
    inner = jnp.pad(specialist_inner_offset.astype(F32), ((0, 8 - experts), (0, 0)))

    params = lambda cid: pltpu.CompilerParams(
        collective_id=cid, has_side_effects=True, vmem_limit_bytes=VMEM_LIMIT
    )
    sds = jax.ShapeDtypeStruct
    xg, dyg, rin, qkv, prob, mix, hid, n2g, awg, par, wearly = pl.pallas_call(
        functools.partial(front_kernel, fsdp, early),
        out_shape=[
            sds((2 * images, rows, width), BF),
            sds((2 * images, rows, width), BF),
            sds((2 * images, rows, width), BF),
            sds((3, 2 * images, rows, hw), BF),
            sds((2 * images, heads * rows, rows), BF),
            sds((2 * images, rows, hw), BF),
            sds((2, rows, width), F32),
            sds((2 * images, rows, width), BF),
            sds((fsdp, own, 4 * hw), BF),
            sds((16, width), F32),
            sds((max(early, 1), fsdp, 2, own, ff), BF),
        ],
        in_specs=[spec(pltpu.SMEM), spec(V), spec(V), spec(V), spec(V), spec(H), spec(H)],
        out_specs=[spec(V)] * 10 + [spec(H)],
        scratch_shapes=[
            vmem((fsdp, 16, 128)),
            vmem((2, images, rows, width)),
            vmem((2, 2, rows, width)),
            vmem((2, rows, width)),
        ]
        + pair_sems(2 + early, half)
        + row_sems(6)
        + row_sems(2)
        + [DMA((2 * experts,))],
        compiler_params=params(1),
        name="front",
    )(counts, x_own, dy_own, small_par, att_w, w1, w2)

    wide = 2 * width + 256
    total, gout, glate, hb, ob = pl.pallas_call(
        functools.partial(expert_kernel, fsdp, early, red_early),
        out_shape=[
            sds((2, rows, wide), F32),
            sds((max(red_early, 1), 2, own, ff), F32),
            sds((max(late_red, 1), fsdp, 2, own, ff), BF),
            sds((8, ff), F32),
            sds((8, width), F32),
        ],
        in_specs=[spec(V), spec(V), spec(V), spec(H), spec(H), spec(H), spec(V), spec(V), spec(V)],
        out_specs=[spec(V), spec(V), spec(H), spec(V), spec(V)],
        scratch_shapes=[
            vmem((experts, fsdp, 2, own, ff)),
            vmem((2, full, wide), F32),
            vmem((2, slots, full)),
            vmem((2, slots, width)),
            vmem((2, slots, width)),
            vmem((2, slots, ff)),
            vmem((2, slots, ff)),
            vmem((2, 8, full), jnp.int32),
            vmem((2, 8, full), F32),
            vmem((2, images, rows, wide)),
            vmem((2, 2, rows, wide)),
            vmem((2, rows, wide)),
            vmem((max(red_early, 1), half, 2, own, ff)),
            vmem((max(red_early, 1), half, 2, own, ff)),
        ]
        + pair_sems(max(late, 1), half)
        + pair_sems(max(red_early, 1), half)
        + row_sems(2)
        + [DMA((3 * experts,)), DMA((max(late_red, 1),))],
        compiler_params=params(2),
        name="experts",
    )(n2g, dyg, par, wearly, w1, w2, inner, route, prio_col)

    y_out, gx_out, ga_out, gl_out, small = pl.pallas_call(
        functools.partial(back_kernel, fsdp, experts),
        out_shape=[
            sds((2, own_rows, width), F32),
            sds((2, own_rows, width), F32),
            sds((own, 4 * hw), F32),
            sds((late_red, 2, own, ff), F32),
            sds((24, width), F32),
        ],
        in_specs=[spec(V)] * 15,
        out_specs=[spec(V)] * 5,
        scratch_shapes=[
            vmem((2 * images, rows, width)),
            vmem((2 * images, rows, hw)),
            vmem((3, 2 * images, rows, hw)),
            vmem((2, rows, width), F32),
            vmem((fsdp, own, 4 * hw)),
            vmem((2, images, rows, width)),
            vmem((2, 2, rows, width)),
            vmem((2, rows, width)),
            vmem((late_red, half, 2, own, ff)),
            vmem((late_red, half, 2, own, ff)),
            vmem((half, own, 4 * hw)),
            vmem((half, own, 4 * hw)),
            vmem((16, width), F32),
            vmem((16, width), F32),
            vmem((24, width), F32),
            vmem((half, 24, width), F32),
            vmem((24, width), F32),
        ]
        + pair_sems(late_red + 1, half)
        + row_sems(2)
        + row_sems(2)
        + [DMA((2 + half,)), DMA((2 + half,))],
        compiler_params=params(3),
        name="back",
    )(total, hid, n2g, dy_own, x_own, xg, rin, qkv, prob, mix, awg, par, glate, hb, ob)

    grads = jnp.concatenate([gout, gl_out], axis=0)
    cut = lax.dynamic_slice_in_dim(small, f_index * own, own, 1)
    return (
        y_out,
        gx_out,
        cut[0],
        cut[1],
        ga_out[:, : 3 * hw].reshape(own, 3, hw),
        ga_out[:, 3 * hw :].T,
        cut[2],
        cut[3],
        cut[4],
        cut[5 : 5 + experts].T,
        grads[:, 0],
        small[16 : 16 + experts],
        grads[:, 1].transpose(0, 2, 1),
        cut[5 + experts : 5 + 2 * experts],
    )


def solution(mesh):
    placed = (
        P(None, ("fsdp", "tp"), None),
        P(None, ("fsdp", "tp"), None),
        P(None, "fsdp"),
        P(None, "fsdp", None),
        P(None, "fsdp", None),
        P("fsdp"),
        P("fsdp"),
        P("fsdp", None, "tp"),
        P("tp", "fsdp"),
        P("fsdp"),
        P("fsdp"),
        P("fsdp"),
        P("fsdp", None),
        P(None, "fsdp", "tp"),
        P(None, "tp"),
        P(None, "tp", "fsdp"),
        P(None, "fsdp"),
    )
    return jax.shard_map(
        per_device,
        mesh=mesh,
        in_specs=placed,
        out_specs=(
            P(None, ("fsdp", "tp"), None),
            P(None, ("fsdp", "tp"), None),
            P("fsdp"),
            P("fsdp"),
            P("fsdp", None, "tp"),
            P("tp", "fsdp"),
            P("fsdp"),
            P("fsdp"),
            P("fsdp"),
            P("fsdp", None),
            P(None, "fsdp", "tp"),
            P(None, "tp"),
            P(None, "tp", "fsdp"),
            P(None, "fsdp"),
        ),
        check_vma=False,
    )
```

```python
import functools
import math

import jax
import jax.numpy as jnp
from jax import lax
from jax.experimental import pallas as pl
from jax.experimental.pallas import tpu as pltpu
from jax.sharding import PartitionSpec as P

HEAD_DIM = 64
NORM_EPS = 1e-06
MASK_FILL = -1000000000.0
MESH = pl.DeviceIdType.MESH
BF = jnp.bfloat16
F32 = jnp.float32
DMA = pltpu.SemaphoreType.DMA

VMEM_LIMIT = 63 << 20


def dot_nn(a, b):
    return lax.dot_general(a, b, (((1,), (0,)), ((), ())), preferred_element_type=F32)


def dot_nt(a, b):
    return lax.dot_general(a, b, (((1,), (1,)), ((), ())), preferred_element_type=F32)


def dot_tn(a, b):
    return lax.dot_general(a, b, (((0,), (0,)), ((), ())), preferred_element_type=F32)


def norm_parts(values):
    row_mean = jnp.mean(values, axis=-1, keepdims=True)
    centred = values - row_mean
    row_var = jnp.mean(centred * centred, axis=-1, keepdims=True)
    inv_std = lax.rsqrt(row_var + NORM_EPS)
    return centred * inv_std, inv_std


def norm_back(scaled, normed, inv_std):
    return inv_std * (
        scaled
        - jnp.mean(scaled, axis=-1, keepdims=True)
        - normed * jnp.mean(scaled * normed, axis=-1, keepdims=True)
    )


def gelu_parts(x):
    z = jnp.abs(x) * (1.0 / math.sqrt(2.0))
    t = 1.0 / (1.0 + 0.3275911 * z)
    expo = jnp.exp(-0.5 * x * x)
    poly = t * (
        0.254829592
        + t * (-0.284496736 + t * (1.421413741 + t * (-1.453152027 + t * 1.061405429)))
    )
    tail = 0.5 * poly * expo
    cdf = jnp.where(x >= 0, 1.0 - tail, tail)
    return x * cdf, cdf + x * (expo * (1.0 / math.sqrt(2.0 * math.pi)))


def remote(src, dst, send, recv, dev):
    return pltpu.make_async_remote_copy(
        src_ref=src, dst_ref=dst, send_sem=send, recv_sem=recv, device_id=dev, device_id_type=MESH
    )


def half_of(count):
    return count // 2


class Net:
    def __init__(self, fsdp):
        self.fsdp = fsdp
        self.half = fsdp // 2
        self.f = f = lax.axis_index("fsdp")
        self.t = t = lax.axis_index("tp")
        self.pf = f + 1 - 2 * lax.rem(f, 2)
        self.t2 = lax.rem(t + 2, 4)
        self.s = t + 1 - 2 * lax.rem(t, 2)
        self.s2 = lax.rem(self.s + 2, 4)
        self.partner = (self.pf, t)
        self.across = (f, self.t2)
        self.sibling = (f, self.s)

    def at(self, base, k):
        return lax.rem(base + 2 * k + self.fsdp, self.fsdp)

    def line(self, k):
        return (self.at(self.f, k), self.t)

    def barrier(self):
        sem = pltpu.get_barrier_semaphore()
        peers = [self.partner, self.across, self.sibling]
        peers += [self.line(k) for k in range(1, self.half)]
        for peer in peers:
            pl.semaphore_signal(sem, inc=1, device_id=peer, device_id_type=MESH)
        pl.semaphore_wait(sem, len(peers))


class Gather:
    def __init__(self, net, block, sems, unit):
        self.net, self.block, self.unit = net, block, unit
        self.ps, self.pr, self.ls, self.lr = sems

    def _pair(self, j, k):
        u = self.unit
        return remote(self.block(j), self.block(j), self.ps.at[u, k], self.pr.at[u, k], self.net.partner)

    def _line(self, j, k):
        u = self.unit
        return remote(self.block(j), self.block(j), self.ls.at[u, k], self.lr.at[u, k], self.net.line(k))

    def send(self, steps):
        for k in steps:
            if k == 0:
                self._pair(self.net.f, 0).start()
            else:
                self._line(self.net.f, k).start()

    def forward(self, steps):
        n = self.net
        for k in steps:
            j = n.at(n.f, -k)
            self._line(j, k).wait_recv()
            self._pair(j, k).start()

    def finish(self):
        n = self.net
        for k in range(n.half):
            self._pair(n.at(n.pf, -k), k).wait_recv()

    def drain(self):
        n = self.net
        for k in range(n.half):
            self._pair(n.f, k).wait_send()
        for k in range(1, n.half):
            self._line(n.f, k).wait_send()


class Reduce:
    def __init__(self, net, block, first, second, sems, unit, fetch=None):
        self.net, self.block, self.first, self.second, self.unit = net, block, first, second, unit
        self.ps, self.pr, self.ls, self.lr = sems
        self.fetch = fetch

    def _pair(self, k):
        n, u = self.net, self.unit
        return remote(
            self.block(n.at(n.pf, k)), self.first(k), self.ps.at[u, k], self.pr.at[u, k], n.partner
        )

    def _line(self, k):
        n, u = self.net, self.unit
        return remote(
            self.block(n.at(n.f, k)), self.second(k), self.ls.at[u, k], self.lr.at[u, k], n.line(k)
        )

    def start(self):
        for k in list(range(1, self.net.half)) + [0]:
            self._pair(k).start()

    def middle(self):
        n = self.net
        for k in range(1, n.half):
            self._pair(k).wait_recv()
            mine = self.block(n.at(n.f, k))
            mine[...] = (mine[...].astype(F32) + self.first(k)[...].astype(F32)).astype(BF)
            self._line(k).start()

    def _load(self, k):
        return pltpu.make_async_copy(self.second(k), self.first(k), self.fetch.at[self.unit, k])

    def collect(self):
        for k in range(1, self.net.half):
            self._line(k).wait_recv()
            self._load(k).start()

    def finish(self):
        n = self.net
        self._pair(0).wait_recv()
        total = self.block(n.f)[...].astype(F32) + self.first(0)[...].astype(F32)
        for k in range(1, n.half):
            if self.fetch is None:
                self._line(k).wait_recv()
                total = total + self.second(k)[...].astype(F32)
            else:
                self._load(k).wait()
                total = total + self.first(k)[...].astype(F32)
        return total

    def drain(self):
        for k in range(self.net.half):
            self._pair(k).wait_send()
        for k in range(1, self.net.half):
            self._line(k).wait_send()


class RowGather:
    def __init__(self, net, block, sems, unit):
        self.net, self.block, self.unit = net, block, unit
        self.ys, self.yr, self.cs, self.cr = sems

    def _y(self, j):
        u = self.unit
        return remote(self.block(j), self.block(j), self.ys.at[u], self.yr.at[u], self.net.across)

    def _c(self, j, k):
        u = self.unit
        return remote(self.block(j), self.block(j), self.cs.at[u, k], self.cr.at[u, k], self.net.sibling)

    def start(self):
        self._y(self.net.t).start()
        self._c(self.net.t, 0).start()

    def forward(self):
        n = self.net
        self._y(n.t2).wait_recv()
        self._c(n.t2, 1).start()

    def finish(self):
        n = self.net
        self._c(n.s, 0).wait_recv()
        self._c(n.s2, 1).wait_recv()

    def drain(self):
        n = self.net
        self._y(n.t).wait_send()
        self._c(n.t, 0).wait_send()
        self._c(n.t2, 1).wait_send()


class RowReduce:
    def __init__(self, net, block, first, second, sems, unit):
        self.net, self.block, self.first, self.second, self.unit = net, block, first, second, unit
        self.ys, self.yr, self.cs, self.cr = sems

    def _c(self, k):
        n, u = self.net, self.unit
        j = n.s2 if k == 0 else n.s
        return remote(self.block(j), self.first(k), self.cs.at[u, k], self.cr.at[u, k], n.sibling)

    def _y(self):
        n, u = self.net, self.unit
        return remote(self.block(n.t2), self.second(), self.ys.at[u], self.yr.at[u], n.across)

    def start(self):
        self._c(0).start()
        self._c(1).start()

    def middle(self, add=None):
        n = self.net
        self._c(0).wait_recv()
        mine = self.block(n.t2)
        if add is None:
            mine[...] = (mine[...].astype(F32) + self.first(0)[...].astype(F32)).astype(BF)
        else:
            add(mine, self.first(0))
        self._y().start()

    def finish(self):
        n = self.net
        self._c(1).wait_recv()
        self._y().wait_recv()
        return (
            self.block(n.t)[...].astype(F32)
            + self.first(1)[...].astype(F32)
            + self.second()[...].astype(F32)
        )

    def drain(self):
        self._c(0).wait_send()
        self._c(1).wait_send()
        self._y().wait_send()


def head_masks(rows, width):
    lane = lax.broadcasted_iota(jnp.int32, (rows, width), 1)
    return [
        (lane >= h * HEAD_DIM) & (lane < (h + 1) * HEAD_DIM) for h in range(width // HEAD_DIM)
    ]


def stack_heads(rows, masks):
    zero = jnp.zeros_like(rows)
    return jnp.concatenate([jnp.where(mask, rows, zero) for mask in masks], axis=0)


def merge_heads(stacked, masks):
    count = masks[0].shape[0]
    total = jnp.where(masks[0], stacked[:count], 0.0)
    for h in range(1, len(masks)):
        total = jnp.where(masks[h], stacked[h * count : (h + 1) * count], total)
    return total


def block_kernel(fsdp, experts, *refs):
    it = iter(refs)
    take = lambda n: [next(it) for _ in range(n)]
    cnt, x_in, dy_in = take(3)
    vectors = take(7)
    qkv_in, mix_in, w1_in, w2_in, b1_in, route_in, prio_in = take(7)
    y_out, gx_out, gq_out, gm_out, g1_out, g2_out = take(6)
    vec_out = take(5)
    router_out, ob_out, hb_out, r2 = take(4)
    rowsb, dyg, rin, qkv, prob, mix, hid, awg, par, parg = take(10)
    wbuf, part, first, second, r1, a1, a2 = take(7)
    hot_s, gts, xs, vs, gas, dps, sid, rp, dmx, hb, ob, b1 = take(12)
    z1, z2, z3, z4, zs = take(5)
    ga = take(4)
    rs = take(4)
    rg = take(4)
    rr = take(4)
    loc, sm_s, sm_r, fetch = take(4)
    net = Net(fsdp)
    f, t = net.f, net.t
    live, width = x_in.shape[1], x_in.shape[2]
    rows = rowsb.shape[1]
    images = rowsb.shape[0] // 2
    full = images * rows
    hw = qkv.shape[3]
    own = width // fsdp
    order = []
    for k in range(1, half_of(fsdp)):
        for step in (k, half_of(fsdp) - k):
            if step not in order:
                order.append(step)
    third = -(-len(order) // 3)
    near, far, last = order[:third], order[third : 2 * third], order[2 * third :]
    no_rows = jnp.zeros((rows - live, width), F32)

    def padded(ref, m):
        return jnp.concatenate([ref[m].astype(F32), no_rows], axis=0)

    slots = hot_s.shape[1]
    ff = wbuf.shape[4]
    wide = 2 * width
    scale = 1.0 / math.sqrt(HEAD_DIM)

    gat_par = Gather(net, lambda j: parg.at[j], ga, 0)
    gat_aw = Gather(net, lambda j: awg.at[j], ga, 1)
    gat = lambda e: Gather(net, lambda j: wbuf.at[e, j], ga, 2 + e)
    red_e = lambda e: Reduce(
        net, lambda j: wbuf.at[e, j], lambda k: r1.at[e, k], lambda k: r2.at[e, k], rs, e, fetch
    )
    red_a = Reduce(net, lambda j: awg.at[j], lambda k: a1.at[k], lambda k: a2.at[k], rs, experts)

    def row_gather(buf, m, unit):
        return RowGather(net, lambda j: buf.at[m * images + j], rg, unit)

    def row_reduce(m, lo, hi, unit):
        return RowReduce(
            net,
            lambda j: part.at[m, j, :, lo:hi],
            lambda k: first.at[m, k, :, lo:hi],
            lambda: second.at[m, :, lo:hi],
            rr,
            unit,
        )

    row_x = [row_gather(rowsb, m, m) for m in range(2)]
    row_dy = [row_gather(dyg, m, 2 + m) for m in range(2)]
    row_n2 = [row_gather(rowsb, m, 4 + m) for m in range(2)]
    row_h = [row_gather(rowsb, m, 6 + m) for m in range(2)]
    red_att = [row_reduce(m, 0, width, m) for m in range(2)]
    red_mid = [row_reduce(m, width, wide + 256, 2 + m) for m in range(2)]
    red_out = [row_reduce(m, 0, width, 4 + m) for m in range(2)]
    red_low = [row_reduce(m, width, wide, 6 + m) for m in range(2)]

    copies = []
    for e in range(experts):
        for i, src in enumerate((w1_in, w2_in)):
            copies.append(pltpu.make_async_copy(src.at[e], wbuf.at[e, f, i], loc.at[2 * e + i]))
    for copy in copies:
        copy.start()
    net.barrier()
    for m in range(2):
        rowsb[m * images + t] = padded(x_in, m).astype(BF)
        row_x[m].start()
    zs[...] = jnp.zeros_like(zs)
    at = 0
    for ref in vectors:
        count = ref.shape[0]
        zs[at : at + count, :own] = ref[...].astype(F32)
        at += count
    parg[f] = zs[0:16, :128].astype(BF)
    gat_par.send([0] + order)
    awg[f] = jnp.concatenate([qkv_in[0], qkv_in[1], qkv_in[2], mix_in[...]], axis=1)
    gat_aw.send([0] + order)
    for m in range(2):
        dyg[m * images + t] = padded(dy_in, m).astype(BF)
    b1[0:experts, :] = b1_in[...].astype(F32)
    gat_par.forward(order)
    row_x[0].forward()
    gat_par.finish()

    place = lax.broadcasted_iota(jnp.int32, (128, width), 0)
    column = lax.broadcasted_iota(jnp.int32, (128, width), 1)
    joined = jnp.zeros((16, width), F32)
    for j in range(fsdp):
        hot = ((column == place + j * own) & (place < own)).astype(BF)
        joined = joined + dot_nn(parg[j], hot)
    par[...] = joined
    gain_one, shift_one = par[0:1, :], par[1:2, :]
    mix_bias, gain_two, shift_two = par[2:3, :], par[3:4, :], par[4:5, :]

    def first_norm(i, carry):
        normed, _ = norm_parts(rowsb[i].astype(F32))
        rin[i] = (normed * gain_one + shift_one).astype(BF)
        return carry

    gat_aw.forward(order)
    for copy in copies:
        copy.wait()
    def send_pair(group):
        for steps in ([0], near, far, last):
            for e in group:
                gat(e).send(steps)

    def forward_pair(group, steps):
        for e in group:
            gat(e).forward(steps)

    send_pair((0, 1))
    row_x[0].finish()
    lax.fori_loop(0, images, first_norm, 0)
    row_x[1].forward()
    for m in range(2):
        row_dy[m].start()
    row_x[1].finish()
    lax.fori_loop(images, 2 * images, first_norm, 0)
    gat_aw.finish()

    def project(m, carry):
        span = pl.ds(m * images, images)
        weights = awg[...].reshape(width, 4 * hw)
        block = rin[span].reshape(full, width)
        for c in range(3):
            made = dot_nn(block, weights[:, c * hw : (c + 1) * hw])
            qkv[c, span] = made.astype(BF).reshape(images, rows, hw)
        return carry

    lax.fori_loop(0, 2, project, 0)
    masks = head_masks(rows, hw)
    key_pos = lax.broadcasted_iota(jnp.int32, (len(masks) * rows, rows), 1)

    def attend(i, carry):
        stacked = stack_heads(qkv[0, i], masks)
        scores = dot_nt(stacked, qkv[1, i]) * scale
        scores = jnp.where(key_pos < cnt[i // images, lax.rem(i, images)], scores, MASK_FILL)
        expo = jnp.exp(scores - jnp.max(scores, axis=-1, keepdims=True))
        probs = (expo / jnp.sum(expo, axis=-1, keepdims=True)).astype(BF)
        prob[i] = probs
        mix[i] = merge_heads(dot_nn(probs, qkv[2, i]), masks).astype(BF)
        return carry

    for op in row_x:
        op.drain()
    out_w = awg[...].reshape(width, 4 * hw)[:, 3 * hw :]
    for m in range(2):
        lax.fori_loop(m * images, (m + 1) * images, attend, 0)
        block = mix[m * images : (m + 1) * images].reshape(full, hw)
        part[m, :, :, :width] = dot_nt(block, out_w).astype(BF).reshape(images, rows, width)
        red_att[m].start()
        if m == 0:
            for op in row_dy:
                op.forward()
            red_att[0].middle()
            forward_pair((0, 1), near)
            send_pair((2, 3))
    red_att[1].middle()

    def second_norm(m, carry):
        hidden = padded(x_in, m) + row_reduce(m, 0, width, m).finish() + mix_bias
        hid[m] = hidden
        normed, _ = norm_parts(hidden)
        rowsb[m * images + t] = (normed * gain_two + shift_two).astype(BF)
        row_gather(rowsb, m, 4 + m).start()
        return carry

    lax.fori_loop(0, 2, second_norm, 0)
    for m in range(2):
        row_n2[m].forward()
        row_dy[m].finish()
        red_att[m].drain()
        part[m] = jnp.zeros_like(part[m])
    forward_pair((0, 1), far)

    hb[...] = jnp.zeros_like(hb)
    ob[...] = jnp.zeros_like(ob)

    def find_slots(m, carry):
        by_image = lambda row, fill: jnp.concatenate(
            sum(
                [
                    [row[:, i * live : (i + 1) * live], jnp.full((1, rows - live), fill, jnp.int32)]
                    for i in range(images)
                ],
                [],
            ),
            axis=1,
        )
        e0, e1 = by_image(route_in[m, 0:1, :], -1), by_image(route_in[m, 1:2, :], -1)
        rank = by_image(prio_in[m], live * images)
        high = rank // 32
        digit = lax.broadcasted_iota(jnp.int32, (16, full), 0)
        digits = jnp.where(digit == 0, high, jnp.where(digit == 1, rank - 32 * high, 0))
        digit = lax.broadcasted_iota(jnp.int32, (16, 128), 0)
        worth = jnp.where(digit == 0, 32, jnp.where(digit == 1, 1, 0))
        column = dot_tn(digits.astype(F32).astype(BF), worth.astype(F32).astype(BF))[:, 0:1]
        lower = (column < rank.astype(F32)).astype(BF)
        kind = lax.broadcasted_iota(jnp.int32, (16, full), 0)
        named = jnp.where(kind < experts, e0, e1) == jnp.where(kind < experts, kind, kind - experts)
        named = jnp.where((kind < 2 * experts) & named, 1.0, 0.0)
        counts = dot_nn(named.astype(BF), lower)
        totals = jnp.sum(named, axis=1, keepdims=True)
        for k in range(2):
            where_slot = jnp.full((1, full), -1.0, F32)
            for e in range(experts):
                c = k * experts + e
                before = counts[c : c + 1, :]
                if k == 1:
                    before = before + totals[e : e + 1, :]
                kept = (named[c : c + 1, :] > 0.5) & (before < slots)
                where_slot = jnp.where(kept, before + e * slots, where_slot)
            sid[m, k : k + 1, :] = where_slot.astype(jnp.int32)
        return carry

    lax.fori_loop(0, 2, find_slots, 0)
    for m in range(2):
        row_n2[m].finish()
        n2m = rowsb[m * images : (m + 1) * images].reshape(full, width)
        logits = dot_nt(par[...].astype(BF), n2m)[5 : 5 + experts, :]
        expo = jnp.exp(logits - jnp.max(logits, axis=0, keepdims=True))
        rp[m, 0:experts, :] = expo / jnp.sum(expo, axis=0, keepdims=True)
        row_n2[m].drain()
    forward_pair((0, 1), last)

    slot_row = lax.broadcasted_iota(jnp.int32, (slots, full), 0)
    lane = lax.broadcasted_iota(jnp.int32, (slots, 128), 1)

    def add_split(mine, other):
        mine[:, :width] = (mine[:, :width].astype(F32) + other[:, :width].astype(F32)).astype(BF)
        pair = [mine[:, width : width + 128].astype(F32), mine[:, width + 128 :].astype(F32)]
        pair += [other[:, width : width + 128].astype(F32), other[:, width + 128 :].astype(F32)]
        value = (pair[0] + pair[2]) + (pair[1] + pair[3])
        high = value.astype(BF)
        mine[:, width : width + 128] = high
        mine[:, width + 128 :] = (value - high.astype(F32)).astype(BF)

    schedule = {
        (0, 1): lambda: forward_pair((2, 3), near),
        (1, 0): lambda: forward_pair((2, 3), far),
        (1, 3): lambda: forward_pair((2,), last),
        (2, 1): lambda: (forward_pair((3,), last), red_e(0).start(), red_e(1).start()),
        (2, 3): lambda: red_e(2).start(),
        (3, 2): lambda: red_mid[0].middle(add_split),
        (3, 3): lambda: (red_e(3).start(), red_mid[1].middle(add_split)),
    }

    def ticks(e, point):
        for (expert_at, point_at), act in schedule.items():
            if point_at == point:

                @pl.when(e == expert_at)
                def _():
                    act()

    def expert(e, carry):
        def dispatch(m, carry):
            hot = (slot_row + e * slots == sid[m, 0:1, :]) | (slot_row + e * slots == sid[m, 1:2, :])
            hot_s[m] = jnp.where(hot, 1.0, 0.0).astype(BF)
            gate = jnp.sum(jnp.where(hot, rp[m, pl.ds(e, 1), :], 0.0), axis=1, keepdims=True)
            gts[m] = jnp.broadcast_to(gate, (slots, 128))
            n2m = rowsb[pl.ds(m * images, images)].reshape(full, width)
            xs[m] = dot_nn(hot_s[m], n2m).astype(BF)
            dym = dyg[pl.ds(m * images, images)].reshape(full, width)
            vals = dot_nn(hot_s[m], dym)
            ob[pl.ds(e, 1), :] += jnp.sum(gate * vals, axis=0, keepdims=True)
            vs[m] = vals.astype(BF)
            return carry

        lax.fori_loop(0, 2, dispatch, 0)
        ticks(e, 0)
        gat(e).finish()


        def hidden_units(m, carry):
            gate = gts[m][:, 0:1]
            d_gate = jnp.zeros((slots, 1), F32)
            for lo in range(0, ff, 256):
                span = slice(lo, lo + 256)
                pre = dot_nn(xs[m], wbuf[e, :, 0, :, span].reshape(width, 256))
                act, slope = gelu_parts(pre + b1[pl.ds(e, 1), span])
                gas[m, :, span] = (gate * act).astype(BF)
                back = dot_nn(vs[m], wbuf[e, :, 1, :, span].reshape(width, 256))
                d_gate = d_gate + jnp.sum(act * back, axis=1, keepdims=True)
                d_pre = gate * slope * back
                hb[pl.ds(e, 1), span] += jnp.sum(d_pre, axis=0, keepdims=True)
                dps[m, :, span] = d_pre.astype(BF)
            high = d_gate.astype(BF)
            low = (d_gate - high.astype(F32)).astype(BF)
            zero = jnp.zeros((slots, 128), BF)
            extra = [
                jnp.where(lane == e, high, jnp.where(lane == 16 + e, jnp.ones_like(zero), zero)),
                jnp.where(lane == e, low, zero),
            ]
            lower, upper = slice(0, fsdp // 2), slice(fsdp // 2, fsdp)
            part_of = lambda i, cut: wbuf[e, cut, i].reshape(width // 2, ff)
            pieces = [
                lambda: dot_nt(gas[m], part_of(1, lower)).astype(BF),
                lambda: dot_nt(gas[m], part_of(1, upper)).astype(BF),
                lambda: dot_nt(dps[m], part_of(0, lower)).astype(BF),
                lambda: dot_nt(dps[m], part_of(0, upper)).astype(BF),
                lambda: jnp.concatenate(extra, axis=1),
            ]
            lo = 0
            for make in pieces:
                piece = make()
                span = slice(lo, lo + piece.shape[1])
                lo = span.stop
                more = dot_tn(hot_s[m], piece).reshape(images, rows, piece.shape[1])
                part[m, :, :, span] = (part[m, :, :, span].astype(F32) + more).astype(BF)

            @pl.when(e == experts - 1)
            def _():
                row_reduce(m, width, wide + 256, 2 + m).start()

            @pl.when(m == 0)
            def _():
                ticks(e, 1)

            return carry

        lax.fori_loop(0, 2, hidden_units, 0)
        ticks(e, 2)
        gat(e).drain()

        two = 2 * slots
        for n in range(2):
            cut = slice(n * (width // 2), (n + 1) * (width // 2))
            blocks = slice(n * fsdp // 2, (n + 1) * fsdp // 2)
            for i, (left, right) in enumerate(((xs, dps), (vs, gas))):
                made = dot_tn(left[:, :, cut].reshape(two, width // 2), right[...].reshape(two, ff))
                wbuf[e, blocks, i] = made.astype(BF).reshape(fsdp // 2, own, ff)
        ticks(e, 3)
        return carry

    lax.fori_loop(0, experts, expert, 0)

    red_e(0).middle()

    zs[...] = jnp.zeros_like(zs)
    lane = lax.broadcasted_iota(jnp.int32, (rows, 128), 1)
    lane16 = lax.broadcasted_iota(jnp.int32, (rows, 16), 1)
    router_lane = (lane16 >= 5) & (lane16 < 5 + experts)

    def router_back(m, carry):
        hidden = hid[m]
        normed, inv = norm_parts(hidden)
        dy = dyg[m * images + t].astype(F32)
        n2 = rowsb[m * images + t]
        logits = jnp.where(router_lane, dot_nt(n2, par[...].astype(BF)), -1e30)
        expo = jnp.exp(logits - jnp.max(logits, axis=1, keepdims=True))
        probs = expo / jnp.sum(expo, axis=1, keepdims=True)
        got = row_reduce(m, width, wide + 256, 2 + m).finish()
        sums = got[:, width : width + 128] + got[:, width + 128 :]
        pcol, qcol, out = [], [], hidden
        for e in range(experts):
            p_e = jnp.sum(jnp.where(lane16 == 5 + e, probs, 0.0), axis=1, keepdims=True)
            kept = 0.25 * jnp.sum(jnp.where(lane == 16 + e, sums, 0.0), axis=1, keepdims=True)
            q_e = jnp.sum(jnp.where(lane == e, sums, 0.0), axis=1, keepdims=True)
            bias = par[5 + experts + e : 6 + experts + e, :]
            q_e = q_e + kept * jnp.sum(dy * bias, axis=1, keepdims=True)
            out = out + (kept * p_e) * bias
            pcol.append(p_e)
            qcol.append(q_e)
        y_out[m] = out[:live]
        mean_q = pcol[0] * qcol[0]
        for e in range(1, experts):
            mean_q = mean_q + pcol[e] * qcol[e]
        mid = got[:, :width]
        for e in range(experts):
            d_logit = (pcol[e] * (qcol[e] - mean_q)).astype(BF).astype(F32)
            mid = mid + d_logit * par[5 + e : 6 + e, :]
            zs[5 + e : 6 + e, :] += jnp.sum(d_logit * n2.astype(F32), axis=0, keepdims=True)
        d_hidden = dy + norm_back(mid * gain_two, normed, inv)
        hid[m] = d_hidden
        rowsb[m * images + t] = d_hidden.astype(BF)
        row_gather(rowsb, m, 6 + m).start()
        zs[2:3, :] += jnp.sum(d_hidden, axis=0, keepdims=True)
        zs[3:4, :] += jnp.sum(mid * normed, axis=0, keepdims=True)
        zs[4:5, :] += jnp.sum(mid, axis=0, keepdims=True)
        return carry

    lax.fori_loop(0, 2, router_back, 0)
    zs[5 + experts : 5 + 2 * experts, :] = 0.25 * ob[0:experts, :]
    zs[16 : 16 + experts, :] = hb[0:experts, :]
    for m in range(2):
        row_h[m].forward()
        red_mid[m].drain()
    red_e(1).middle()

    def attend_back(i, carry):
        stacked_d = stack_heads(dmx[i], masks)
        stacked_q = stack_heads(qkv[0, i], masks)
        probs_low = prob[i]
        probs = probs_low.astype(F32)
        d_prob = dot_nt(stacked_d, qkv[2, i])
        d_score = probs * (d_prob - jnp.sum(probs * d_prob, axis=-1, keepdims=True))
        d_score = d_score.astype(BF)
        qkv[0, i] = (merge_heads(dot_nn(d_score, qkv[1, i]), masks) * scale).astype(BF)
        qkv[1, i] = (dot_tn(d_score, stacked_q) * scale).astype(BF)
        qkv[2, i] = dot_tn(probs_low, stacked_d).astype(BF)
        return carry

    for m in range(2):
        row_h[m].finish()
        red_out[m].start()
        span = slice(m * images, (m + 1) * images)
        block = rowsb[span].reshape(full, width)
        weights = awg[...].reshape(width, 4 * hw)
        dmx[span] = dot_nn(block, weights[:, 3 * hw :]).astype(BF).reshape(images, rows, hw)
        lax.fori_loop(m * images, (m + 1) * images, attend_back, 0)
        for n in range(2):
            cut = slice(n * fsdp // 2, (n + 1) * fsdp // 2)
            weights = awg[cut].reshape(width // 2, 4 * hw)
            low = jnp.zeros((full, width // 2), F32)
            for c in range(3):
                low = low + dot_nt(qkv[c, span].reshape(full, hw), weights[:, c * hw : (c + 1) * hw])
            here = slice(n * (width // 2), (n + 1) * (width // 2))
            zs[1:2, here] += jnp.sum(low, axis=0, keepdims=True)
            normed = rin[span, :, here].astype(F32).reshape(full, width // 2)
            zs[0:1, here] += jnp.sum(low * normed, axis=0, keepdims=True)
            at = width + n * (width // 2)
            part[m, :, :, at : at + width // 2] = low.astype(BF).reshape(images, rows, width // 2)
        red_low[m].start()
        red_low[m].middle()
        red_out[m].middle()

    gat_aw.drain()

    def att_grads(n, carry):
        cut = pl.ds(pl.multiple_of(n * (width // 2), 128), width // 2)
        flat_in = rin[:, :, cut].reshape(2 * full, width // 2)
        made = [dot_tn(flat_in, qkv[c].reshape(2 * full, hw)) for c in range(3)]
        flat_h = rowsb[:, :, cut].reshape(2 * full, width // 2)
        made.append(dot_tn(flat_h, mix[...].reshape(2 * full, hw)))
        joined = jnp.concatenate(made, axis=1).astype(BF)
        awg[pl.ds(n * (fsdp // 2), fsdp // 2)] = joined.reshape(fsdp // 2, own, 4 * hw)
        return carry

    zs[0:1, :] = (zs[0:1, :] - shift_one * zs[1:2, :]) / gain_one

    hops = [(z1, 16, net.sibling), (z2, 16, net.across), (z3, 24, net.partner)]

    def hop(i):
        buf, count, dev = hops[i]
        return remote(zs.at[0:count], buf, sm_s.at[i], sm_r.at[i], dev)

    def hop_end(i):
        buf, count, dev = hops[i]
        hop(i).wait()
        zs[0:count] = zs[0:count] + buf[...]

    hop(0).start()
    lax.fori_loop(0, 2, att_grads, 0)
    red_a.start()
    red_e(2).middle()
    hop_end(0)
    hop(1).start()

    def first_back(m, carry):
        low = row_reduce(m, width, wide, 6 + m).finish()
        normed, inv = norm_parts(padded(x_in, m))
        gx_out[m] = (hid[m] + norm_back(low * gain_one, normed, inv))[:live]
        return carry

    lax.fori_loop(0, 2, first_back, 0)
    hop_end(1)
    hop(2).start()
    for m in range(2):
        y_out[m] += red_out[m].finish()[:live]
    hop_end(2)
    for k in range(1, net.half):
        remote(zs, z4.at[k], sm_s.at[2 + k], sm_r.at[2 + k], net.line(k)).start()
    red_e(3).middle()
    red_a.middle()
    for e in range(experts - 1):
        red_e(e).collect()
    outs = []
    red_e(experts - 1).collect()
    for e in range(experts):
        both = red_e(e).finish()
        for i, dst in enumerate((g1_out, g2_out)):
            if e > 1:
                outs[2 * e - 4 + i].wait()
            stage = hid.at[e % 2, i * own : (i + 1) * own]
            stage[...] = both[i]
            outs.append(pltpu.make_async_copy(stage, dst.at[e], loc.at[2 * e + i]))
            outs[-1].start()
    made = red_a.finish()
    for c in range(3):
        gq_out[c] = made[:, c * hw : (c + 1) * hw]
    gm_out[...] = made[:, 3 * hw :]
    sums = zs[...]
    for k in range(1, net.half):
        remote(zs, z4.at[k], sm_s.at[2 + k], sm_r.at[2 + k], net.line(k)).wait()
        sums = sums + z4[k]
    hb_out[...] = sums[16 : 16 + experts]
    mine = pltpu.roll(sums, lax.rem(width - own * f, width), 1)[:, :own]
    for i in range(5):
        vec_out[i][...] = mine[i : i + 1]
    router_out[...] = mine[5 : 5 + experts]
    ob_out[...] = mine[5 + experts : 5 + 2 * experts]
    for copy in outs[-4:]:
        copy.wait()
    for op in [red_e(e) for e in range(experts)] + [red_a, gat_par] + row_dy + row_h + red_out + red_low:
        op.drain()


def vmem(shape, dtype=BF):
    return pltpu.VMEM(shape, dtype)


def spec(space):
    return pl.BlockSpec(memory_space=space)


V = pltpu.VMEM
H = pltpu.HBM


def pair_sems(units, half):
    return [DMA((units, half)) for _ in range(4)]


def row_sems(units):
    return [DMA((units,)), DMA((units,)), DMA((units, 2)), DMA((units, 2))]


def per_device(
    patch_embeddings,
    upstream_gradient,
    picture_valid_count,
    assigned_specialists,
    filling_sequence_place,
    leading_scale_factor,
    leading_offset_vector,
    query_value_matrix,
    mixing_projection_matrix,
    mixing_offset_vector,
    central_scale_factor,
    central_offset_vector,
    gating_projection,
    specialist_widen_matrix,
    specialist_inner_offset,
    specialist_contract_matrix,
    specialist_final_offset,
):
    fsdp = lax.axis_size("fsdp")
    half = fsdp // 2
    tp = lax.axis_size("tp")
    own_rows, width = patch_embeddings.shape[1:]
    rows = -(-own_rows // 16) * 16
    images = tp
    full = images * rows
    own = leading_scale_factor.shape[0]
    hw = query_value_matrix.shape[2]
    heads = hw // HEAD_DIM
    experts, _, ff = specialist_widen_matrix.shape
    slots = 2 * own_rows * tp // experts
    f_index = lax.axis_index("fsdp")

    row = lambda v: v.reshape(1, own)
    vectors = [
        row(leading_scale_factor),
        row(leading_offset_vector),
        row(mixing_offset_vector),
        row(central_scale_factor),
        row(central_offset_vector),
        gating_projection.T,
        specialist_final_offset,
    ]
    w1 = specialist_widen_matrix
    w2 = specialist_contract_matrix.transpose(0, 2, 1)
    sds = jax.ShapeDtypeStruct
    wide = 2 * width + 256
    outs = pl.pallas_call(
        functools.partial(block_kernel, fsdp, experts),
        out_shape=[
            sds((2, own_rows, width), F32),
            sds((2, own_rows, width), F32),
            sds((3, own, hw), F32),
            sds((own, hw), F32),
            sds((experts, own, ff), F32),
            sds((experts, own, ff), F32),
        ]
        + [sds((1, own), F32)] * 5
        + [
            sds((experts, own), F32),
            sds((experts, own), F32),
            sds((experts, ff), F32),
            sds((experts, half, 2, own, ff), BF),
        ],
        in_specs=[spec(pltpu.SMEM)] + [spec(V)] * 11 + [spec(H)] * 2 + [spec(V)] * 3,
        out_specs=[spec(V)] * 4 + [spec(H)] * 2 + [spec(V)] * 8 + [spec(H)],
        scratch_shapes=[
            vmem((2 * images, rows, width)),
            vmem((2 * images, rows, width)),
            vmem((2 * images, rows, width)),
            vmem((3, 2 * images, rows, hw)),
            vmem((2 * images, heads * rows, rows)),
            vmem((2 * images, rows, hw)),
            vmem((2, rows, width), F32),
            vmem((fsdp, own, 4 * hw)),
            vmem((16, width), F32),
            vmem((fsdp, 16, 128)),
            vmem((experts, fsdp, 2, own, ff)),
            vmem((2, images, rows, wide)),
            vmem((2, 2, rows, wide)),
            vmem((2, rows, wide)),
            vmem((experts, half, 2, own, ff)),
            vmem((half, own, 4 * hw)),
            vmem((half, own, 4 * hw)),
            vmem((2, slots, full)),
            vmem((2, slots, 128), F32),
            vmem((2, slots, width)),
            vmem((2, slots, width)),
            vmem((2, slots, ff)),
            vmem((2, slots, ff)),
            vmem((2, 8, full), jnp.int32),
            vmem((2, 8, full), F32),
            vmem((2 * images, rows, hw)),
            vmem((8, ff), F32),
            vmem((8, width), F32),
            vmem((8, ff), F32),
            vmem((16, width), F32),
            vmem((16, width), F32),
            vmem((24, width), F32),
            vmem((half, 24, width), F32),
            vmem((24, width), F32),
        ]
        + pair_sems(2 + experts, half)
        + pair_sems(1 + experts, half)
        + row_sems(8)
        + row_sems(8)
        + [DMA((2 * experts + 2,)), DMA((2 + half,)), DMA((2 + half,)), DMA((experts, half))],
        compiler_params=pltpu.CompilerParams(
            collective_id=1, has_side_effects=True, vmem_limit_bytes=VMEM_LIMIT
        ),
        name="block",
    )(
        picture_valid_count,
        patch_embeddings,
        upstream_gradient,
        *vectors,
        query_value_matrix.transpose(1, 0, 2),
        mixing_projection_matrix.T,
        w1,
        w2,
        specialist_inner_offset,
        assigned_specialists.transpose(0, 2, 1),
        filling_sequence_place,
    )
    flat = [v.reshape(own) for v in outs[6:11]]
    return (
        outs[0],
        outs[1],
        flat[0],
        flat[1],
        outs[2].transpose(1, 0, 2),
        outs[3].T,
        flat[2],
        flat[3],
        flat[4],
        outs[11].T,
        outs[4],
        outs[13],
        outs[5].transpose(0, 2, 1),
        outs[12],
    )


def solution(mesh):
    placed = (
        P(None, ("fsdp", "tp"), None),
        P(None, ("fsdp", "tp"), None),
        P(None, "fsdp"),
        P(None, "fsdp", None),
        P(None, "fsdp", None),
        P("fsdp"),
        P("fsdp"),
        P("fsdp", None, "tp"),
        P("tp", "fsdp"),
        P("fsdp"),
        P("fsdp"),
        P("fsdp"),
        P("fsdp", None),
        P(None, "fsdp", "tp"),
        P(None, "tp"),
        P(None, "tp", "fsdp"),
        P(None, "fsdp"),
    )
    return jax.shard_map(
        per_device,
        mesh=mesh,
        in_specs=placed,
        out_specs=(
            P(None, ("fsdp", "tp"), None),
            P(None, ("fsdp", "tp"), None),
            P("fsdp"),
            P("fsdp"),
            P("fsdp", None, "tp"),
            P("tp", "fsdp"),
            P("fsdp"),
            P("fsdp"),
            P("fsdp"),
            P("fsdp", None),
            P(None, "fsdp", "tp"),
            P(None, "tp"),
            P(None, "tp", "fsdp"),
            P(None, "fsdp"),
        ),
        check_vma=False,
    )
```

```python
import functools
import math

import jax
import jax.numpy as jnp
from jax import lax
from jax.experimental import pallas as pl
from jax.experimental.pallas import tpu as pltpu
from jax.sharding import PartitionSpec as P

HEAD_DIM = 64
NORM_EPS = 1e-06
MASK_FILL = -1000000000.0
MESH = pl.DeviceIdType.MESH
BF = jnp.bfloat16
F32 = jnp.float32
DMA = pltpu.SemaphoreType.DMA

VMEM_LIMIT = 63 << 20


def dot_nn(a, b):
    return lax.dot_general(a, b, (((1,), (0,)), ((), ())), preferred_element_type=F32)


def dot_nt(a, b):
    return lax.dot_general(a, b, (((1,), (1,)), ((), ())), preferred_element_type=F32)


def dot_tn(a, b):
    return lax.dot_general(a, b, (((0,), (0,)), ((), ())), preferred_element_type=F32)


def norm_parts(values):
    row_mean = jnp.mean(values, axis=-1, keepdims=True)
    centred = values - row_mean
    row_var = jnp.mean(centred * centred, axis=-1, keepdims=True)
    inv_std = lax.rsqrt(row_var + NORM_EPS)
    return centred * inv_std, inv_std


def norm_back(scaled, normed, inv_std):
    return inv_std * (
        scaled
        - jnp.mean(scaled, axis=-1, keepdims=True)
        - normed * jnp.mean(scaled * normed, axis=-1, keepdims=True)
    )


def gelu_parts(x):
    z = jnp.abs(x) * (1.0 / math.sqrt(2.0))
    t = 1.0 / (1.0 + 0.3275911 * z)
    expo = jnp.exp(-0.5 * x * x)
    poly = t * (
        0.254829592
        + t * (-0.284496736 + t * (1.421413741 + t * (-1.453152027 + t * 1.061405429)))
    )
    tail = 0.5 * poly * expo
    cdf = jnp.where(x >= 0, 1.0 - tail, tail)
    return x * cdf, cdf + x * (expo * (1.0 / math.sqrt(2.0 * math.pi)))


def remote(src, dst, send, recv, dev):
    return pltpu.make_async_remote_copy(
        src_ref=src, dst_ref=dst, send_sem=send, recv_sem=recv, device_id=dev, device_id_type=MESH
    )


def half_of(count):
    return count // 2


class Net:
    def __init__(self, fsdp):
        self.fsdp = fsdp
        self.half = fsdp // 2
        self.f = f = lax.axis_index("fsdp")
        self.t = t = lax.axis_index("tp")
        self.pf = f + 1 - 2 * lax.rem(f, 2)
        self.t2 = lax.rem(t + 2, 4)
        self.s = t + 1 - 2 * lax.rem(t, 2)
        self.s2 = lax.rem(self.s + 2, 4)
        self.partner = (self.pf, t)
        self.across = (f, self.t2)
        self.sibling = (f, self.s)

    def at(self, base, k):
        return lax.rem(base + 2 * k + self.fsdp, self.fsdp)

    def line(self, k):
        return (self.at(self.f, k), self.t)

    def barrier(self):
        sem = pltpu.get_barrier_semaphore()
        peers = [self.partner, self.across, self.sibling]
        peers += [self.line(k) for k in range(1, self.half)]
        for peer in peers:
            pl.semaphore_signal(sem, inc=1, device_id=peer, device_id_type=MESH)
        pl.semaphore_wait(sem, len(peers))


class Gather:
    def __init__(self, net, block, sems, unit):
        self.net, self.block, self.unit = net, block, unit
        self.ps, self.pr, self.ls, self.lr = sems

    def _pair(self, j, k):
        u = self.unit
        return remote(self.block(j), self.block(j), self.ps.at[u, k], self.pr.at[u, k], self.net.partner)

    def _line(self, j, k):
        u = self.unit
        return remote(self.block(j), self.block(j), self.ls.at[u, k], self.lr.at[u, k], self.net.line(k))

    def send(self, steps):
        for k in steps:
            if k == 0:
                self._pair(self.net.f, 0).start()
            else:
                self._line(self.net.f, k).start()

    def forward(self, steps):
        n = self.net
        for k in steps:
            j = n.at(n.f, -k)
            self._line(j, k).wait_recv()
            self._pair(j, k).start()

    def finish(self):
        n = self.net
        for k in range(n.half):
            self._pair(n.at(n.pf, -k), k).wait_recv()

    def drain(self):
        n = self.net
        for k in range(n.half):
            self._pair(n.f, k).wait_send()
        for k in range(1, n.half):
            self._line(n.f, k).wait_send()


class Reduce:
    def __init__(self, net, block, first, second, sems, unit, fetch=None):
        self.net, self.block, self.first, self.second, self.unit = net, block, first, second, unit
        self.ps, self.pr, self.ls, self.lr = sems
        self.fetch = fetch

    def _pair(self, k):
        n, u = self.net, self.unit
        return remote(
            self.block(n.at(n.pf, k)), self.first(k), self.ps.at[u, k], self.pr.at[u, k], n.partner
        )

    def _line(self, k):
        n, u = self.net, self.unit
        return remote(
            self.block(n.at(n.f, k)), self.second(k), self.ls.at[u, k], self.lr.at[u, k], n.line(k)
        )

    def start(self):
        for k in list(range(1, self.net.half)) + [0]:
            self._pair(k).start()

    def middle(self, steps):
        n = self.net
        for k in steps:
            self._pair(k).wait_recv()
            mine = self.block(n.at(n.f, k))
            mine[...] = (mine[...].astype(F32) + self.first(k)[...].astype(F32)).astype(BF)
            self._line(k).start()

    def _load(self, k):
        return pltpu.make_async_copy(self.second(k), self.first(k), self.fetch.at[self.unit, k])

    def collect(self):
        for k in range(1, self.net.half):
            self._line(k).wait_recv()
            self._load(k).start()

    def finish(self):
        n = self.net
        self._pair(0).wait_recv()
        total = self.block(n.f)[...].astype(F32) + self.first(0)[...].astype(F32)
        for k in range(1, n.half):
            if self.fetch is None:
                self._line(k).wait_recv()
                total = total + self.second(k)[...].astype(F32)
            else:
                self._load(k).wait()
                total = total + self.first(k)[...].astype(F32)
        return total

    def drain(self):
        for k in range(self.net.half):
            self._pair(k).wait_send()
        for k in range(1, self.net.half):
            self._line(k).wait_send()


class RowGather:
    def __init__(self, net, block, sems, unit):
        self.net, self.block, self.unit = net, block, unit
        self.ys, self.yr, self.cs, self.cr = sems

    def _y(self, j):
        u = self.unit
        return remote(self.block(j), self.block(j), self.ys.at[u], self.yr.at[u], self.net.across)

    def _c(self, j, k):
        u = self.unit
        return remote(self.block(j), self.block(j), self.cs.at[u, k], self.cr.at[u, k], self.net.sibling)

    def start(self):
        self._y(self.net.t).start()
        self._c(self.net.t, 0).start()

    def forward(self):
        n = self.net
        self._y(n.t2).wait_recv()
        self._c(n.t2, 1).start()

    def finish(self):
        n = self.net
        self._c(n.s, 0).wait_recv()
        self._c(n.s2, 1).wait_recv()

    def drain(self):
        n = self.net
        self._y(n.t).wait_send()
        self._c(n.t, 0).wait_send()
        self._c(n.t2, 1).wait_send()


class RowReduce:
    def __init__(self, net, block, first, second, sems, unit):
        self.net, self.block, self.first, self.second, self.unit = net, block, first, second, unit
        self.ys, self.yr, self.cs, self.cr = sems

    def _c(self, k):
        n, u = self.net, self.unit
        j = n.s2 if k == 0 else n.s
        return remote(self.block(j), self.first(k), self.cs.at[u, k], self.cr.at[u, k], n.sibling)

    def _y(self):
        n, u = self.net, self.unit
        return remote(self.block(n.t2), self.second(), self.ys.at[u], self.yr.at[u], n.across)

    def start(self):
        self._c(0).start()
        self._c(1).start()

    def middle(self, add=None):
        n = self.net
        self._c(0).wait_recv()
        mine = self.block(n.t2)
        if add is None:
            mine[...] = (mine[...].astype(F32) + self.first(0)[...].astype(F32)).astype(BF)
        else:
            add(mine, self.first(0))
        self._y().start()

    def finish(self):
        n = self.net
        self._c(1).wait_recv()
        self._y().wait_recv()
        return (
            self.block(n.t)[...].astype(F32)
            + self.first(1)[...].astype(F32)
            + self.second()[...].astype(F32)
        )

    def drain(self):
        self._c(0).wait_send()
        self._c(1).wait_send()
        self._y().wait_send()


def head_masks(rows, width):
    lane = lax.broadcasted_iota(jnp.int32, (rows, width), 1)
    return [
        (lane >= h * HEAD_DIM) & (lane < (h + 1) * HEAD_DIM) for h in range(width // HEAD_DIM)
    ]


def stack_heads(rows, masks):
    zero = jnp.zeros_like(rows)
    return jnp.concatenate([jnp.where(mask, rows, zero) for mask in masks], axis=0)


def merge_heads(stacked, masks):
    count = masks[0].shape[0]
    total = jnp.where(masks[0], stacked[:count], 0.0)
    for h in range(1, len(masks)):
        total = jnp.where(masks[h], stacked[h * count : (h + 1) * count], total)
    return total


def block_kernel(fsdp, experts, *refs):
    it = iter(refs)
    take = lambda n: [next(it) for _ in range(n)]
    cnt, x_in, dy_in = take(3)
    vectors = take(7)
    qkv_in, mix_in, w1_in, w2_in, b1_in, route_in, prio_in = take(7)
    y_out, gx_out, gq_out, gm_out, g1_out, g2_out = take(6)
    small_out, r2 = take(2)
    rowsb, dyg, rin, qkv, prob, mix, hid, awg, par, parg = take(10)
    wbuf, part, first, second, r1, a1, a2 = take(7)
    hot_s, gts, xs, vs, gas, dps, sid, rp, dmx, hb, ob, b1 = take(12)
    z1, z2, z3, z4, zs = take(5)
    ga = take(4)
    rs = take(4)
    rg = take(4)
    rr = take(4)
    loc, sm_s, sm_r, fetch = take(4)
    net = Net(fsdp)
    f, t = net.f, net.t
    live, width = x_in.shape[1], x_in.shape[2]
    rows = rowsb.shape[1]
    images = rowsb.shape[0] // 2
    full = images * rows
    hw = qkv.shape[3]
    own = width // fsdp
    order = []
    for k in range(1, half_of(fsdp)):
        for step in (k, half_of(fsdp) - k):
            if step not in order:
                order.append(step)
    third = -(-len(order) // 3)
    steps = list(range(1, half_of(fsdp)))
    low_steps, mid_steps, high_steps = steps[:third], steps[third : 2 * third], steps[2 * third :]
    near, far, last = order[:third], order[third : 2 * third], order[2 * third :]
    no_rows = jnp.zeros((rows - live, width), F32)

    def padded(ref, m):
        return jnp.concatenate([ref[m].astype(F32), no_rows], axis=0)

    slots = hot_s.shape[1]
    ff = wbuf.shape[4]
    wide = 2 * width
    scale = 1.0 / math.sqrt(HEAD_DIM)

    gat_par = Gather(net, lambda j: parg.at[j], ga, 0)
    gat_aw = Gather(net, lambda j: awg.at[j], ga, 1)
    gat = lambda e: Gather(net, lambda j: wbuf.at[e, j], ga, 2 + e)
    red_e = lambda e: Reduce(
        net, lambda j: wbuf.at[e, j], lambda k: r1.at[e, k], lambda k: r2.at[e, k], rs, e, fetch
    )
    red_a = Reduce(net, lambda j: awg.at[j], lambda k: a1.at[k], lambda k: a2.at[k], rs, experts)

    def row_gather(buf, m, unit):
        return RowGather(net, lambda j: buf.at[m * images + j], rg, unit)

    def row_reduce(m, lo, hi, unit):
        return RowReduce(
            net,
            lambda j: part.at[m, j, :, lo:hi],
            lambda k: first.at[m, k, :, lo:hi],
            lambda: second.at[m, :, lo:hi],
            rr,
            unit,
        )

    row_x = [row_gather(rowsb, m, m) for m in range(2)]
    row_dy = [row_gather(dyg, m, 2 + m) for m in range(2)]
    row_n2 = [row_gather(rowsb, m, 4 + m) for m in range(2)]
    row_h = [row_gather(rowsb, m, 6 + m) for m in range(2)]
    red_att = [row_reduce(m, 0, width, m) for m in range(2)]
    red_mid = [row_reduce(m, width, wide + 256, 2 + m) for m in range(2)]
    red_out = [row_reduce(m, 0, width, 4 + m) for m in range(2)]
    red_low = [row_reduce(m, width, wide, 6 + m) for m in range(2)]

    copies = []
    for e in range(experts):
        for i, src in enumerate((w1_in, w2_in)):
            copies.append(pltpu.make_async_copy(src.at[e], wbuf.at[e, f, i], loc.at[2 * e + i]))
    for copy in copies:
        copy.start()
    net.barrier()
    for m in range(2):
        rowsb[m * images + t] = padded(x_in, m).astype(BF)
        row_x[m].start()
    zs[...] = jnp.zeros_like(zs)
    at = 0
    for ref in vectors:
        count = ref.shape[0]
        zs[at : at + count, :own] = ref[...].astype(F32)
        at += count
    parg[f] = zs[0:16, :128].astype(BF)
    gat_par.send([0] + order)
    same = lax.broadcasted_iota(jnp.int32, (hw, hw), 0) == lax.broadcasted_iota(jnp.int32, (hw, hw), 1)
    turned = dot_tn(mix_in[...], same.astype(BF)).astype(BF)
    awg[f] = jnp.concatenate([qkv_in[0], qkv_in[1], qkv_in[2], turned], axis=1)
    gat_aw.send([0] + order)
    for m in range(2):
        dyg[m * images + t] = padded(dy_in, m).astype(BF)
    b1[0:experts, :] = b1_in[...].astype(F32)
    gat_par.forward(order)
    row_x[0].forward()
    gat_par.finish()

    place = lax.broadcasted_iota(jnp.int32, (128, width), 0)
    column = lax.broadcasted_iota(jnp.int32, (128, width), 1)
    joined = jnp.zeros((16, width), F32)
    for j in range(fsdp):
        hot = ((column == place + j * own) & (place < own)).astype(BF)
        joined = joined + dot_nn(parg[j], hot)
    par[...] = joined
    gain_one, shift_one = par[0:1, :], par[1:2, :]
    mix_bias, gain_two, shift_two = par[2:3, :], par[3:4, :], par[4:5, :]

    def first_norm(i, carry):
        normed, _ = norm_parts(rowsb[i].astype(F32))
        rin[i] = (normed * gain_one + shift_one).astype(BF)
        return carry

    gat_aw.forward(order)
    for copy in copies:
        copy.wait()
    def send_pair(group):
        for steps in ([0], near, far, last):
            for e in group:
                gat(e).send(steps)

    def forward_pair(group, steps):
        for e in group:
            gat(e).forward(steps)

    send_pair((0, 1))
    row_x[0].finish()
    lax.fori_loop(0, images, first_norm, 0)
    row_x[1].forward()
    for m in range(2):
        row_dy[m].start()
    row_x[1].finish()
    lax.fori_loop(images, 2 * images, first_norm, 0)
    gat_aw.finish()

    def project(m, carry):
        span = pl.ds(m * images, images)
        weights = awg[...].reshape(width, 4 * hw)
        block = rin[span].reshape(full, width)
        for c in range(3):
            made = dot_nn(block, weights[:, c * hw : (c + 1) * hw])
            qkv[c, span] = made.astype(BF).reshape(images, rows, hw)
        return carry

    lax.fori_loop(0, 2, project, 0)
    masks = head_masks(rows, hw)
    key_pos = lax.broadcasted_iota(jnp.int32, (len(masks) * rows, rows), 1)

    def attend(i, carry):
        stacked = stack_heads(qkv[0, i], masks)
        scores = dot_nt(stacked, qkv[1, i]) * scale
        scores = jnp.where(key_pos < cnt[i // images, lax.rem(i, images)], scores, MASK_FILL)
        expo = jnp.exp(scores - jnp.max(scores, axis=-1, keepdims=True))
        probs = (expo / jnp.sum(expo, axis=-1, keepdims=True)).astype(BF)
        prob[i] = probs
        mix[i] = merge_heads(dot_nn(probs, qkv[2, i]), masks).astype(BF)
        return carry

    for op in row_x:
        op.drain()
    out_w = awg[...].reshape(width, 4 * hw)[:, 3 * hw :]
    for m in range(2):
        lax.fori_loop(m * images, (m + 1) * images, attend, 0)
        block = mix[m * images : (m + 1) * images].reshape(full, hw)
        part[m, :, :, :width] = dot_nt(block, out_w).astype(BF).reshape(images, rows, width)
        red_att[m].start()
        if m == 0:
            for op in row_dy:
                op.forward()
            red_att[0].middle()
            forward_pair((0, 1), near)
            send_pair((2, 3))
    red_att[1].middle()

    def second_norm(m, carry):
        hidden = padded(x_in, m) + row_reduce(m, 0, width, m).finish() + mix_bias
        hid[m] = hidden
        normed, _ = norm_parts(hidden)
        rowsb[m * images + t] = (normed * gain_two + shift_two).astype(BF)
        row_gather(rowsb, m, 4 + m).start()
        return carry

    lax.fori_loop(0, 2, second_norm, 0)
    forward_pair((0, 1), far)
    for m in range(2):
        row_n2[m].forward()
        row_dy[m].finish()
        red_att[m].drain()
        part[m] = jnp.zeros_like(part[m])

    hb[...] = jnp.zeros_like(hb)
    ob[...] = jnp.zeros_like(ob)

    def find_slots(m, carry):
        by_image = lambda row, fill: jnp.concatenate(
            sum(
                [
                    [row[:, i * live : (i + 1) * live], jnp.full((1, rows - live), fill, jnp.int32)]
                    for i in range(images)
                ],
                [],
            ),
            axis=1,
        )
        e0, e1 = by_image(route_in[m, 0:1, :], -1), by_image(route_in[m, 1:2, :], -1)
        rank = by_image(prio_in[m], live * images)
        high = rank // 32
        digit = lax.broadcasted_iota(jnp.int32, (16, full), 0)
        digits = jnp.where(digit == 0, high, jnp.where(digit == 1, rank - 32 * high, 0))
        digit = lax.broadcasted_iota(jnp.int32, (16, 128), 0)
        worth = jnp.where(digit == 0, 32, jnp.where(digit == 1, 1, 0))
        column = dot_tn(digits.astype(F32).astype(BF), worth.astype(F32).astype(BF))[:, 0:1]
        lower = (column < rank.astype(F32)).astype(BF)
        kind = lax.broadcasted_iota(jnp.int32, (16, full), 0)
        named = jnp.where(kind < experts, e0, e1) == jnp.where(kind < experts, kind, kind - experts)
        named = jnp.where((kind < 2 * experts) & named, 1.0, 0.0)
        counts = dot_nn(named.astype(BF), lower)
        totals = jnp.sum(named, axis=1, keepdims=True)
        for k in range(2):
            where_slot = jnp.full((1, full), -1.0, F32)
            for e in range(experts):
                c = k * experts + e
                before = counts[c : c + 1, :]
                if k == 1:
                    before = before + totals[e : e + 1, :]
                kept = (named[c : c + 1, :] > 0.5) & (before < slots)
                where_slot = jnp.where(kept, before + e * slots, where_slot)
            sid[m, k : k + 1, :] = where_slot.astype(jnp.int32)
        return carry

    lax.fori_loop(0, 2, find_slots, 0)
    for m in range(2):
        row_n2[m].finish()
        n2m = rowsb[m * images : (m + 1) * images].reshape(full, width)
        logits = dot_nt(par[...].astype(BF), n2m)[5 : 5 + experts, :]
        expo = jnp.exp(logits - jnp.max(logits, axis=0, keepdims=True))
        rp[m, 0:experts, :] = expo / jnp.sum(expo, axis=0, keepdims=True)
        row_n2[m].drain()
    forward_pair((0, 1), last)

    slot_row = lax.broadcasted_iota(jnp.int32, (slots, full), 0)
    lane = lax.broadcasted_iota(jnp.int32, (slots, 128), 1)

    def add_split(mine, other):
        mine[:, :width] = (mine[:, :width].astype(F32) + other[:, :width].astype(F32)).astype(BF)
        pair = [mine[:, width : width + 128].astype(F32), mine[:, width + 128 :].astype(F32)]
        pair += [other[:, width : width + 128].astype(F32), other[:, width + 128 :].astype(F32)]
        value = (pair[0] + pair[2]) + (pair[1] + pair[3])
        high = value.astype(BF)
        mine[:, width : width + 128] = high
        mine[:, width + 128 :] = (value - high.astype(F32)).astype(BF)

    schedule = {
        (0, 1): lambda: forward_pair((2, 3), near),
        (1, 0): lambda: forward_pair((2, 3), far),
        (1, 2): lambda: forward_pair((2,), last),
        (2, 0): lambda: (forward_pair((3,), last), red_e(0).start(), red_e(1).start()),
        (2, 3): lambda: red_e(2).start(),
        (3, 1): lambda: red_e(0).middle(low_steps),
        (3, 2): lambda: (red_mid[0].middle(add_split), red_e(0).middle(mid_steps)),
        (3, 3): lambda: (red_e(3).start(), red_mid[1].middle(add_split)),
    }

    def ticks(e, point):
        for (expert_at, point_at), act in schedule.items():
            if point_at == point:

                @pl.when(e == expert_at)
                def _():
                    act()

    def expert(e, carry):
        def dispatch(m, carry):
            hot = (slot_row + e * slots == sid[m, 0:1, :]) | (slot_row + e * slots == sid[m, 1:2, :])
            hot_s[m] = jnp.where(hot, 1.0, 0.0).astype(BF)
            gate = jnp.sum(jnp.where(hot, rp[m, pl.ds(e, 1), :], 0.0), axis=1, keepdims=True)
            gts[m] = jnp.broadcast_to(gate, (slots, 128))
            n2m = rowsb[pl.ds(m * images, images)].reshape(full, width)
            xs[m] = dot_nn(hot_s[m], n2m).astype(BF)
            dym = dyg[pl.ds(m * images, images)].reshape(full, width)
            vals = dot_nn(hot_s[m], dym)
            ob[pl.ds(e, 1), :] += jnp.sum(gate * vals, axis=0, keepdims=True)
            vs[m] = vals.astype(BF)
            return carry

        lax.fori_loop(0, 2, dispatch, 0)
        ticks(e, 0)
        gat(e).finish()


        def hidden_units(m, carry):
            gate = gts[m][:, 0:1]
            d_gate = jnp.zeros((slots, 1), F32)
            for lo in range(0, ff, 256):
                span = slice(lo, lo + 256)
                pre = dot_nn(xs[m], wbuf[e, :, 0, :, span].reshape(width, 256))
                act, slope = gelu_parts(pre + b1[pl.ds(e, 1), span])
                gas[m, :, span] = (gate * act).astype(BF)
                back = dot_nn(vs[m], wbuf[e, :, 1, :, span].reshape(width, 256))
                d_gate = d_gate + jnp.sum(act * back, axis=1, keepdims=True)
                d_pre = gate * slope * back
                hb[pl.ds(e, 1), span] += jnp.sum(d_pre, axis=0, keepdims=True)
                dps[m, :, span] = d_pre.astype(BF)
            high = d_gate.astype(BF)
            low = (d_gate - high.astype(F32)).astype(BF)
            zero = jnp.zeros((slots, 128), BF)
            extra = [
                jnp.where(lane == e, high, jnp.where(lane == 16 + e, jnp.ones_like(zero), zero)),
                jnp.where(lane == e, low, zero),
            ]
            lower, upper = slice(0, fsdp // 2), slice(fsdp // 2, fsdp)
            part_of = lambda i, cut: wbuf[e, cut, i].reshape(width // 2, ff)
            pieces = [
                lambda: dot_nt(gas[m], part_of(1, lower)).astype(BF),
                lambda: dot_nt(gas[m], part_of(1, upper)).astype(BF),
                lambda: dot_nt(dps[m], part_of(0, lower)).astype(BF),
                lambda: dot_nt(dps[m], part_of(0, upper)).astype(BF),
                lambda: jnp.concatenate(extra, axis=1),
            ]
            lo = 0
            for make in pieces:
                piece = make()
                span = slice(lo, lo + piece.shape[1])
                lo = span.stop
                more = dot_tn(hot_s[m], piece).reshape(images, rows, piece.shape[1])
                part[m, :, :, span] = (part[m, :, :, span].astype(F32) + more).astype(BF)

            @pl.when(e == experts - 1)
            def _():
                row_reduce(m, width, wide + 256, 2 + m).start()

            @pl.when(m == 0)
            def _():
                ticks(e, 1)

            return carry

        lax.fori_loop(0, 2, hidden_units, 0)
        ticks(e, 2)
        gat(e).drain()

        two = 2 * slots
        for n in range(2):
            cut = slice(n * (width // 2), (n + 1) * (width // 2))
            blocks = slice(n * fsdp // 2, (n + 1) * fsdp // 2)
            for i, (left, right) in enumerate(((xs, dps), (vs, gas))):
                made = dot_tn(left[:, :, cut].reshape(two, width // 2), right[...].reshape(two, ff))
                wbuf[e, blocks, i] = made.astype(BF).reshape(fsdp // 2, own, ff)
        ticks(e, 3)
        return carry

    lax.fori_loop(0, experts, expert, 0)

    red_e(0).middle(high_steps)
    red_e(1).middle(low_steps + mid_steps)

    zs[...] = jnp.zeros_like(zs)
    lane = lax.broadcasted_iota(jnp.int32, (rows, 128), 1)
    lane16 = lax.broadcasted_iota(jnp.int32, (rows, 16), 1)
    router_lane = (lane16 >= 5) & (lane16 < 5 + experts)

    def router_back(m, carry):
        hidden = hid[m]
        normed, inv = norm_parts(hidden)
        dy = dyg[m * images + t].astype(F32)
        n2 = rowsb[m * images + t]
        logits = jnp.where(router_lane, dot_nt(n2, par[...].astype(BF)), -1e30)
        expo = jnp.exp(logits - jnp.max(logits, axis=1, keepdims=True))
        probs = expo / jnp.sum(expo, axis=1, keepdims=True)
        got = row_reduce(m, width, wide + 256, 2 + m).finish()
        sums = got[:, width : width + 128] + got[:, width + 128 :]
        pcol, qcol, out = [], [], hidden
        for e in range(experts):
            p_e = jnp.sum(jnp.where(lane16 == 5 + e, probs, 0.0), axis=1, keepdims=True)
            kept = 0.25 * jnp.sum(jnp.where(lane == 16 + e, sums, 0.0), axis=1, keepdims=True)
            q_e = jnp.sum(jnp.where(lane == e, sums, 0.0), axis=1, keepdims=True)
            bias = par[5 + experts + e : 6 + experts + e, :]
            q_e = q_e + kept * jnp.sum(dy * bias, axis=1, keepdims=True)
            out = out + (kept * p_e) * bias
            pcol.append(p_e)
            qcol.append(q_e)
        y_out[m] = out[:live]
        mean_q = pcol[0] * qcol[0]
        for e in range(1, experts):
            mean_q = mean_q + pcol[e] * qcol[e]
        mid = got[:, :width]
        for e in range(experts):
            d_logit = (pcol[e] * (qcol[e] - mean_q)).astype(BF).astype(F32)
            mid = mid + d_logit * par[5 + e : 6 + e, :]
            zs[5 + e : 6 + e, :] += jnp.sum(d_logit * n2.astype(F32), axis=0, keepdims=True)
        d_hidden = dy + norm_back(mid * gain_two, normed, inv)
        hid[m] = d_hidden
        rowsb[m * images + t] = d_hidden.astype(BF)
        row_gather(rowsb, m, 6 + m).start()

        @pl.when(m == 0)
        def _():
            red_e(1).middle(high_steps)

        zs[2:3, :] += jnp.sum(d_hidden, axis=0, keepdims=True)
        zs[3:4, :] += jnp.sum(mid * normed, axis=0, keepdims=True)
        zs[4:5, :] += jnp.sum(mid, axis=0, keepdims=True)
        return carry

    lax.fori_loop(0, 2, router_back, 0)
    zs[5 + experts : 5 + 2 * experts, :] = 0.25 * ob[0:experts, :]
    zs[16 : 16 + experts, :] = hb[0:experts, :]
    for m in range(2):
        row_h[m].forward()
        red_mid[m].drain()

    def attend_back(i, carry):
        stacked_d = stack_heads(dmx[i], masks)
        stacked_q = stack_heads(qkv[0, i], masks)
        probs_low = prob[i]
        probs = probs_low.astype(F32)
        d_prob = dot_nt(stacked_d, qkv[2, i])
        d_score = probs * (d_prob - jnp.sum(probs * d_prob, axis=-1, keepdims=True))
        d_score = d_score.astype(BF)
        qkv[0, i] = (merge_heads(dot_nn(d_score, qkv[1, i]), masks) * scale).astype(BF)
        qkv[1, i] = (dot_tn(d_score, stacked_q) * scale).astype(BF)
        qkv[2, i] = dot_tn(probs_low, stacked_d).astype(BF)
        return carry

    for m in range(2):
        row_h[m].finish()
        span = slice(m * images, (m + 1) * images)
        block = rowsb[span].reshape(full, width)
        weights = awg[...].reshape(width, 4 * hw)
        dmx[span] = dot_nn(block, weights[:, 3 * hw :]).astype(BF).reshape(images, rows, hw)
        lax.fori_loop(m * images, (m + 1) * images, attend_back, 0)
        for n in range(2):
            cut = slice(n * fsdp // 2, (n + 1) * fsdp // 2)
            weights = awg[cut].reshape(width // 2, 4 * hw)
            low = jnp.zeros((full, width // 2), F32)
            for c in range(3):
                low = low + dot_nt(qkv[c, span].reshape(full, hw), weights[:, c * hw : (c + 1) * hw])
            here = slice(n * (width // 2), (n + 1) * (width // 2))
            zs[1:2, here] += jnp.sum(low, axis=0, keepdims=True)
            normed = rin[span, :, here].astype(F32).reshape(full, width // 2)
            zs[0:1, here] += jnp.sum(low * normed, axis=0, keepdims=True)
            at = width + n * (width // 2)
            part[m, :, :, at : at + width // 2] = low.astype(BF).reshape(images, rows, width // 2)
        red_low[m].start()
        red_low[m].middle()
        red_e(2).middle((low_steps + mid_steps, high_steps)[m])

    gat_aw.drain()

    def att_grads(n, carry):
        cut = pl.ds(pl.multiple_of(n * (width // 2), 128), width // 2)
        flat_in = rin[:, :, cut].reshape(2 * full, width // 2)
        made = [dot_tn(flat_in, qkv[c].reshape(2 * full, hw)) for c in range(3)]
        flat_h = rowsb[:, :, cut].reshape(2 * full, width // 2)
        made.append(dot_tn(flat_h, mix[...].reshape(2 * full, hw)))
        joined = jnp.concatenate(made, axis=1).astype(BF)
        awg[pl.ds(n * (fsdp // 2), fsdp // 2)] = joined.reshape(fsdp // 2, own, 4 * hw)
        return carry

    zs[0:1, :] = (zs[0:1, :] - shift_one * zs[1:2, :]) / gain_one

    hops = [(z1, 16, net.sibling), (z2, 16, net.across), (z3, 24, net.partner)]

    def hop(i):
        buf, count, dev = hops[i]
        return remote(zs.at[0:count], buf, sm_s.at[i], sm_r.at[i], dev)

    def hop_end(i):
        buf, count, dev = hops[i]
        hop(i).wait()
        zs[0:count] = zs[0:count] + buf[...]

    hop(0).start()
    lax.fori_loop(0, 2, att_grads, 0)
    hop_end(0)
    hop(1).start()
    for m in range(2):
        red_out[m].start()

    def first_back(m, carry):
        low = row_reduce(m, width, wide, 6 + m).finish()
        normed, inv = norm_parts(padded(x_in, m))
        gx_out[m] = (hid[m] + norm_back(low * gain_one, normed, inv))[:live]
        return carry

    lax.fori_loop(0, 2, first_back, 0)
    hop_end(1)
    hop(2).start()
    red_a.start()
    for m in range(2):
        red_out[m].middle()
    outs = []

    def expert_out(e):
        both = red_e(e).finish()
        for i, dst in enumerate((g1_out, g2_out)):
            if e > 1:
                outs[2 * e - 4 + i].wait()
            stage = hid.at[e % 2, i * own : (i + 1) * own]
            stage[...] = both[i]
            outs.append(pltpu.make_async_copy(stage, dst.at[e], loc.at[2 * e + i]))
            outs[-1].start()

    red_e(0).collect()
    red_e(1).collect()
    expert_out(0)
    expert_out(1)
    red_e(3).middle(steps)
    hop_end(2)
    for k in range(1, net.half):
        remote(zs, z4.at[k], sm_s.at[2 + k], sm_r.at[2 + k], net.line(k)).start()
    for m in range(2):
        y_out[m] += red_out[m].finish()[:live]
    red_e(2).collect()
    expert_out(2)
    red_a.middle(steps)
    red_e(3).collect()
    expert_out(3)
    made = red_a.finish()
    for c in range(3):
        gq_out[c] = made[:, c * hw : (c + 1) * hw]
    gm_out[...] = made[:, 3 * hw :]
    sums = zs[...]
    for k in range(1, net.half):
        remote(zs, z4.at[k], sm_s.at[2 + k], sm_r.at[2 + k], net.line(k)).wait()
        sums = sums + z4[k]
    small_out[...] = sums
    for copy in outs[-4:]:
        copy.wait()
    for op in [red_e(e) for e in range(experts)] + [red_a, gat_par] + row_dy + row_h + red_out + red_low:
        op.drain()


def finish_kernel(own, experts, *refs):
    it = iter(refs)
    take = lambda n: [next(it) for _ in range(n)]
    small, gm = take(2)
    large = take(5)
    vec_out = take(5)
    router_out, ob_out, hb_out, gm_out = take(4)
    large_out = take(5)
    held = take(5)
    (sem,) = take(1)
    loads = [pltpu.make_async_copy(large[i], held[i], sem.at[0, i]) for i in range(5)]
    stores = [pltpu.make_async_copy(held[i], large_out[i], sem.at[1, i]) for i in range(5)]
    for load in loads:
        load.start()
    for load, store in zip(loads, stores):
        load.wait()
        store.start()
    sums = small[...]
    width = sums.shape[1]
    hb_out[...] = sums[16 : 16 + experts]
    mine = pltpu.roll(sums, lax.rem(width - own * lax.axis_index("fsdp"), width), 1)[:, :own]
    for i in range(5):
        vec_out[i][...] = mine[i : i + 1]
    router_out[...] = mine[5 : 5 + experts]
    ob_out[...] = mine[5 + experts : 5 + 2 * experts]
    gm_out[...] = gm[...].T
    for store in stores:
        store.wait()


def vmem(shape, dtype=BF):
    return pltpu.VMEM(shape, dtype)


def spec(space):
    return pl.BlockSpec(memory_space=space)


V = pltpu.VMEM
H = pltpu.HBM


def pair_sems(units, half):
    return [DMA((units, half)) for _ in range(4)]


def row_sems(units):
    return [DMA((units,)), DMA((units,)), DMA((units, 2)), DMA((units, 2))]


def per_device(
    patch_embeddings,
    upstream_gradient,
    picture_valid_count,
    assigned_specialists,
    filling_sequence_place,
    leading_scale_factor,
    leading_offset_vector,
    query_value_matrix,
    mixing_projection_matrix,
    mixing_offset_vector,
    central_scale_factor,
    central_offset_vector,
    gating_projection,
    specialist_widen_matrix,
    specialist_inner_offset,
    specialist_contract_matrix,
    specialist_final_offset,
):
    fsdp = lax.axis_size("fsdp")
    half = fsdp // 2
    tp = lax.axis_size("tp")
    own_rows, width = patch_embeddings.shape[1:]
    rows = -(-own_rows // 16) * 16
    images = tp
    full = images * rows
    own = leading_scale_factor.shape[0]
    hw = query_value_matrix.shape[2]
    heads = hw // HEAD_DIM
    experts, _, ff = specialist_widen_matrix.shape
    slots = 2 * own_rows * tp // experts
    f_index = lax.axis_index("fsdp")

    row = lambda v: v.reshape(1, own)
    vectors = [
        row(leading_scale_factor),
        row(leading_offset_vector),
        row(mixing_offset_vector),
        row(central_scale_factor),
        row(central_offset_vector),
        gating_projection.T,
        specialist_final_offset,
    ]
    w1 = specialist_widen_matrix
    w2 = specialist_contract_matrix.transpose(0, 2, 1)
    sds = jax.ShapeDtypeStruct
    wide = 2 * width + 256
    outs = pl.pallas_call(
        functools.partial(block_kernel, fsdp, experts),
        out_shape=[
            sds((2, own_rows, width), F32),
            sds((2, own_rows, width), F32),
            sds((3, own, hw), F32),
            sds((own, hw), F32),
            sds((experts, own, ff), F32),
            sds((experts, own, ff), F32),
        ]
        + [
            sds((24, width), F32),
            sds((experts, half, 2, own, ff), BF),
        ],
        in_specs=[spec(pltpu.SMEM)] + [spec(V)] * 11 + [spec(H)] * 2 + [spec(V)] * 3,
        out_specs=[spec(V)] * 4 + [spec(H)] * 2 + [spec(V), spec(H)],
        scratch_shapes=[
            vmem((2 * images, rows, width)),
            vmem((2 * images, rows, width)),
            vmem((2 * images, rows, width)),
            vmem((3, 2 * images, rows, hw)),
            vmem((2 * images, heads * rows, rows)),
            vmem((2 * images, rows, hw)),
            vmem((2, rows, width), F32),
            vmem((fsdp, own, 4 * hw)),
            vmem((16, width), F32),
            vmem((fsdp, 16, 128)),
            vmem((experts, fsdp, 2, own, ff)),
            vmem((2, images, rows, wide)),
            vmem((2, 2, rows, wide)),
            vmem((2, rows, wide)),
            vmem((experts, half, 2, own, ff)),
            vmem((half, own, 4 * hw)),
            vmem((half, own, 4 * hw)),
            vmem((2, slots, full)),
            vmem((2, slots, 128), F32),
            vmem((2, slots, width)),
            vmem((2, slots, width)),
            vmem((2, slots, ff)),
            vmem((2, slots, ff)),
            vmem((2, 8, full), jnp.int32),
            vmem((2, 8, full), F32),
            vmem((2 * images, rows, hw)),
            vmem((8, ff), F32),
            vmem((8, width), F32),
            vmem((8, ff), F32),
            vmem((16, width), F32),
            vmem((16, width), F32),
            vmem((24, width), F32),
            vmem((half, 24, width), F32),
            vmem((24, width), F32),
        ]
        + pair_sems(2 + experts, half)
        + pair_sems(1 + experts, half)
        + row_sems(8)
        + row_sems(8)
        + [DMA((2 * experts + 2,)), DMA((2 + half,)), DMA((2 + half,)), DMA((experts, half))],
        compiler_params=pltpu.CompilerParams(
            collective_id=1, has_side_effects=True, vmem_limit_bytes=VMEM_LIMIT
        ),
        name="block",
    )(
        picture_valid_count,
        patch_embeddings,
        upstream_gradient,
        *vectors,
        query_value_matrix.transpose(1, 0, 2),
        mixing_projection_matrix,
        w1,
        w2,
        specialist_inner_offset,
        assigned_specialists.transpose(0, 2, 1),
        filling_sequence_place,
    )
    y_out, gx_out, gq, gm, g1, g2, small = outs[:7]
    large = [y_out, gx_out, gq, g1, g2]
    outs = pl.pallas_call(
        functools.partial(finish_kernel, own, experts),
        out_shape=[sds((1, own), F32)] * 5
        + [
            sds((experts, own), F32),
            sds((experts, own), F32),
            sds((experts, ff), F32),
            sds((hw, own), F32),
        ]
        + [sds(v.shape, F32) for v in large],
        in_specs=[spec(V)] * 2 + [spec(H)] * 5,
        out_specs=[spec(V)] * 9 + [spec(H)] * 5,
        scratch_shapes=[vmem(v.shape, F32) for v in large] + [DMA((2, 5))],
        compiler_params=pltpu.CompilerParams(vmem_limit_bytes=VMEM_LIMIT),
        name="finish",
    )(small, gm, *large)
    flat = [v.reshape(own) for v in outs[:5]]
    router, ob, hb, gm, y_out, gx_out, gq, g1, g2 = outs[5:]
    return (
        y_out,
        gx_out,
        flat[0],
        flat[1],
        gq.transpose(1, 0, 2),
        gm,
        flat[2],
        flat[3],
        flat[4],
        router.T,
        g1,
        hb,
        g2.transpose(0, 2, 1),
        ob,
    )


def solution(mesh):
    placed = (
        P(None, ("fsdp", "tp"), None),
        P(None, ("fsdp", "tp"), None),
        P(None, "fsdp"),
        P(None, "fsdp", None),
        P(None, "fsdp", None),
        P("fsdp"),
        P("fsdp"),
        P("fsdp", None, "tp"),
        P("tp", "fsdp"),
        P("fsdp"),
        P("fsdp"),
        P("fsdp"),
        P("fsdp", None),
        P(None, "fsdp", "tp"),
        P(None, "tp"),
        P(None, "tp", "fsdp"),
        P(None, "fsdp"),
    )
    return jax.shard_map(
        per_device,
        mesh=mesh,
        in_specs=placed,
        out_specs=(
            P(None, ("fsdp", "tp"), None),
            P(None, ("fsdp", "tp"), None),
            P("fsdp"),
            P("fsdp"),
            P("fsdp", None, "tp"),
            P("tp", "fsdp"),
            P("fsdp"),
            P("fsdp"),
            P("fsdp"),
            P("fsdp", None),
            P(None, "fsdp", "tp"),
            P(None, "tp"),
            P(None, "tp", "fsdp"),
            P(None, "fsdp"),
        ),
        check_vma=False,
    )
```

```python
import functools
import math

import jax
import jax.numpy as jnp
from jax import lax
from jax.experimental import pallas as pl
from jax.experimental.pallas import tpu as pltpu
from jax.sharding import PartitionSpec as P

HEAD_DIM = 64
NORM_EPS = 1e-06
MASK_FILL = -1000000000.0
MESH = pl.DeviceIdType.MESH
BF = jnp.bfloat16
F32 = jnp.float32
DMA = pltpu.SemaphoreType.DMA

VMEM_LIMIT = 63 << 20


def dot_nn(a, b):
    return lax.dot_general(a, b, (((1,), (0,)), ((), ())), preferred_element_type=F32)


def dot_nt(a, b):
    return lax.dot_general(a, b, (((1,), (1,)), ((), ())), preferred_element_type=F32)


def dot_tn(a, b):
    return lax.dot_general(a, b, (((0,), (0,)), ((), ())), preferred_element_type=F32)


def norm_parts(values):
    row_mean = jnp.mean(values, axis=-1, keepdims=True)
    centred = values - row_mean
    row_var = jnp.mean(centred * centred, axis=-1, keepdims=True)
    inv_std = lax.rsqrt(row_var + NORM_EPS)
    return centred * inv_std, inv_std


def norm_back(scaled, normed, inv_std):
    return inv_std * (
        scaled
        - jnp.mean(scaled, axis=-1, keepdims=True)
        - normed * jnp.mean(scaled * normed, axis=-1, keepdims=True)
    )


def gelu_parts(x):
    z = jnp.abs(x) * (1.0 / math.sqrt(2.0))
    t = 1.0 / (1.0 + 0.3275911 * z)
    expo = jnp.exp(-0.5 * x * x)
    poly = t * (
        0.254829592
        + t * (-0.284496736 + t * (1.421413741 + t * (-1.453152027 + t * 1.061405429)))
    )
    tail = 0.5 * poly * expo
    cdf = jnp.where(x >= 0, 1.0 - tail, tail)
    return x * cdf, cdf + x * (expo * (1.0 / math.sqrt(2.0 * math.pi)))


def remote(src, dst, send, recv, dev):
    return pltpu.make_async_remote_copy(
        src_ref=src, dst_ref=dst, send_sem=send, recv_sem=recv, device_id=dev, device_id_type=MESH
    )


def half_of(count):
    return count // 2


class Net:
    def __init__(self, fsdp):
        self.fsdp = fsdp
        self.half = fsdp // 2
        self.f = f = lax.axis_index("fsdp")
        self.t = t = lax.axis_index("tp")
        self.pf = f + 1 - 2 * lax.rem(f, 2)
        self.t2 = lax.rem(t + 2, 4)
        self.s = t + 1 - 2 * lax.rem(t, 2)
        self.s2 = lax.rem(self.s + 2, 4)
        self.partner = (self.pf, t)
        self.across = (f, self.t2)
        self.sibling = (f, self.s)

    def at(self, base, k):
        return lax.rem(base + 2 * k + self.fsdp, self.fsdp)

    def line(self, k):
        return (self.at(self.f, k), self.t)

    def arrive(self):
        peers = [self.partner, self.across, self.sibling]
        peers += [self.line(k) for k in range(1, self.half)]
        for peer in peers:
            pl.semaphore_signal(
                pltpu.get_barrier_semaphore(), inc=1, device_id=peer, device_id_type=MESH
            )
        return len(peers)


class Gather:
    def __init__(self, net, block, sems, unit):
        self.net, self.block, self.unit = net, block, unit
        self.ps, self.pr, self.ls, self.lr = sems

    def _pair(self, j, k):
        u = self.unit
        return remote(self.block(j), self.block(j), self.ps.at[u, k], self.pr.at[u, k], self.net.partner)

    def _line(self, j, k):
        u = self.unit
        return remote(self.block(j), self.block(j), self.ls.at[u, k], self.lr.at[u, k], self.net.line(k))

    def send(self, steps):
        for k in steps:
            if k == 0:
                self._pair(self.net.f, 0).start()
            else:
                self._line(self.net.f, k).start()

    def forward(self, steps):
        n = self.net
        for k in steps:
            j = n.at(n.f, -k)
            self._line(j, k).wait_recv()
            self._pair(j, k).start()

    def finish(self):
        n = self.net
        for k in range(n.half):
            self._pair(n.at(n.pf, -k), k).wait_recv()

    def drain(self):
        n = self.net
        for k in range(n.half):
            self._pair(n.f, k).wait_send()
        for k in range(1, n.half):
            self._line(n.f, k).wait_send()


class Reduce:
    def __init__(self, net, block, first, second, sems, unit, fetch=None):
        self.net, self.block, self.first, self.second, self.unit = net, block, first, second, unit
        self.ps, self.pr, self.ls, self.lr = sems
        self.fetch = fetch

    def _pair(self, k):
        n, u = self.net, self.unit
        return remote(
            self.block(n.at(n.pf, k)), self.first(k), self.ps.at[u, k], self.pr.at[u, k], n.partner
        )

    def _line(self, k):
        n, u = self.net, self.unit
        return remote(
            self.block(n.at(n.f, k)), self.second(k), self.ls.at[u, k], self.lr.at[u, k], n.line(k)
        )

    def start(self):
        for k in list(range(1, self.net.half)) + [0]:
            self._pair(k).start()

    def middle(self, steps):
        n = self.net
        for k in steps:
            self._pair(k).wait_recv()
            mine = self.block(n.at(n.f, k))
            mine[...] = (mine[...].astype(F32) + self.first(k)[...].astype(F32)).astype(BF)
            self._line(k).start()

    def _load(self, k):
        return pltpu.make_async_copy(self.second(k), self.first(k), self.fetch.at[self.unit, k])

    def collect(self):
        for k in range(1, self.net.half):
            self._line(k).wait_recv()
            self._load(k).start()

    def finish(self):
        n = self.net
        self._pair(0).wait_recv()
        total = self.block(n.f)[...].astype(F32) + self.first(0)[...].astype(F32)
        for k in range(1, n.half):
            if self.fetch is None:
                self._line(k).wait_recv()
                total = total + self.second(k)[...].astype(F32)
            else:
                self._load(k).wait()
                total = total + self.first(k)[...].astype(F32)
        return total

    def drain(self):
        for k in range(self.net.half):
            self._pair(k).wait_send()
        for k in range(1, self.net.half):
            self._line(k).wait_send()


class RowGather:
    def __init__(self, net, block, sems, unit):
        self.net, self.block, self.unit = net, block, unit
        self.ys, self.yr, self.cs, self.cr = sems

    def _y(self, j):
        u = self.unit
        return remote(self.block(j), self.block(j), self.ys.at[u], self.yr.at[u], self.net.across)

    def _c(self, j, k):
        u = self.unit
        return remote(self.block(j), self.block(j), self.cs.at[u, k], self.cr.at[u, k], self.net.sibling)

    def start(self):
        self._y(self.net.t).start()
        self._c(self.net.t, 0).start()

    def forward(self):
        n = self.net
        self._y(n.t2).wait_recv()
        self._c(n.t2, 1).start()

    def finish(self):
        n = self.net
        self._c(n.s, 0).wait_recv()
        self._c(n.s2, 1).wait_recv()

    def drain(self):
        n = self.net
        self._y(n.t).wait_send()
        self._c(n.t, 0).wait_send()
        self._c(n.t2, 1).wait_send()


class RowReduce:
    def __init__(self, net, block, first, second, sems, unit):
        self.net, self.block, self.first, self.second, self.unit = net, block, first, second, unit
        self.ys, self.yr, self.cs, self.cr = sems

    def _c(self, k):
        n, u = self.net, self.unit
        j = n.s2 if k == 0 else n.s
        return remote(self.block(j), self.first(k), self.cs.at[u, k], self.cr.at[u, k], n.sibling)

    def _y(self):
        n, u = self.net, self.unit
        return remote(self.block(n.t2), self.second(), self.ys.at[u], self.yr.at[u], n.across)

    def start(self):
        self._c(0).start()
        self._c(1).start()

    def middle(self, add=None):
        n = self.net
        self._c(0).wait_recv()
        mine = self.block(n.t2)
        if add is None:
            mine[...] = (mine[...].astype(F32) + self.first(0)[...].astype(F32)).astype(BF)
        else:
            add(mine, self.first(0))
        self._y().start()

    def finish(self):
        n = self.net
        self._c(1).wait_recv()
        self._y().wait_recv()
        return (
            self.block(n.t)[...].astype(F32)
            + self.first(1)[...].astype(F32)
            + self.second()[...].astype(F32)
        )

    def drain(self):
        self._c(0).wait_send()
        self._c(1).wait_send()
        self._y().wait_send()


def head_masks(rows, width):
    lane = lax.broadcasted_iota(jnp.int32, (rows, width), 1)
    return [
        (lane >= h * HEAD_DIM) & (lane < (h + 1) * HEAD_DIM) for h in range(width // HEAD_DIM)
    ]


def stack_heads(rows, masks):
    zero = jnp.zeros_like(rows)
    return jnp.concatenate([jnp.where(mask, rows, zero) for mask in masks], axis=0)


def merge_heads(stacked, masks):
    count = masks[0].shape[0]
    total = jnp.where(masks[0], stacked[:count], 0.0)
    for h in range(1, len(masks)):
        total = jnp.where(masks[h], stacked[h * count : (h + 1) * count], total)
    return total


def block_kernel(fsdp, experts, *refs):
    it = iter(refs)
    take = lambda n: [next(it) for _ in range(n)]
    cnt, x_in, dy_in = take(3)
    vectors = take(7)
    qkv_in, mix_in, w1_in, w2_in, b1_in, route_in, prio_in = take(7)
    y_out, gx_out, gq_out, gm_out, g1_out, g2_out = take(6)
    small_out, r2 = take(2)
    rowsb, dyg, rin, qkv, prob, mix, hid, awg, par, parg = take(10)
    wbuf, part, first, second, r1, a1, a2 = take(7)
    hot_s, gts, xs, vs, gas, dps, sid, rp, dmx, hb, ob, b1 = take(12)
    z1, z2, z3, z4, zs = take(5)
    ga = take(4)
    rs = take(4)
    rg = take(4)
    rr = take(4)
    loc, sm_s, sm_r, fetch = take(4)
    net = Net(fsdp)
    f, t = net.f, net.t
    live, width = x_in.shape[1], x_in.shape[2]
    rows = rowsb.shape[1]
    images = rowsb.shape[0] // 2
    full = images * rows
    hw = qkv.shape[3]
    own = width // fsdp
    order = []
    for k in range(1, half_of(fsdp)):
        for step in (k, half_of(fsdp) - k):
            if step not in order:
                order.append(step)
    third = -(-len(order) // 3)
    steps = list(range(1, half_of(fsdp)))
    low_steps, mid_steps, high_steps = steps[:third], steps[third : 2 * third], steps[2 * third :]
    near, far, last = order[:third], order[third : 2 * third], order[2 * third :]
    no_rows = jnp.zeros((rows - live, width), F32)

    def padded(ref, m):
        return jnp.concatenate([ref[m].astype(F32), no_rows], axis=0)

    slots = hot_s.shape[1]
    ff = wbuf.shape[4]
    wide = 2 * width
    scale = 1.0 / math.sqrt(HEAD_DIM)

    gat_par = Gather(net, lambda j: parg.at[j], ga, 0)
    gat_aw = Gather(net, lambda j: awg.at[j], ga, 1)
    gat = lambda e: Gather(net, lambda j: wbuf.at[e, j], ga, 2 + e)
    red_e = lambda e: Reduce(
        net, lambda j: wbuf.at[e, j], lambda k: r1.at[e, k], lambda k: r2.at[e, k], rs, e, fetch
    )
    red_a = Reduce(net, lambda j: awg.at[j], lambda k: a1.at[k], lambda k: a2.at[k], rs, experts)

    def row_gather(buf, m, unit):
        return RowGather(net, lambda j: buf.at[m * images + j], rg, unit)

    def row_reduce(m, lo, hi, unit):
        return RowReduce(
            net,
            lambda j: part.at[m, j, :, lo:hi],
            lambda k: first.at[m, k, :, lo:hi],
            lambda: second.at[m, :, lo:hi],
            rr,
            unit,
        )

    row_x = [row_gather(rowsb, m, m) for m in range(2)]
    row_dy = [row_gather(dyg, m, 2 + m) for m in range(2)]
    row_n2 = [row_gather(rowsb, m, 4 + m) for m in range(2)]
    row_h = [row_gather(rowsb, m, 6 + m) for m in range(2)]
    red_att = [row_reduce(m, 0, width, m) for m in range(2)]
    red_mid = [row_reduce(m, width, wide + 256, 2 + m) for m in range(2)]
    red_out = [row_reduce(m, 0, width, 4 + m) for m in range(2)]
    red_low = [row_reduce(m, width, wide, 6 + m) for m in range(2)]

    arrived = net.arrive()
    copies = []
    for e in range(experts):
        for i, src in enumerate((w1_in, w2_in)):
            copies.append(pltpu.make_async_copy(src.at[e], wbuf.at[e, f, i], loc.at[2 * e + i]))
    for copy in copies:
        copy.start()
    zs[...] = jnp.zeros_like(zs)
    at = 0
    for ref in vectors:
        count = ref.shape[0]
        zs[at : at + count, :own] = ref[...].astype(F32)
        at += count
    parg[f] = zs[0:16, :128].astype(BF)
    same = lax.broadcasted_iota(jnp.int32, (hw, hw), 0) == lax.broadcasted_iota(jnp.int32, (hw, hw), 1)
    turned = dot_tn(mix_in[...], same.astype(BF)).astype(BF)
    awg[f] = jnp.concatenate([qkv_in[0], qkv_in[1], qkv_in[2], turned], axis=1)
    for m in range(2):
        rowsb[m * images + t] = padded(x_in, m).astype(BF)
    pl.semaphore_wait(pltpu.get_barrier_semaphore(), arrived)
    gat_par.send([0] + order)
    row_x[0].start()
    gat_aw.send([0] + order)
    row_x[1].start()
    for m in range(2):
        dyg[m * images + t] = padded(dy_in, m).astype(BF)
    b1[0:experts, :] = b1_in[...].astype(F32)
    gat_par.forward(order)
    row_x[0].forward()
    gat_par.finish()

    place = lax.broadcasted_iota(jnp.int32, (128, width), 0)
    column = lax.broadcasted_iota(jnp.int32, (128, width), 1)
    joined = jnp.zeros((16, width), F32)
    for j in range(fsdp):
        hot = ((column == place + j * own) & (place < own)).astype(BF)
        joined = joined + dot_nn(parg[j], hot)
    par[...] = joined
    gain_one, shift_one = par[0:1, :], par[1:2, :]
    mix_bias, gain_two, shift_two = par[2:3, :], par[3:4, :], par[4:5, :]

    def first_norm(i, carry):
        normed, _ = norm_parts(rowsb[i].astype(F32))
        rin[i] = (normed * gain_one + shift_one).astype(BF)
        return carry

    gat_aw.forward(order)
    for copy in copies:
        copy.wait()
    def send_pair(group):
        for steps in ([0], near, far, last):
            for e in group:
                gat(e).send(steps)

    def forward_pair(group, steps):
        for e in group:
            gat(e).forward(steps)

    send_pair((0, 1))
    row_x[0].finish()
    lax.fori_loop(0, images, first_norm, 0)
    row_x[1].forward()
    for m in range(2):
        row_dy[m].start()
    row_x[1].finish()
    lax.fori_loop(images, 2 * images, first_norm, 0)
    gat_aw.finish()

    def project(m, carry):
        span = pl.ds(m * images, images)
        weights = awg[...].reshape(width, 4 * hw)
        block = rin[span].reshape(full, width)
        for c in range(3):
            made = dot_nn(block, weights[:, c * hw : (c + 1) * hw])
            qkv[c, span] = made.astype(BF).reshape(images, rows, hw)
        return carry

    lax.fori_loop(0, 2, project, 0)
    masks = head_masks(rows, hw)
    key_pos = lax.broadcasted_iota(jnp.int32, (len(masks) * rows, rows), 1)

    def attend(i, carry):
        stacked = stack_heads(qkv[0, i], masks)
        scores = dot_nt(stacked, qkv[1, i]) * scale
        scores = jnp.where(key_pos < cnt[i // images, lax.rem(i, images)], scores, MASK_FILL)
        expo = jnp.exp(scores - jnp.max(scores, axis=-1, keepdims=True))
        probs = (expo / jnp.sum(expo, axis=-1, keepdims=True)).astype(BF)
        prob[i] = probs
        mix[i] = merge_heads(dot_nn(probs, qkv[2, i]), masks).astype(BF)
        return carry

    for op in row_x:
        op.drain()
    out_w = awg[...].reshape(width, 4 * hw)[:, 3 * hw :]
    for m in range(2):
        lax.fori_loop(m * images, (m + 1) * images, attend, 0)
        block = mix[m * images : (m + 1) * images].reshape(full, hw)
        part[m, :, :, :width] = dot_nt(block, out_w).astype(BF).reshape(images, rows, width)
        red_att[m].start()
        if m == 0:
            for op in row_dy:
                op.forward()
            red_att[0].middle()
            forward_pair((0, 1), near)
            send_pair((2, 3))
    red_att[1].middle()

    def second_norm(m, carry):
        hidden = padded(x_in, m) + row_reduce(m, 0, width, m).finish() + mix_bias
        hid[m] = hidden
        normed, _ = norm_parts(hidden)
        rowsb[m * images + t] = (normed * gain_two + shift_two).astype(BF)
        row_gather(rowsb, m, 4 + m).start()
        return carry

    lax.fori_loop(0, 2, second_norm, 0)
    forward_pair((0, 1), far)
    for m in range(2):
        row_n2[m].forward()
        row_dy[m].finish()
        red_att[m].drain()
        part[m] = jnp.zeros_like(part[m])

    hb[...] = jnp.zeros_like(hb)
    ob[...] = jnp.zeros_like(ob)

    def find_slots(m, carry):
        by_image = lambda row, fill: jnp.concatenate(
            sum(
                [
                    [row[:, i * live : (i + 1) * live], jnp.full((1, rows - live), fill, jnp.int32)]
                    for i in range(images)
                ],
                [],
            ),
            axis=1,
        )
        e0, e1 = by_image(route_in[m, 0:1, :], -1), by_image(route_in[m, 1:2, :], -1)
        rank = by_image(prio_in[m], live * images)
        high = rank // 32
        digit = lax.broadcasted_iota(jnp.int32, (16, full), 0)
        digits = jnp.where(digit == 0, high, jnp.where(digit == 1, rank - 32 * high, 0))
        digit = lax.broadcasted_iota(jnp.int32, (16, 128), 0)
        worth = jnp.where(digit == 0, 32, jnp.where(digit == 1, 1, 0))
        column = dot_tn(digits.astype(F32).astype(BF), worth.astype(F32).astype(BF))[:, 0:1]
        lower = (column < rank.astype(F32)).astype(BF)
        kind = lax.broadcasted_iota(jnp.int32, (16, full), 0)
        named = jnp.where(kind < experts, e0, e1) == jnp.where(kind < experts, kind, kind - experts)
        named = jnp.where((kind < 2 * experts) & named, 1.0, 0.0)
        counts = dot_nn(named.astype(BF), lower)
        totals = jnp.sum(named, axis=1, keepdims=True)
        for k in range(2):
            where_slot = jnp.full((1, full), -1.0, F32)
            for e in range(experts):
                c = k * experts + e
                before = counts[c : c + 1, :]
                if k == 1:
                    before = before + totals[e : e + 1, :]
                kept = (named[c : c + 1, :] > 0.5) & (before < slots)
                where_slot = jnp.where(kept, before + e * slots, where_slot)
            sid[m, k : k + 1, :] = where_slot.astype(jnp.int32)
        return carry

    lax.fori_loop(0, 2, find_slots, 0)
    for m in range(2):
        row_n2[m].finish()
        n2m = rowsb[m * images : (m + 1) * images].reshape(full, width)
        logits = dot_nt(par[...].astype(BF), n2m)[5 : 5 + experts, :]
        expo = jnp.exp(logits - jnp.max(logits, axis=0, keepdims=True))
        rp[m, 0:experts, :] = expo / jnp.sum(expo, axis=0, keepdims=True)
        row_n2[m].drain()
    forward_pair((0, 1), last)

    slot_row = lax.broadcasted_iota(jnp.int32, (slots, full), 0)
    lane = lax.broadcasted_iota(jnp.int32, (slots, 128), 1)

    def add_split(mine, other):
        mine[:, :width] = (mine[:, :width].astype(F32) + other[:, :width].astype(F32)).astype(BF)
        pair = [mine[:, width : width + 128].astype(F32), mine[:, width + 128 :].astype(F32)]
        pair += [other[:, width : width + 128].astype(F32), other[:, width + 128 :].astype(F32)]
        value = (pair[0] + pair[2]) + (pair[1] + pair[3])
        high = value.astype(BF)
        mine[:, width : width + 128] = high
        mine[:, width + 128 :] = (value - high.astype(F32)).astype(BF)

    schedule = {
        (0, 1): lambda: forward_pair((2, 3), near),
        (1, 0): lambda: forward_pair((2, 3), far),
        (1, 2): lambda: forward_pair((2,), last),
        (2, 0): lambda: (forward_pair((3,), last), red_e(0).start(), red_e(1).start()),
        (2, 3): lambda: red_e(2).start(),
        (3, 1): lambda: red_e(0).middle(low_steps),
        (3, 2): lambda: (red_mid[0].middle(add_split), red_e(0).middle(mid_steps)),
        (3, 3): lambda: (red_e(3).start(), red_mid[1].middle(add_split)),
    }

    def ticks(e, point):
        for (expert_at, point_at), act in schedule.items():
            if point_at == point:

                @pl.when(e == expert_at)
                def _():
                    act()

    def expert(e, carry):
        def dispatch(m, carry):
            hot = (slot_row + e * slots == sid[m, 0:1, :]) | (slot_row + e * slots == sid[m, 1:2, :])
            hot_s[m] = jnp.where(hot, 1.0, 0.0).astype(BF)
            gate = jnp.sum(jnp.where(hot, rp[m, pl.ds(e, 1), :], 0.0), axis=1, keepdims=True)
            gts[m] = jnp.broadcast_to(gate, (slots, 128))
            n2m = rowsb[pl.ds(m * images, images)].reshape(full, width)
            xs[m] = dot_nn(hot_s[m], n2m).astype(BF)
            dym = dyg[pl.ds(m * images, images)].reshape(full, width)
            vals = dot_nn(hot_s[m], dym)
            ob[pl.ds(e, 1), :] += jnp.sum(gate * vals, axis=0, keepdims=True)
            vs[m] = vals.astype(BF)
            return carry

        lax.fori_loop(0, 2, dispatch, 0)
        ticks(e, 0)
        gat(e).finish()


        def hidden_units(m, carry):
            gate = gts[m][:, 0:1]
            d_gate = jnp.zeros((slots, 1), F32)
            for lo in range(0, ff, 256):
                span = slice(lo, lo + 256)
                pre = dot_nn(xs[m], wbuf[e, :, 0, :, span].reshape(width, 256))
                act, slope = gelu_parts(pre + b1[pl.ds(e, 1), span])
                gas[m, :, span] = (gate * act).astype(BF)
                back = dot_nn(vs[m], wbuf[e, :, 1, :, span].reshape(width, 256))
                d_gate = d_gate + jnp.sum(act * back, axis=1, keepdims=True)
                d_pre = gate * slope * back
                hb[pl.ds(e, 1), span] += jnp.sum(d_pre, axis=0, keepdims=True)
                dps[m, :, span] = d_pre.astype(BF)
            high = d_gate.astype(BF)
            low = (d_gate - high.astype(F32)).astype(BF)
            zero = jnp.zeros((slots, 128), BF)
            extra = [
                jnp.where(lane == e, high, jnp.where(lane == 16 + e, jnp.ones_like(zero), zero)),
                jnp.where(lane == e, low, zero),
            ]
            lower, upper = slice(0, fsdp // 2), slice(fsdp // 2, fsdp)
            part_of = lambda i, cut: wbuf[e, cut, i].reshape(width // 2, ff)
            pieces = [
                lambda: dot_nt(gas[m], part_of(1, lower)).astype(BF),
                lambda: dot_nt(gas[m], part_of(1, upper)).astype(BF),
                lambda: dot_nt(dps[m], part_of(0, lower)).astype(BF),
                lambda: dot_nt(dps[m], part_of(0, upper)).astype(BF),
                lambda: jnp.concatenate(extra, axis=1),
            ]
            lo = 0
            for make in pieces:
                piece = make()
                span = slice(lo, lo + piece.shape[1])
                lo = span.stop
                more = dot_tn(hot_s[m], piece).reshape(images, rows, piece.shape[1])
                part[m, :, :, span] = (part[m, :, :, span].astype(F32) + more).astype(BF)

            @pl.when(e == experts - 1)
            def _():
                row_reduce(m, width, wide + 256, 2 + m).start()

            @pl.when(m == 0)
            def _():
                ticks(e, 1)

            return carry

        lax.fori_loop(0, 2, hidden_units, 0)
        ticks(e, 2)
        gat(e).drain()

        two = 2 * slots
        for n in range(2):
            cut = slice(n * (width // 2), (n + 1) * (width // 2))
            blocks = slice(n * fsdp // 2, (n + 1) * fsdp // 2)
            for i, (left, right) in enumerate(((xs, dps), (vs, gas))):
                made = dot_tn(left[:, :, cut].reshape(two, width // 2), right[...].reshape(two, ff))
                wbuf[e, blocks, i] = made.astype(BF).reshape(fsdp // 2, own, ff)
        ticks(e, 3)
        return carry

    lax.fori_loop(0, experts, expert, 0)

    red_e(0).middle(high_steps)
    red_e(1).middle(low_steps + mid_steps)

    zs[...] = jnp.zeros_like(zs)
    lane = lax.broadcasted_iota(jnp.int32, (rows, 128), 1)
    lane16 = lax.broadcasted_iota(jnp.int32, (rows, 16), 1)
    router_lane = (lane16 >= 5) & (lane16 < 5 + experts)

    def router_back(m, carry):
        hidden = hid[m]
        normed, inv = norm_parts(hidden)
        dy = dyg[m * images + t].astype(F32)
        n2 = rowsb[m * images + t]
        logits = jnp.where(router_lane, dot_nt(n2, par[...].astype(BF)), -1e30)
        expo = jnp.exp(logits - jnp.max(logits, axis=1, keepdims=True))
        probs = expo / jnp.sum(expo, axis=1, keepdims=True)
        got = row_reduce(m, width, wide + 256, 2 + m).finish()
        sums = got[:, width : width + 128] + got[:, width + 128 :]
        pcol, qcol, out = [], [], hidden
        for e in range(experts):
            p_e = jnp.sum(jnp.where(lane16 == 5 + e, probs, 0.0), axis=1, keepdims=True)
            kept = 0.25 * jnp.sum(jnp.where(lane == 16 + e, sums, 0.0), axis=1, keepdims=True)
            q_e = jnp.sum(jnp.where(lane == e, sums, 0.0), axis=1, keepdims=True)
            bias = par[5 + experts + e : 6 + experts + e, :]
            q_e = q_e + kept * jnp.sum(dy * bias, axis=1, keepdims=True)
            out = out + (kept * p_e) * bias
            pcol.append(p_e)
            qcol.append(q_e)
        y_out[m] = out[:live]
        mean_q = pcol[0] * qcol[0]
        for e in range(1, experts):
            mean_q = mean_q + pcol[e] * qcol[e]
        mid = got[:, :width]
        for e in range(experts):
            d_logit = (pcol[e] * (qcol[e] - mean_q)).astype(BF).astype(F32)
            mid = mid + d_logit * par[5 + e : 6 + e, :]
            zs[5 + e : 6 + e, :] += jnp.sum(d_logit * n2.astype(F32), axis=0, keepdims=True)
        d_hidden = dy + norm_back(mid * gain_two, normed, inv)
        hid[m] = d_hidden
        rowsb[m * images + t] = d_hidden.astype(BF)
        row_gather(rowsb, m, 6 + m).start()

        @pl.when(m == 0)
        def _():
            red_e(1).middle(high_steps)

        zs[2:3, :] += jnp.sum(d_hidden, axis=0, keepdims=True)
        zs[3:4, :] += jnp.sum(mid * normed, axis=0, keepdims=True)
        zs[4:5, :] += jnp.sum(mid, axis=0, keepdims=True)
        return carry

    lax.fori_loop(0, 2, router_back, 0)
    zs[5 + experts : 5 + 2 * experts, :] = 0.25 * ob[0:experts, :]
    zs[16 : 16 + experts, :] = hb[0:experts, :]
    for m in range(2):
        row_h[m].forward()
        red_mid[m].drain()

    def attend_back(i, carry):
        stacked_d = stack_heads(dmx[i], masks)
        stacked_q = stack_heads(qkv[0, i], masks)
        probs_low = prob[i]
        probs = probs_low.astype(F32)
        d_prob = dot_nt(stacked_d, qkv[2, i])
        d_score = probs * (d_prob - jnp.sum(probs * d_prob, axis=-1, keepdims=True))
        d_score = d_score.astype(BF)
        qkv[0, i] = (merge_heads(dot_nn(d_score, qkv[1, i]), masks) * scale).astype(BF)
        qkv[1, i] = (dot_tn(d_score, stacked_q) * scale).astype(BF)
        qkv[2, i] = dot_tn(probs_low, stacked_d).astype(BF)
        return carry

    for m in range(2):
        row_h[m].finish()
        span = slice(m * images, (m + 1) * images)
        block = rowsb[span].reshape(full, width)
        weights = awg[...].reshape(width, 4 * hw)
        dmx[span] = dot_nn(block, weights[:, 3 * hw :]).astype(BF).reshape(images, rows, hw)
        lax.fori_loop(m * images, (m + 1) * images, attend_back, 0)
        for n in range(2):
            cut = slice(n * fsdp // 2, (n + 1) * fsdp // 2)
            weights = awg[cut].reshape(width // 2, 4 * hw)
            low = jnp.zeros((full, width // 2), F32)
            for c in range(3):
                low = low + dot_nt(qkv[c, span].reshape(full, hw), weights[:, c * hw : (c + 1) * hw])
            here = slice(n * (width // 2), (n + 1) * (width // 2))
            zs[1:2, here] += jnp.sum(low, axis=0, keepdims=True)
            normed = rin[span, :, here].astype(F32).reshape(full, width // 2)
            zs[0:1, here] += jnp.sum(low * normed, axis=0, keepdims=True)
            at = width + n * (width // 2)
            part[m, :, :, at : at + width // 2] = low.astype(BF).reshape(images, rows, width // 2)
        red_low[m].start()
        red_low[m].middle()
        red_e(2).middle((low_steps + mid_steps, high_steps)[m])

    gat_aw.drain()

    def att_grads(n, carry):
        cut = pl.ds(pl.multiple_of(n * (width // 2), 128), width // 2)
        flat_in = rin[:, :, cut].reshape(2 * full, width // 2)
        made = [dot_tn(flat_in, qkv[c].reshape(2 * full, hw)) for c in range(3)]
        flat_h = rowsb[:, :, cut].reshape(2 * full, width // 2)
        made.append(dot_tn(flat_h, mix[...].reshape(2 * full, hw)))
        joined = jnp.concatenate(made, axis=1).astype(BF)
        awg[pl.ds(n * (fsdp // 2), fsdp // 2)] = joined.reshape(fsdp // 2, own, 4 * hw)
        return carry

    zs[0:1, :] = (zs[0:1, :] - shift_one * zs[1:2, :]) / gain_one

    hops = [(z1, 16, net.sibling), (z2, 16, net.across), (z3, 24, net.partner)]

    def hop(i):
        buf, count, dev = hops[i]
        return remote(zs.at[0:count], buf, sm_s.at[i], sm_r.at[i], dev)

    def hop_end(i):
        buf, count, dev = hops[i]
        hop(i).wait()
        zs[0:count] = zs[0:count] + buf[...]

    hop(0).start()
    lax.fori_loop(0, 2, att_grads, 0)
    hop_end(0)
    hop(1).start()
    for m in range(2):
        red_out[m].start()

    def first_back(m, carry):
        low = row_reduce(m, width, wide, 6 + m).finish()
        normed, inv = norm_parts(padded(x_in, m))
        gx_out[m] = (hid[m] + norm_back(low * gain_one, normed, inv))[:live]
        return carry

    lax.fori_loop(0, 2, first_back, 0)
    hop_end(1)
    hop(2).start()
    red_a.start()
    for m in range(2):
        red_out[m].middle()
    outs = []

    def expert_out(e):
        both = red_e(e).finish()
        for i, dst in enumerate((g1_out, g2_out)):
            if e > 1:
                outs[2 * e - 4 + i].wait()
            stage = hid.at[e % 2, i * own : (i + 1) * own]
            stage[...] = both[i]
            outs.append(pltpu.make_async_copy(stage, dst.at[e], loc.at[2 * e + i]))
            outs[-1].start()

    red_e(0).collect()
    red_e(1).collect()
    expert_out(0)
    expert_out(1)
    red_e(3).middle(steps)
    hop_end(2)
    for k in range(1, net.half):
        remote(zs, z4.at[k], sm_s.at[2 + k], sm_r.at[2 + k], net.line(k)).start()
    for m in range(2):
        y_out[m] += red_out[m].finish()[:live]
    red_e(2).collect()
    expert_out(2)
    red_a.middle(steps)
    red_e(3).collect()
    expert_out(3)
    made = red_a.finish()
    for c in range(3):
        gq_out[c] = made[:, c * hw : (c + 1) * hw]
    gm_out[...] = made[:, 3 * hw :]
    sums = zs[...]
    for k in range(1, net.half):
        remote(zs, z4.at[k], sm_s.at[2 + k], sm_r.at[2 + k], net.line(k)).wait()
        sums = sums + z4[k]
    small_out[...] = sums
    for copy in outs[-4:]:
        copy.wait()
    for op in [red_e(e) for e in range(experts)] + [red_a, gat_par] + row_dy + row_h + red_out + red_low:
        op.drain()


def finish_kernel(own, experts, *refs):
    it = iter(refs)
    take = lambda n: [next(it) for _ in range(n)]
    small, gm = take(2)
    large = take(5)
    vec_out = take(5)
    router_out, ob_out, hb_out, gm_out = take(4)
    large_out = take(5)
    held = take(5)
    (sem,) = take(1)
    loads = [pltpu.make_async_copy(large[i], held[i], sem.at[0, i]) for i in range(5)]
    stores = [pltpu.make_async_copy(held[i], large_out[i], sem.at[1, i]) for i in range(5)]
    for load in loads:
        load.start()
    for load, store in zip(loads, stores):
        load.wait()
        store.start()
    sums = small[...]
    width = sums.shape[1]
    hb_out[...] = sums[16 : 16 + experts]
    mine = pltpu.roll(sums, lax.rem(width - own * lax.axis_index("fsdp"), width), 1)[:, :own]
    for i in range(5):
        vec_out[i][...] = mine[i : i + 1]
    router_out[...] = mine[5 : 5 + experts]
    ob_out[...] = mine[5 + experts : 5 + 2 * experts]
    gm_out[...] = gm[...].T
    for store in stores:
        store.wait()


def vmem(shape, dtype=BF):
    return pltpu.VMEM(shape, dtype)


def spec(space):
    return pl.BlockSpec(memory_space=space)


V = pltpu.VMEM
H = pltpu.HBM


def pair_sems(units, half):
    return [DMA((units, half)) for _ in range(4)]


def row_sems(units):
    return [DMA((units,)), DMA((units,)), DMA((units, 2)), DMA((units, 2))]


def per_device(
    patch_embeddings,
    upstream_gradient,
    picture_valid_count,
    assigned_specialists,
    filling_sequence_place,
    leading_scale_factor,
    leading_offset_vector,
    query_value_matrix,
    mixing_projection_matrix,
    mixing_offset_vector,
    central_scale_factor,
    central_offset_vector,
    gating_projection,
    specialist_widen_matrix,
    specialist_inner_offset,
    specialist_contract_matrix,
    specialist_final_offset,
):
    fsdp = lax.axis_size("fsdp")
    half = fsdp // 2
    tp = lax.axis_size("tp")
    own_rows, width = patch_embeddings.shape[1:]
    rows = -(-own_rows // 16) * 16
    images = tp
    full = images * rows
    own = leading_scale_factor.shape[0]
    hw = query_value_matrix.shape[2]
    heads = hw // HEAD_DIM
    experts, _, ff = specialist_widen_matrix.shape
    slots = 2 * own_rows * tp // experts
    f_index = lax.axis_index("fsdp")

    row = lambda v: v.reshape(1, own)
    vectors = [
        row(leading_scale_factor),
        row(leading_offset_vector),
        row(mixing_offset_vector),
        row(central_scale_factor),
        row(central_offset_vector),
        gating_projection.T,
        specialist_final_offset,
    ]
    w1 = specialist_widen_matrix
    w2 = specialist_contract_matrix.transpose(0, 2, 1)
    sds = jax.ShapeDtypeStruct
    wide = 2 * width + 256
    outs = pl.pallas_call(
        functools.partial(block_kernel, fsdp, experts),
        out_shape=[
            sds((2, own_rows, width), F32),
            sds((2, own_rows, width), F32),
            sds((3, own, hw), F32),
            sds((own, hw), F32),
            sds((experts, own, ff), F32),
            sds((experts, own, ff), F32),
        ]
        + [
            sds((24, width), F32),
            sds((experts, half, 2, own, ff), BF),
        ],
        in_specs=[spec(pltpu.SMEM)] + [spec(V)] * 11 + [spec(H)] * 2 + [spec(V)] * 3,
        out_specs=[spec(V)] * 4 + [spec(H)] * 2 + [spec(V), spec(H)],
        scratch_shapes=[
            vmem((2 * images, rows, width)),
            vmem((2 * images, rows, width)),
            vmem((2 * images, rows, width)),
            vmem((3, 2 * images, rows, hw)),
            vmem((2 * images, heads * rows, rows)),
            vmem((2 * images, rows, hw)),
            vmem((2, rows, width), F32),
            vmem((fsdp, own, 4 * hw)),
            vmem((16, width), F32),
            vmem((fsdp, 16, 128)),
            vmem((experts, fsdp, 2, own, ff)),
            vmem((2, images, rows, wide)),
            vmem((2, 2, rows, wide)),
            vmem((2, rows, wide)),
            vmem((experts, half, 2, own, ff)),
            vmem((half, own, 4 * hw)),
            vmem((half, own, 4 * hw)),
            vmem((2, slots, full)),
            vmem((2, slots, 128), F32),
            vmem((2, slots, width)),
            vmem((2, slots, width)),
            vmem((2, slots, ff)),
            vmem((2, slots, ff)),
            vmem((2, 8, full), jnp.int32),
            vmem((2, 8, full), F32),
            vmem((2 * images, rows, hw)),
            vmem((8, ff), F32),
            vmem((8, width), F32),
            vmem((8, ff), F32),
            vmem((16, width), F32),
            vmem((16, width), F32),
            vmem((24, width), F32),
            vmem((half, 24, width), F32),
            vmem((24, width), F32),
        ]
        + pair_sems(2 + experts, half)
        + pair_sems(1 + experts, half)
        + row_sems(8)
        + row_sems(8)
        + [DMA((2 * experts + 2,)), DMA((2 + half,)), DMA((2 + half,)), DMA((experts, half))],
        compiler_params=pltpu.CompilerParams(
            collective_id=1, has_side_effects=True, vmem_limit_bytes=VMEM_LIMIT
        ),
        name="block",
    )(
        picture_valid_count,
        patch_embeddings,
        upstream_gradient,
        *vectors,
        query_value_matrix.transpose(1, 0, 2),
        mixing_projection_matrix,
        w1,
        w2,
        specialist_inner_offset,
        assigned_specialists.transpose(0, 2, 1),
        filling_sequence_place,
    )
    y_out, gx_out, gq, gm, g1, g2, small = outs[:7]
    large = [y_out, gx_out, gq, g1, g2]
    outs = pl.pallas_call(
        functools.partial(finish_kernel, own, experts),
        out_shape=[sds((1, own), F32)] * 5
        + [
            sds((experts, own), F32),
            sds((experts, own), F32),
            sds((experts, ff), F32),
            sds((hw, own), F32),
        ]
        + [sds(v.shape, F32) for v in large],
        in_specs=[spec(V)] * 2 + [spec(H)] * 5,
        out_specs=[spec(V)] * 9 + [spec(H)] * 5,
        scratch_shapes=[vmem(v.shape, F32) for v in large] + [DMA((2, 5))],
        compiler_params=pltpu.CompilerParams(vmem_limit_bytes=VMEM_LIMIT),
        name="finish",
    )(small, gm, *large)
    flat = [v.reshape(own) for v in outs[:5]]
    router, ob, hb, gm, y_out, gx_out, gq, g1, g2 = outs[5:]
    return (
        y_out,
        gx_out,
        flat[0],
        flat[1],
        gq.transpose(1, 0, 2),
        gm,
        flat[2],
        flat[3],
        flat[4],
        router.T,
        g1,
        hb,
        g2.transpose(0, 2, 1),
        ob,
    )


def solution(mesh):
    placed = (
        P(None, ("fsdp", "tp"), None),
        P(None, ("fsdp", "tp"), None),
        P(None, "fsdp"),
        P(None, "fsdp", None),
        P(None, "fsdp", None),
        P("fsdp"),
        P("fsdp"),
        P("fsdp", None, "tp"),
        P("tp", "fsdp"),
        P("fsdp"),
        P("fsdp"),
        P("fsdp"),
        P("fsdp", None),
        P(None, "fsdp", "tp"),
        P(None, "tp"),
        P(None, "tp", "fsdp"),
        P(None, "fsdp"),
    )
    return jax.shard_map(
        per_device,
        mesh=mesh,
        in_specs=placed,
        out_specs=(
            P(None, ("fsdp", "tp"), None),
            P(None, ("fsdp", "tp"), None),
            P("fsdp"),
            P("fsdp"),
            P("fsdp", None, "tp"),
            P("tp", "fsdp"),
            P("fsdp"),
            P("fsdp"),
            P("fsdp"),
            P("fsdp", None),
            P(None, "fsdp", "tp"),
            P(None, "tp"),
            P(None, "tp", "fsdp"),
            P(None, "fsdp"),
        ),
        check_vma=False,
    )
```

```python
import functools
import math

import jax
import jax.numpy as jnp
from jax import lax
from jax.experimental import pallas as pl
from jax.experimental.pallas import tpu as pltpu
from jax.sharding import PartitionSpec as P

HEAD_DIM = 64
NORM_EPS = 1e-06
MASK_FILL = -1000000000.0
MESH = pl.DeviceIdType.MESH
BF = jnp.bfloat16
F32 = jnp.float32
DMA = pltpu.SemaphoreType.DMA

VMEM_LIMIT = 63 << 20


def dot_nn(a, b):
    return lax.dot_general(a, b, (((1,), (0,)), ((), ())), preferred_element_type=F32)


def dot_nt(a, b):
    return lax.dot_general(a, b, (((1,), (1,)), ((), ())), preferred_element_type=F32)


def dot_tn(a, b):
    return lax.dot_general(a, b, (((0,), (0,)), ((), ())), preferred_element_type=F32)


def norm_parts(values):
    row_mean = jnp.mean(values, axis=-1, keepdims=True)
    centred = values - row_mean
    row_var = jnp.mean(centred * centred, axis=-1, keepdims=True)
    inv_std = lax.rsqrt(row_var + NORM_EPS)
    return centred * inv_std, inv_std


def norm_back(scaled, normed, inv_std):
    return inv_std * (
        scaled
        - jnp.mean(scaled, axis=-1, keepdims=True)
        - normed * jnp.mean(scaled * normed, axis=-1, keepdims=True)
    )


def gelu_parts(x):
    z = jnp.abs(x) * (1.0 / math.sqrt(2.0))
    t = 1.0 / (1.0 + 0.3275911 * z)
    expo = jnp.exp(-0.5 * x * x)
    poly = t * (
        0.254829592
        + t * (-0.284496736 + t * (1.421413741 + t * (-1.453152027 + t * 1.061405429)))
    )
    tail = 0.5 * poly * expo
    cdf = jnp.where(x >= 0, 1.0 - tail, tail)
    return x * cdf, cdf + x * (expo * (1.0 / math.sqrt(2.0 * math.pi)))


def remote(src, dst, send, recv, dev):
    return pltpu.make_async_remote_copy(
        src_ref=src, dst_ref=dst, send_sem=send, recv_sem=recv, device_id=dev, device_id_type=MESH
    )


def half_of(count):
    return count // 2


class Net:
    def __init__(self, fsdp):
        self.fsdp = fsdp
        self.half = fsdp // 2
        self.f = f = lax.axis_index("fsdp")
        self.t = t = lax.axis_index("tp")
        self.pf = f + 1 - 2 * lax.rem(f, 2)
        self.t2 = lax.rem(t + 2, 4)
        self.s = t + 1 - 2 * lax.rem(t, 2)
        self.s2 = lax.rem(self.s + 2, 4)
        self.partner = (self.pf, t)
        self.across = (f, self.t2)
        self.sibling = (f, self.s)

    def at(self, base, k):
        return lax.rem(base + 2 * k + self.fsdp, self.fsdp)

    def line(self, k):
        return (self.at(self.f, k), self.t)

    def arrive(self):
        peers = [self.partner, self.across, self.sibling]
        peers += [self.line(k) for k in range(1, self.half)]
        for peer in peers:
            pl.semaphore_signal(
                pltpu.get_barrier_semaphore(), inc=1, device_id=peer, device_id_type=MESH
            )
        return len(peers)


class Gather:
    def __init__(self, net, block, sems, unit):
        self.net, self.block, self.unit = net, block, unit
        self.ps, self.pr, self.ls, self.lr = sems

    def _pair(self, j, k):
        u = self.unit
        return remote(self.block(j), self.block(j), self.ps.at[u, k], self.pr.at[u, k], self.net.partner)

    def _line(self, j, k):
        u = self.unit
        return remote(self.block(j), self.block(j), self.ls.at[u, k], self.lr.at[u, k], self.net.line(k))

    def send(self, steps):
        for k in steps:
            if k == 0:
                self._pair(self.net.f, 0).start()
            else:
                self._line(self.net.f, k).start()

    def forward(self, steps):
        n = self.net
        for k in steps:
            j = n.at(n.f, -k)
            self._line(j, k).wait_recv()
            self._pair(j, k).start()

    def finish(self):
        n = self.net
        for k in range(n.half):
            self._pair(n.at(n.pf, -k), k).wait_recv()

    def drain(self):
        n = self.net
        for k in range(n.half):
            self._pair(n.f, k).wait_send()
        for k in range(1, n.half):
            self._line(n.f, k).wait_send()


class Reduce:
    def __init__(self, net, block, first, second, sems, unit, fetch=None):
        self.net, self.block, self.first, self.second, self.unit = net, block, first, second, unit
        self.ps, self.pr, self.ls, self.lr = sems
        self.fetch = fetch

    def _pair(self, k):
        n, u = self.net, self.unit
        return remote(
            self.block(n.at(n.pf, k)), self.first(k), self.ps.at[u, k], self.pr.at[u, k], n.partner
        )

    def _line(self, k):
        n, u = self.net, self.unit
        return remote(
            self.block(n.at(n.f, k)), self.second(k), self.ls.at[u, k], self.lr.at[u, k], n.line(k)
        )

    def start(self):
        for k in list(range(1, self.net.half)) + [0]:
            self._pair(k).start()

    def middle(self, steps):
        n = self.net
        for k in steps:
            self._pair(k).wait_recv()
            mine = self.block(n.at(n.f, k))
            mine[...] = (mine[...].astype(F32) + self.first(k)[...].astype(F32)).astype(BF)
            self._line(k).start()

    def _load(self, k):
        return pltpu.make_async_copy(self.second(k), self.first(k), self.fetch.at[self.unit, k])

    def collect(self):
        for k in range(1, self.net.half):
            self._line(k).wait_recv()
            self._load(k).start()

    def finish(self):
        n = self.net
        self._pair(0).wait_recv()
        total = self.block(n.f)[...].astype(F32) + self.first(0)[...].astype(F32)
        for k in range(1, n.half):
            if self.fetch is None:
                self._line(k).wait_recv()
                total = total + self.second(k)[...].astype(F32)
            else:
                self._load(k).wait()
                total = total + self.first(k)[...].astype(F32)
        return total

    def drain(self):
        for k in range(self.net.half):
            self._pair(k).wait_send()
        for k in range(1, self.net.half):
            self._line(k).wait_send()


class RowGather:
    def __init__(self, net, block, sems, unit):
        self.net, self.block, self.unit = net, block, unit
        self.ys, self.yr, self.cs, self.cr = sems

    def _y(self, j):
        u = self.unit
        return remote(self.block(j), self.block(j), self.ys.at[u], self.yr.at[u], self.net.across)

    def _c(self, j, k):
        u = self.unit
        return remote(self.block(j), self.block(j), self.cs.at[u, k], self.cr.at[u, k], self.net.sibling)

    def start(self):
        self._y(self.net.t).start()
        self._c(self.net.t, 0).start()

    def forward(self):
        n = self.net
        self._y(n.t2).wait_recv()
        self._c(n.t2, 1).start()

    def finish(self):
        n = self.net
        self._c(n.s, 0).wait_recv()
        self._c(n.s2, 1).wait_recv()

    def drain(self):
        n = self.net
        self._y(n.t).wait_send()
        self._c(n.t, 0).wait_send()
        self._c(n.t2, 1).wait_send()


class RowReduce:
    def __init__(self, net, block, first, second, sems, unit):
        self.net, self.block, self.first, self.second, self.unit = net, block, first, second, unit
        self.ys, self.yr, self.cs, self.cr = sems

    def _c(self, k):
        n, u = self.net, self.unit
        j = n.s2 if k == 0 else n.s
        return remote(self.block(j), self.first(k), self.cs.at[u, k], self.cr.at[u, k], n.sibling)

    def _y(self):
        n, u = self.net, self.unit
        return remote(self.block(n.t2), self.second(), self.ys.at[u], self.yr.at[u], n.across)

    def start(self):
        self._c(0).start()
        self._c(1).start()

    def middle(self, add=None):
        n = self.net
        self._c(0).wait_recv()
        mine = self.block(n.t2)
        if add is None:
            mine[...] = (mine[...].astype(F32) + self.first(0)[...].astype(F32)).astype(BF)
        else:
            add(mine, self.first(0))
        self._y().start()

    def finish(self):
        n = self.net
        self._c(1).wait_recv()
        self._y().wait_recv()
        return (
            self.block(n.t)[...].astype(F32)
            + self.first(1)[...].astype(F32)
            + self.second()[...].astype(F32)
        )

    def drain(self):
        self._c(0).wait_send()
        self._c(1).wait_send()
        self._y().wait_send()


def head_masks(rows, width):
    lane = lax.broadcasted_iota(jnp.int32, (rows, width), 1)
    return [
        (lane >= h * HEAD_DIM) & (lane < (h + 1) * HEAD_DIM) for h in range(width // HEAD_DIM)
    ]


def stack_heads(rows, masks):
    zero = jnp.zeros_like(rows)
    return jnp.concatenate([jnp.where(mask, rows, zero) for mask in masks], axis=0)


def merge_heads(stacked, masks):
    count = masks[0].shape[0]
    total = jnp.where(masks[0], stacked[:count], 0.0)
    for h in range(1, len(masks)):
        total = jnp.where(masks[h], stacked[h * count : (h + 1) * count], total)
    return total


def block_kernel(fsdp, experts, *refs):
    it = iter(refs)
    take = lambda n: [next(it) for _ in range(n)]
    cnt, x_in, dy_in = take(3)
    vectors = take(7)
    qkv_in, mix_in, w1_in, w2_in, b1_in, route_in, prio_in = take(7)
    y_out, gx_out, gq_out, gm_out, g1_out, g2_out = take(6)
    small_out, r2 = take(2)
    rowsb, dyg, rin, qkv, prob, mix, hid, awg, par, parg = take(10)
    wbuf, part, first, second, r1, a1, a2 = take(7)
    hot_s, gts, xs, vs, gas, dps, sid, rp, dmx, hb, ob, b1, r2_last = take(13)
    z1, z2, z3, z4, zs = take(5)
    ga = take(4)
    rs = take(4)
    rg = take(4)
    rr = take(4)
    loc, sm_s, sm_r, fetch = take(4)
    net = Net(fsdp)
    f, t = net.f, net.t
    live, width = x_in.shape[1], x_in.shape[2]
    rows = rowsb.shape[1]
    images = rowsb.shape[0] // 2
    full = images * rows
    hw = qkv.shape[3]
    own = width // fsdp
    order = []
    for k in range(1, half_of(fsdp)):
        for step in (k, half_of(fsdp) - k):
            if step not in order:
                order.append(step)
    third = -(-len(order) // 3)
    steps = list(range(1, half_of(fsdp)))
    low_steps, mid_steps, high_steps = steps[:third], steps[third : 2 * third], steps[2 * third :]
    near, far, last = order[:third], order[third : 2 * third], order[2 * third :]
    no_rows = jnp.zeros((rows - live, width), F32)

    def padded(ref, m):
        return jnp.concatenate([ref[m].astype(F32), no_rows], axis=0)

    slots = hot_s.shape[1]
    ff = wbuf.shape[4]
    wide = 2 * width
    scale = 1.0 / math.sqrt(HEAD_DIM)

    gat_par = Gather(net, lambda j: parg.at[j], ga, 0)
    gat_aw = Gather(net, lambda j: awg.at[j], ga, 1)
    gat = lambda e: Gather(net, lambda j: wbuf.at[e, j], ga, 2 + e)
    def red_e(e):
        final = e == experts - 1
        second_of = lambda k: r2_last.at[k - 1] if final else r2.at[e, k]
        return Reduce(
            net,
            lambda j: wbuf.at[e, j],
            lambda k: r1.at[e, k],
            second_of,
            rs,
            e,
            None if final else fetch,
        )

    red_a = Reduce(net, lambda j: awg.at[j], lambda k: a1.at[k], lambda k: a2.at[k], rs, experts)

    def row_gather(buf, m, unit):
        return RowGather(net, lambda j: buf.at[m * images + j], rg, unit)

    def row_reduce(m, lo, hi, unit):
        return RowReduce(
            net,
            lambda j: part.at[m, j, :, lo:hi],
            lambda k: first.at[m, k, :, lo:hi],
            lambda: second.at[m, :, lo:hi],
            rr,
            unit,
        )

    row_x = [row_gather(rowsb, m, m) for m in range(2)]
    row_dy = [row_gather(dyg, m, 2 + m) for m in range(2)]
    row_n2 = [row_gather(rowsb, m, 4 + m) for m in range(2)]
    row_h = [row_gather(rowsb, m, 6 + m) for m in range(2)]
    red_att = [row_reduce(m, 0, width, m) for m in range(2)]
    red_mid = [row_reduce(m, width, wide + 256, 2 + m) for m in range(2)]
    red_out = [row_reduce(m, 0, width, 4 + m) for m in range(2)]
    red_low = [row_reduce(m, width, wide, 6 + m) for m in range(2)]

    arrived = net.arrive()
    copies = []
    for e in range(experts):
        for i, src in enumerate((w1_in, w2_in)):
            copies.append(pltpu.make_async_copy(src.at[e], wbuf.at[e, f, i], loc.at[2 * e + i]))
    for copy in copies:
        copy.start()
    zs[...] = jnp.zeros_like(zs)
    at = 0
    for ref in vectors:
        count = ref.shape[0]
        zs[at : at + count, :own] = ref[...].astype(F32)
        at += count
    parg[f] = zs[0:16, :128].astype(BF)
    same = lax.broadcasted_iota(jnp.int32, (hw, hw), 0) == lax.broadcasted_iota(jnp.int32, (hw, hw), 1)
    turned = dot_tn(mix_in[...], same.astype(BF)).astype(BF)
    awg[f] = jnp.concatenate([qkv_in[0], qkv_in[1], qkv_in[2], turned], axis=1)
    for m in range(2):
        rowsb[m * images + t] = padded(x_in, m).astype(BF)
    pl.semaphore_wait(pltpu.get_barrier_semaphore(), arrived)
    gat_par.send([0] + order)
    row_x[0].start()
    gat_aw.send([0] + order)
    row_x[1].start()
    for m in range(2):
        dyg[m * images + t] = padded(dy_in, m).astype(BF)
    b1[0:experts, :] = b1_in[...].astype(F32)
    gat_par.forward(order)
    row_x[0].forward()
    gat_par.finish()

    place = lax.broadcasted_iota(jnp.int32, (128, width), 0)
    column = lax.broadcasted_iota(jnp.int32, (128, width), 1)
    joined = jnp.zeros((16, width), F32)
    for j in range(fsdp):
        hot = ((column == place + j * own) & (place < own)).astype(BF)
        joined = joined + dot_nn(parg[j], hot)
    par[...] = joined
    gain_one, shift_one = par[0:1, :], par[1:2, :]
    mix_bias, gain_two, shift_two = par[2:3, :], par[3:4, :], par[4:5, :]

    def first_norm(i, carry):
        normed, _ = norm_parts(rowsb[i].astype(F32))
        rin[i] = (normed * gain_one + shift_one).astype(BF)
        return carry

    gat_aw.forward(order)
    for copy in copies:
        copy.wait()
    def send_pair(group):
        for steps in ([0], near, far, last):
            for e in group:
                gat(e).send(steps)

    def forward_pair(group, steps):
        for e in group:
            gat(e).forward(steps)

    send_pair((0, 1))
    row_x[0].finish()
    lax.fori_loop(0, images, first_norm, 0)
    row_x[1].forward()
    for m in range(2):
        row_dy[m].start()
    row_x[1].finish()
    lax.fori_loop(images, 2 * images, first_norm, 0)
    gat_aw.finish()

    def project(m, carry):
        span = pl.ds(m * images, images)
        weights = awg[...].reshape(width, 4 * hw)
        block = rin[span].reshape(full, width)
        for c in range(3):
            made = dot_nn(block, weights[:, c * hw : (c + 1) * hw])
            qkv[c, span] = made.astype(BF).reshape(images, rows, hw)
        return carry

    lax.fori_loop(0, 2, project, 0)
    masks = head_masks(rows, hw)
    key_pos = lax.broadcasted_iota(jnp.int32, (len(masks) * rows, rows), 1)

    def attend(i, carry):
        stacked = stack_heads(qkv[0, i], masks)
        scores = dot_nt(stacked, qkv[1, i]) * scale
        scores = jnp.where(key_pos < cnt[i // images, lax.rem(i, images)], scores, MASK_FILL)
        expo = jnp.exp(scores - jnp.max(scores, axis=-1, keepdims=True))
        probs = (expo / jnp.sum(expo, axis=-1, keepdims=True)).astype(BF)
        prob[i] = probs
        mix[i] = merge_heads(dot_nn(probs, qkv[2, i]), masks).astype(BF)
        return carry

    for op in row_x:
        op.drain()
    out_w = awg[...].reshape(width, 4 * hw)[:, 3 * hw :]
    for m in range(2):
        lax.fori_loop(m * images, (m + 1) * images, attend, 0)
        block = mix[m * images : (m + 1) * images].reshape(full, hw)
        part[m, :, :, :width] = dot_nt(block, out_w).astype(BF).reshape(images, rows, width)
        red_att[m].start()
        if m == 0:
            for op in row_dy:
                op.forward()
            red_att[0].middle()
            forward_pair((0, 1), near)
            send_pair((2, 3))
    red_att[1].middle()

    def second_norm(m, carry):
        hidden = padded(x_in, m) + row_reduce(m, 0, width, m).finish() + mix_bias
        hid[m] = hidden
        normed, _ = norm_parts(hidden)
        rowsb[m * images + t] = (normed * gain_two + shift_two).astype(BF)
        row_gather(rowsb, m, 4 + m).start()
        return carry

    lax.fori_loop(0, 2, second_norm, 0)
    forward_pair((0, 1), far)
    for m in range(2):
        row_n2[m].forward()
        row_dy[m].finish()
        red_att[m].drain()
        part[m] = jnp.zeros_like(part[m])

    hb[...] = jnp.zeros_like(hb)
    ob[...] = jnp.zeros_like(ob)

    def find_slots(m, carry):
        by_image = lambda row, fill: jnp.concatenate(
            sum(
                [
                    [row[:, i * live : (i + 1) * live], jnp.full((1, rows - live), fill, jnp.int32)]
                    for i in range(images)
                ],
                [],
            ),
            axis=1,
        )
        e0, e1 = by_image(route_in[m, 0:1, :], -1), by_image(route_in[m, 1:2, :], -1)
        rank = by_image(prio_in[m], live * images)
        high = rank // 32
        digit = lax.broadcasted_iota(jnp.int32, (16, full), 0)
        digits = jnp.where(digit == 0, high, jnp.where(digit == 1, rank - 32 * high, 0))
        digit = lax.broadcasted_iota(jnp.int32, (16, 128), 0)
        worth = jnp.where(digit == 0, 32, jnp.where(digit == 1, 1, 0))
        column = dot_tn(digits.astype(F32).astype(BF), worth.astype(F32).astype(BF))[:, 0:1]
        lower = (column < rank.astype(F32)).astype(BF)
        kind = lax.broadcasted_iota(jnp.int32, (16, full), 0)
        named = jnp.where(kind < experts, e0, e1) == jnp.where(kind < experts, kind, kind - experts)
        named = jnp.where((kind < 2 * experts) & named, 1.0, 0.0)
        counts = dot_nn(named.astype(BF), lower)
        totals = jnp.sum(named, axis=1, keepdims=True)
        for k in range(2):
            where_slot = jnp.full((1, full), -1.0, F32)
            for e in range(experts):
                c = k * experts + e
                before = counts[c : c + 1, :]
                if k == 1:
                    before = before + totals[e : e + 1, :]
                kept = (named[c : c + 1, :] > 0.5) & (before < slots)
                where_slot = jnp.where(kept, before + e * slots, where_slot)
            sid[m, k : k + 1, :] = where_slot.astype(jnp.int32)
        return carry

    lax.fori_loop(0, 2, find_slots, 0)
    for m in range(2):
        row_n2[m].finish()
        n2m = rowsb[m * images : (m + 1) * images].reshape(full, width)
        logits = dot_nt(par[...].astype(BF), n2m)[5 : 5 + experts, :]
        expo = jnp.exp(logits - jnp.max(logits, axis=0, keepdims=True))
        rp[m, 0:experts, :] = expo / jnp.sum(expo, axis=0, keepdims=True)
        row_n2[m].drain()
    forward_pair((0, 1), last)

    slot_row = lax.broadcasted_iota(jnp.int32, (slots, full), 0)
    lane = lax.broadcasted_iota(jnp.int32, (slots, 128), 1)

    def add_split(mine, other):
        mine[:, :width] = (mine[:, :width].astype(F32) + other[:, :width].astype(F32)).astype(BF)
        pair = [mine[:, width : width + 128].astype(F32), mine[:, width + 128 :].astype(F32)]
        pair += [other[:, width : width + 128].astype(F32), other[:, width + 128 :].astype(F32)]
        value = (pair[0] + pair[2]) + (pair[1] + pair[3])
        high = value.astype(BF)
        mine[:, width : width + 128] = high
        mine[:, width + 128 :] = (value - high.astype(F32)).astype(BF)

    schedule = {
        (0, 1): lambda: forward_pair((2, 3), near),
        (1, 0): lambda: forward_pair((2, 3), far),
        (1, 2): lambda: forward_pair((2,), last),
        (2, 0): lambda: (forward_pair((3,), last), red_e(0).start(), red_e(1).start()),
        (2, 3): lambda: red_e(2).start(),
        (3, 1): lambda: red_e(0).middle(low_steps),
        (3, 2): lambda: (red_mid[0].middle(add_split), red_e(0).middle(mid_steps)),
        (3, 3): lambda: (red_e(3).start(), red_mid[1].middle(add_split)),
    }

    def ticks(e, point):
        for (expert_at, point_at), act in schedule.items():
            if point_at == point:

                @pl.when(e == expert_at)
                def _():
                    act()

    def expert(e, carry):
        def dispatch(m, carry):
            hot = (slot_row + e * slots == sid[m, 0:1, :]) | (slot_row + e * slots == sid[m, 1:2, :])
            hot_s[m] = jnp.where(hot, 1.0, 0.0).astype(BF)
            gate = jnp.sum(jnp.where(hot, rp[m, pl.ds(e, 1), :], 0.0), axis=1, keepdims=True)
            gts[m] = jnp.broadcast_to(gate, (slots, 128))
            n2m = rowsb[pl.ds(m * images, images)].reshape(full, width)
            xs[m] = dot_nn(hot_s[m], n2m).astype(BF)
            dym = dyg[pl.ds(m * images, images)].reshape(full, width)
            vals = dot_nn(hot_s[m], dym)
            ob[pl.ds(e, 1), :] += jnp.sum(gate * vals, axis=0, keepdims=True)
            vs[m] = vals.astype(BF)
            return carry

        lax.fori_loop(0, 2, dispatch, 0)
        ticks(e, 0)
        gat(e).finish()


        def hidden_units(m, carry):
            gate = gts[m][:, 0:1]
            d_gate = jnp.zeros((slots, 1), F32)
            for lo in range(0, ff, 256):
                span = slice(lo, lo + 256)
                pre = dot_nn(xs[m], wbuf[e, :, 0, :, span].reshape(width, 256))
                act, slope = gelu_parts(pre + b1[pl.ds(e, 1), span])
                gas[m, :, span] = (gate * act).astype(BF)
                back = dot_nn(vs[m], wbuf[e, :, 1, :, span].reshape(width, 256))
                d_gate = d_gate + jnp.sum(act * back, axis=1, keepdims=True)
                d_pre = gate * slope * back
                hb[pl.ds(e, 1), span] += jnp.sum(d_pre, axis=0, keepdims=True)
                dps[m, :, span] = d_pre.astype(BF)
            high = d_gate.astype(BF)
            low = (d_gate - high.astype(F32)).astype(BF)
            zero = jnp.zeros((slots, 128), BF)
            extra = [
                jnp.where(lane == e, high, jnp.where(lane == 16 + e, jnp.ones_like(zero), zero)),
                jnp.where(lane == e, low, zero),
            ]
            lower, upper = slice(0, fsdp // 2), slice(fsdp // 2, fsdp)
            part_of = lambda i, cut: wbuf[e, cut, i].reshape(width // 2, ff)
            pieces = [
                lambda: dot_nt(gas[m], part_of(1, lower)).astype(BF),
                lambda: dot_nt(gas[m], part_of(1, upper)).astype(BF),
                lambda: dot_nt(dps[m], part_of(0, lower)).astype(BF),
                lambda: dot_nt(dps[m], part_of(0, upper)).astype(BF),
                lambda: jnp.concatenate(extra, axis=1),
            ]
            lo = 0
            for make in pieces:
                piece = make()
                span = slice(lo, lo + piece.shape[1])
                lo = span.stop
                more = dot_tn(hot_s[m], piece).reshape(images, rows, piece.shape[1])
                part[m, :, :, span] = (part[m, :, :, span].astype(F32) + more).astype(BF)

            @pl.when(e == experts - 1)
            def _():
                row_reduce(m, width, wide + 256, 2 + m).start()

            @pl.when(m == 0)
            def _():
                ticks(e, 1)

            return carry

        lax.fori_loop(0, 2, hidden_units, 0)
        ticks(e, 2)
        gat(e).drain()

        two = 2 * slots
        for n in range(2):
            cut = slice(n * (width // 2), (n + 1) * (width // 2))
            blocks = slice(n * fsdp // 2, (n + 1) * fsdp // 2)
            for i, (left, right) in enumerate(((xs, dps), (vs, gas))):
                made = dot_tn(left[:, :, cut].reshape(two, width // 2), right[...].reshape(two, ff))
                wbuf[e, blocks, i] = made.astype(BF).reshape(fsdp // 2, own, ff)
        ticks(e, 3)
        return carry

    lax.fori_loop(0, experts, expert, 0)

    red_e(0).middle(high_steps)
    red_e(1).middle(low_steps + mid_steps)

    zs[...] = jnp.zeros_like(zs)
    lane = lax.broadcasted_iota(jnp.int32, (rows, 128), 1)
    lane16 = lax.broadcasted_iota(jnp.int32, (rows, 16), 1)
    router_lane = (lane16 >= 5) & (lane16 < 5 + experts)

    def router_back(m, carry):
        hidden = hid[m]
        normed, inv = norm_parts(hidden)
        dy = dyg[m * images + t].astype(F32)
        n2 = rowsb[m * images + t]
        logits = jnp.where(router_lane, dot_nt(n2, par[...].astype(BF)), -1e30)
        expo = jnp.exp(logits - jnp.max(logits, axis=1, keepdims=True))
        probs = expo / jnp.sum(expo, axis=1, keepdims=True)
        got = row_reduce(m, width, wide + 256, 2 + m).finish()
        sums = got[:, width : width + 128] + got[:, width + 128 :]
        pcol, qcol, out = [], [], hidden
        for e in range(experts):
            p_e = jnp.sum(jnp.where(lane16 == 5 + e, probs, 0.0), axis=1, keepdims=True)
            kept = 0.25 * jnp.sum(jnp.where(lane == 16 + e, sums, 0.0), axis=1, keepdims=True)
            q_e = jnp.sum(jnp.where(lane == e, sums, 0.0), axis=1, keepdims=True)
            bias = par[5 + experts + e : 6 + experts + e, :]
            q_e = q_e + kept * jnp.sum(dy * bias, axis=1, keepdims=True)
            out = out + (kept * p_e) * bias
            pcol.append(p_e)
            qcol.append(q_e)
        y_out[m] = out[:live]
        mean_q = pcol[0] * qcol[0]
        for e in range(1, experts):
            mean_q = mean_q + pcol[e] * qcol[e]
        mid = got[:, :width]
        for e in range(experts):
            d_logit = (pcol[e] * (qcol[e] - mean_q)).astype(BF).astype(F32)
            mid = mid + d_logit * par[5 + e : 6 + e, :]
            zs[5 + e : 6 + e, :] += jnp.sum(d_logit * n2.astype(F32), axis=0, keepdims=True)
        d_hidden = dy + norm_back(mid * gain_two, normed, inv)
        hid[m] = d_hidden
        rowsb[m * images + t] = d_hidden.astype(BF)
        row_gather(rowsb, m, 6 + m).start()

        @pl.when(m == 0)
        def _():
            red_e(1).middle(high_steps)

        zs[2:3, :] += jnp.sum(d_hidden, axis=0, keepdims=True)
        zs[3:4, :] += jnp.sum(mid * normed, axis=0, keepdims=True)
        zs[4:5, :] += jnp.sum(mid, axis=0, keepdims=True)
        return carry

    lax.fori_loop(0, 2, router_back, 0)
    zs[5 + experts : 5 + 2 * experts, :] = 0.25 * ob[0:experts, :]
    zs[16 : 16 + experts, :] = hb[0:experts, :]
    for m in range(2):
        row_h[m].forward()
        red_mid[m].drain()

    def attend_back(i, carry):
        stacked_d = stack_heads(dmx[i], masks)
        stacked_q = stack_heads(qkv[0, i], masks)
        probs_low = prob[i]
        probs = probs_low.astype(F32)
        d_prob = dot_nt(stacked_d, qkv[2, i])
        d_score = probs * (d_prob - jnp.sum(probs * d_prob, axis=-1, keepdims=True))
        d_score = d_score.astype(BF)
        qkv[0, i] = (merge_heads(dot_nn(d_score, qkv[1, i]), masks) * scale).astype(BF)
        qkv[1, i] = (dot_tn(d_score, stacked_q) * scale).astype(BF)
        qkv[2, i] = dot_tn(probs_low, stacked_d).astype(BF)
        return carry

    for m in range(2):
        row_h[m].finish()
        span = slice(m * images, (m + 1) * images)
        block = rowsb[span].reshape(full, width)
        weights = awg[...].reshape(width, 4 * hw)
        dmx[span] = dot_nn(block, weights[:, 3 * hw :]).astype(BF).reshape(images, rows, hw)
        lax.fori_loop(m * images, (m + 1) * images, attend_back, 0)
        for n in range(2):
            cut = slice(n * fsdp // 2, (n + 1) * fsdp // 2)
            weights = awg[cut].reshape(width // 2, 4 * hw)
            low = jnp.zeros((full, width // 2), F32)
            for c in range(3):
                low = low + dot_nt(qkv[c, span].reshape(full, hw), weights[:, c * hw : (c + 1) * hw])
            here = slice(n * (width // 2), (n + 1) * (width // 2))
            zs[1:2, here] += jnp.sum(low, axis=0, keepdims=True)
            normed = rin[span, :, here].astype(F32).reshape(full, width // 2)
            zs[0:1, here] += jnp.sum(low * normed, axis=0, keepdims=True)
            at = width + n * (width // 2)
            part[m, :, :, at : at + width // 2] = low.astype(BF).reshape(images, rows, width // 2)
        red_low[m].start()
        red_low[m].middle()
        red_e(2).middle((low_steps + mid_steps, high_steps)[m])

    gat_aw.drain()

    def att_grads(n, carry):
        cut = pl.ds(pl.multiple_of(n * (width // 2), 128), width // 2)
        flat_in = rin[:, :, cut].reshape(2 * full, width // 2)
        made = [dot_tn(flat_in, qkv[c].reshape(2 * full, hw)) for c in range(3)]
        flat_h = rowsb[:, :, cut].reshape(2 * full, width // 2)
        made.append(dot_tn(flat_h, mix[...].reshape(2 * full, hw)))
        joined = jnp.concatenate(made, axis=1).astype(BF)
        awg[pl.ds(n * (fsdp // 2), fsdp // 2)] = joined.reshape(fsdp // 2, own, 4 * hw)
        return carry

    zs[0:1, :] = (zs[0:1, :] - shift_one * zs[1:2, :]) / gain_one

    hops = [(z1, 16, net.sibling), (z2, 16, net.across), (z3, 24, net.partner)]

    def hop(i):
        buf, count, dev = hops[i]
        return remote(zs.at[0:count], buf, sm_s.at[i], sm_r.at[i], dev)

    def hop_end(i):
        buf, count, dev = hops[i]
        hop(i).wait()
        zs[0:count] = zs[0:count] + buf[...]

    hop(0).start()
    lax.fori_loop(0, 2, att_grads, 0)
    hop_end(0)
    hop(1).start()
    for m in range(2):
        red_out[m].start()

    def first_back(m, carry):
        low = row_reduce(m, width, wide, 6 + m).finish()
        normed, inv = norm_parts(padded(x_in, m))
        gx_out[m] = (hid[m] + norm_back(low * gain_one, normed, inv))[:live]
        return carry

    lax.fori_loop(0, 2, first_back, 0)
    hop_end(1)
    hop(2).start()
    red_a.start()
    for m in range(2):
        red_out[m].middle()
    outs = []

    def expert_out(e):
        both = red_e(e).finish()
        for i, dst in enumerate((g1_out, g2_out)):
            if e > 1:
                outs[2 * e - 4 + i].wait()
            stage = hid.at[e % 2, i * own : (i + 1) * own]
            stage[...] = both[i]
            outs.append(pltpu.make_async_copy(stage, dst.at[e], loc.at[2 * e + i]))
            outs[-1].start()

    red_e(0).collect()
    red_e(1).collect()
    expert_out(0)
    expert_out(1)
    red_e(3).middle(steps)
    hop_end(2)
    for k in range(1, net.half):
        remote(zs, z4.at[k], sm_s.at[2 + k], sm_r.at[2 + k], net.line(k)).start()
    for m in range(2):
        y_out[m] += red_out[m].finish()[:live]
    red_e(2).collect()
    expert_out(2)
    red_a.middle(steps)
    expert_out(3)
    made = red_a.finish()
    for c in range(3):
        gq_out[c] = made[:, c * hw : (c + 1) * hw]
    gm_out[...] = made[:, 3 * hw :]
    sums = zs[...]
    for k in range(1, net.half):
        remote(zs, z4.at[k], sm_s.at[2 + k], sm_r.at[2 + k], net.line(k)).wait()
        sums = sums + z4[k]
    small_out[...] = sums
    for copy in outs[-4:]:
        copy.wait()
    for op in [red_e(e) for e in range(experts)] + [red_a, gat_par] + row_dy + row_h + red_out + red_low:
        op.drain()


def finish_kernel(own, experts, *refs):
    it = iter(refs)
    take = lambda n: [next(it) for _ in range(n)]
    small, gm = take(2)
    large = take(5)
    vec_out = take(5)
    router_out, ob_out, hb_out, gm_out = take(4)
    large_out = take(5)
    held = take(5)
    (sem,) = take(1)
    loads = [pltpu.make_async_copy(large[i], held[i], sem.at[0, i]) for i in range(5)]
    stores = [pltpu.make_async_copy(held[i], large_out[i], sem.at[1, i]) for i in range(5)]
    for load in loads:
        load.start()
    for load, store in zip(loads, stores):
        load.wait()
        store.start()
    sums = small[...]
    width = sums.shape[1]
    hb_out[...] = sums[16 : 16 + experts]
    mine = pltpu.roll(sums, lax.rem(width - own * lax.axis_index("fsdp"), width), 1)[:, :own]
    for i in range(5):
        vec_out[i][...] = mine[i : i + 1]
    router_out[...] = mine[5 : 5 + experts]
    ob_out[...] = mine[5 + experts : 5 + 2 * experts]
    gm_out[...] = gm[...].T
    for store in stores:
        store.wait()


def vmem(shape, dtype=BF):
    return pltpu.VMEM(shape, dtype)


def spec(space):
    return pl.BlockSpec(memory_space=space)


V = pltpu.VMEM
H = pltpu.HBM


def pair_sems(units, half):
    return [DMA((units, half)) for _ in range(4)]


def row_sems(units):
    return [DMA((units,)), DMA((units,)), DMA((units, 2)), DMA((units, 2))]


def per_device(
    patch_embeddings,
    upstream_gradient,
    picture_valid_count,
    assigned_specialists,
    filling_sequence_place,
    leading_scale_factor,
    leading_offset_vector,
    query_value_matrix,
    mixing_projection_matrix,
    mixing_offset_vector,
    central_scale_factor,
    central_offset_vector,
    gating_projection,
    specialist_widen_matrix,
    specialist_inner_offset,
    specialist_contract_matrix,
    specialist_final_offset,
):
    fsdp = lax.axis_size("fsdp")
    half = fsdp // 2
    tp = lax.axis_size("tp")
    own_rows, width = patch_embeddings.shape[1:]
    rows = -(-own_rows // 16) * 16
    images = tp
    full = images * rows
    own = leading_scale_factor.shape[0]
    hw = query_value_matrix.shape[2]
    heads = hw // HEAD_DIM
    experts, _, ff = specialist_widen_matrix.shape
    slots = 2 * own_rows * tp // experts
    f_index = lax.axis_index("fsdp")

    row = lambda v: v.reshape(1, own)
    vectors = [
        row(leading_scale_factor),
        row(leading_offset_vector),
        row(mixing_offset_vector),
        row(central_scale_factor),
        row(central_offset_vector),
        gating_projection.T,
        specialist_final_offset,
    ]
    w1 = specialist_widen_matrix
    w2 = specialist_contract_matrix.transpose(0, 2, 1)
    sds = jax.ShapeDtypeStruct
    wide = 2 * width + 256
    outs = pl.pallas_call(
        functools.partial(block_kernel, fsdp, experts),
        out_shape=[
            sds((2, own_rows, width), F32),
            sds((2, own_rows, width), F32),
            sds((3, own, hw), F32),
            sds((own, hw), F32),
            sds((experts, own, ff), F32),
            sds((experts, own, ff), F32),
        ]
        + [
            sds((24, width), F32),
            sds((experts, half, 2, own, ff), BF),
        ],
        in_specs=[spec(pltpu.SMEM)] + [spec(V)] * 11 + [spec(H)] * 2 + [spec(V)] * 3,
        out_specs=[spec(V)] * 4 + [spec(H)] * 2 + [spec(V), spec(H)],
        scratch_shapes=[
            vmem((2 * images, rows, width)),
            vmem((2 * images, rows, width)),
            vmem((2 * images, rows, width)),
            vmem((3, 2 * images, rows, hw)),
            vmem((2 * images, heads * rows, rows)),
            vmem((2 * images, rows, hw)),
            vmem((2, rows, width), F32),
            vmem((fsdp, own, 4 * hw)),
            vmem((16, width), F32),
            vmem((fsdp, 16, 128)),
            vmem((experts, fsdp, 2, own, ff)),
            vmem((2, images, rows, wide)),
            vmem((2, 2, rows, wide)),
            vmem((2, rows, wide)),
            vmem((experts, half, 2, own, ff)),
            vmem((half, own, 4 * hw)),
            vmem((half, own, 4 * hw)),
            vmem((2, slots, full)),
            vmem((2, slots, 128), F32),
            vmem((2, slots, width)),
            vmem((2, slots, width)),
            vmem((2, slots, ff)),
            vmem((2, slots, ff)),
            vmem((2, 8, full), jnp.int32),
            vmem((2, 8, full), F32),
            vmem((2 * images, rows, hw)),
            vmem((8, ff), F32),
            vmem((8, width), F32),
            vmem((8, ff), F32),
            vmem((half - 1, 2, own, ff)),
            vmem((16, width), F32),
            vmem((16, width), F32),
            vmem((24, width), F32),
            vmem((half, 24, width), F32),
            vmem((24, width), F32),
        ]
        + pair_sems(2 + experts, half)
        + pair_sems(1 + experts, half)
        + row_sems(8)
        + row_sems(8)
        + [DMA((2 * experts + 2,)), DMA((2 + half,)), DMA((2 + half,)), DMA((experts, half))],
        compiler_params=pltpu.CompilerParams(
            collective_id=1, has_side_effects=True, vmem_limit_bytes=VMEM_LIMIT
        ),
        name="block",
    )(
        picture_valid_count,
        patch_embeddings,
        upstream_gradient,
        *vectors,
        query_value_matrix.transpose(1, 0, 2),
        mixing_projection_matrix,
        w1,
        w2,
        specialist_inner_offset,
        assigned_specialists.transpose(0, 2, 1),
        filling_sequence_place,
    )
    y_out, gx_out, gq, gm, g1, g2, small = outs[:7]
    large = [y_out, gx_out, gq, g1, g2]
    outs = pl.pallas_call(
        functools.partial(finish_kernel, own, experts),
        out_shape=[sds((1, own), F32)] * 5
        + [
            sds((experts, own), F32),
            sds((experts, own), F32),
            sds((experts, ff), F32),
            sds((hw, own), F32),
        ]
        + [sds(v.shape, F32) for v in large],
        in_specs=[spec(V)] * 2 + [spec(H)] * 5,
        out_specs=[spec(V)] * 9 + [spec(H)] * 5,
        scratch_shapes=[vmem(v.shape, F32) for v in large] + [DMA((2, 5))],
        compiler_params=pltpu.CompilerParams(vmem_limit_bytes=VMEM_LIMIT),
        name="finish",
    )(small, gm, *large)
    flat = [v.reshape(own) for v in outs[:5]]
    router, ob, hb, gm, y_out, gx_out, gq, g1, g2 = outs[5:]
    return (
        y_out,
        gx_out,
        flat[0],
        flat[1],
        gq.transpose(1, 0, 2),
        gm,
        flat[2],
        flat[3],
        flat[4],
        router.T,
        g1,
        hb,
        g2.transpose(0, 2, 1),
        ob,
    )


def solution(mesh):
    placed = (
        P(None, ("fsdp", "tp"), None),
        P(None, ("fsdp", "tp"), None),
        P(None, "fsdp"),
        P(None, "fsdp", None),
        P(None, "fsdp", None),
        P("fsdp"),
        P("fsdp"),
        P("fsdp", None, "tp"),
        P("tp", "fsdp"),
        P("fsdp"),
        P("fsdp"),
        P("fsdp"),
        P("fsdp", None),
        P(None, "fsdp", "tp"),
        P(None, "tp"),
        P(None, "tp", "fsdp"),
        P(None, "fsdp"),
    )
    return jax.shard_map(
        per_device,
        mesh=mesh,
        in_specs=placed,
        out_specs=(
            P(None, ("fsdp", "tp"), None),
            P(None, ("fsdp", "tp"), None),
            P("fsdp"),
            P("fsdp"),
            P("fsdp", None, "tp"),
            P("tp", "fsdp"),
            P("fsdp"),
            P("fsdp"),
            P("fsdp"),
            P("fsdp", None),
            P(None, "fsdp", "tp"),
            P(None, "tp"),
            P(None, "tp", "fsdp"),
            P(None, "fsdp"),
        ),
        check_vma=False,
    )
```
